128 devices in a mesh: pipe: 8 (over y, core), seq: 16 (over z, x).
Axes of the slice: x: 4, y: 4, z: 4, core: 2. Of those that a mesh axis runs over, the one named last changes fastest.
Arguments:
- layer_input: bfloat16 [8, 8192, 1024], P('pipe', 'seq'), may hold values from -40 to 40
- handoff: bfloat16 [8, 8192, 1024], P('pipe', 'seq'), may hold values from -6 to 6
- qkv_weight: bfloat16 [8, 1024, 3072], P('pipe'), may hold values from -0.1875 to 0.1875
- out_weight: bfloat16 [8, 1024, 1024], P('pipe'), may hold values from -0.1875 to 0.1875
- neighbours: int32 [8, 16, 64, 8], P('pipe', 'seq'), may hold values from 0 to 63, as said below
- counts: int32 [8, 16, 64], P('pipe', 'seq'), may hold values from 1 to 8
Outputs:
- grad_input: bfloat16 [8, 8192, 1024], P('pipe', 'seq')
- grad_qkv_weight: float32 [8, 3072, 1024], P('pipe', 'seq')
- grad_out_weight: float32 [8, 1024, 1024], P('pipe', 'seq')
The draws below stay inside these ranges and needn't reach their ends.
Inputs may be any that keep to these rules, and one draw needn't show every extreme that they name: `neighbours`: entry 0 of every list is the query block itself; the 8 entries of one list are distinct blocks; entries at or past the count are to be ignored.
All inputs are finite; a program needn't handle non-finite values.
Results may differ from the reference program's by a relative error of at most 0.03.
The reference program's roundings to bfloat16 on the way count: a program that leaves them out, or rounds other values in their place, can miss the bound.
Values may be sent and summed in bfloat16 or wider, within the bound.
A program may use at most 128 MiB of HBM per device.

```python
import jax
import jax.numpy as jnp
from jax import lax

HEAD_DIM = 64
HEADS = 16
D = 1024
BLOCK = 128
MAXNB = 8
SECTIONS = 8
SEQ_LEN = 8192
QBLOCKS = 64


def draw_layer_input(key, part):
    key = jax.random.fold_in(key, 11)
    first = jax.random.fold_in(key, 0)
    values = jax.random.truncated_normal(first, -5.0, 5.0, (SECTIONS, SEQ_LEN, D), jnp.float32)
    return values.astype(jnp.bfloat16)


def draw_qkv_weight(key, part):
    key = jax.random.fold_in(key, 12)
    first = jax.random.fold_in(key, 0)
    values = jax.random.truncated_normal(first, -4.0, 4.0, (SECTIONS, D, 3 * D), jnp.float32) * D ** (-0.5)
    return values.astype(jnp.bfloat16)


def draw_neighbours(key, part):
    key = jax.random.fold_in(key, 13)
    many = jax.random.split(key, SECTIONS * HEADS * QBLOCKS)

    def pick(single):
        return jax.random.permutation(single, QBLOCKS - 1)[:MAXNB - 1].astype(jnp.int32)
    offsets = jax.vmap(pick)(many).reshape(SECTIONS, HEADS, QBLOCKS, MAXNB - 1)
    own = jnp.broadcast_to(jnp.arange(QBLOCKS, dtype=jnp.int32)[None, None, :, None], (SECTIONS, HEADS, QBLOCKS, 1))
    others = (own + 1 + offsets) % QBLOCKS
    return jnp.concatenate([own, others], axis=3).astype(jnp.int32)


def draw_counts(key, part):
    key = jax.random.fold_in(key, 14)
    first, second, third, fourth = jax.random.split(key, 4)
    caps = jax.random.randint(first, (SECTIONS, HEADS, 1), 1, MAXNB + 1, jnp.int32)
    chosen_head = jax.random.randint(second, (SECTIONS, 1, 1), 0, HEADS, jnp.int32)
    head_ids = jnp.arange(HEADS, dtype=jnp.int32)[None, :, None]
    caps = jnp.where(head_ids == chosen_head, MAXNB, caps)
    values = jax.random.randint(third, (SECTIONS, HEADS, QBLOCKS), (caps + 1) // 2, caps + 1, jnp.int32)
    chosen_block = jax.random.randint(fourth, (SECTIONS, 1, 1), 0, QBLOCKS, jnp.int32)
    block_ids = jnp.arange(QBLOCKS, dtype=jnp.int32)[None, None, :]
    values = jnp.where((head_ids == chosen_head) & (block_ids == chosen_block), MAXNB, values)
    return values.astype(jnp.int32)


def steps_of(own_key, shape, cuts, least, top_value):
    def one(axis_at, blocks):
        steps = jax.random.uniform(jax.random.fold_in(jax.random.fold_in(own_key, 6), axis_at), (blocks,), jnp.float32, least / len(cuts), top_value / len(cuts))
        return jnp.repeat(jnp.exp(steps), shape[axis_at] // blocks).reshape((-1,) + (1,) * (len(shape) - axis_at - 1))

    loudness = one(*cuts[0])
    for cut in cuts[1:]:
        loudness = loudness * one(*cut)
    return loudness


def scatter_about(rng, shape, scale, limit, cuts=(), kind=jnp.bfloat16):
    drawn = jax.random.normal(rng, shape, jnp.float32) * scale
    if len(cuts) > 0:
        drawn = steps_of(rng, shape, cuts, -0.22, 0.18) * drawn
    return jnp.clip(drawn, min=-limit, max=limit).astype(kind)


def setup_inputs(seed: int = 0) -> dict:
    seeds = jax.random.split(jax.random.key(seed), 7)
    layer_input = draw_layer_input(jax.random.fold_in(seeds[6], 71), 0)
    handoff = scatter_about(seeds[1], (SECTIONS, SEQ_LEN, D), 1.0, 6.0, ((0, 8), (1, 16)))
    qkv_weight = draw_qkv_weight(jax.random.fold_in(seeds[6], 71), 0)
    out_weight = scatter_about(seeds[3], (SECTIONS, D, D), D ** -0.5, 0.1875, ((0, 8),))
    neighbours = draw_neighbours(jax.random.fold_in(seeds[6], 71), 0)
    counts = draw_counts(jax.random.fold_in(seeds[6], 71), 0)
    return {"layer_input": layer_input, "handoff": handoff, "qkv_weight": qkv_weight, "out_weight": out_weight, "neighbours": neighbours, "counts": counts}


def head_pass(queries, keys_all, values_all, grad_attn, near_blocks, near_count):
    f32 = jnp.float32
    score_scale = HEAD_DIM ** -0.5
    qblocks = SEQ_LEN // BLOCK
    query_blocks = queries.astype(f32).reshape(qblocks, BLOCK, HEAD_DIM)
    key_blocks = keys_all.astype(f32).reshape(qblocks, BLOCK, HEAD_DIM)
    value_blocks = values_all.astype(f32).reshape(qblocks, BLOCK, HEAD_DIM)
    grad_blocks = grad_attn.astype(f32).reshape(qblocks, BLOCK, HEAD_DIM)
    near_keys = key_blocks[near_blocks].reshape(qblocks, MAXNB * BLOCK, HEAD_DIM)
    near_values = value_blocks[near_blocks].reshape(qblocks, MAXNB * BLOCK, HEAD_DIM)
    usable = jnp.repeat(jnp.arange(MAXNB, dtype=jnp.int32)[None, :] < near_count[:, None], BLOCK, axis=1)
    scores = jnp.einsum('bid,bjd->bij', query_blocks, near_keys) * score_scale
    scores = jnp.where(usable[:, None, :], scores, -jnp.inf)
    weights = jnp.exp(scores - jnp.max(scores, axis=-1, keepdims=True))
    weights = weights / jnp.sum(weights, axis=-1, keepdims=True)
    weights_low = lax.optimization_barrier(weights.astype(jnp.bfloat16)).astype(f32)
    attended = jnp.einsum('bij,bjd->bid', weights_low, near_values)
    attended = lax.optimization_barrier(attended.astype(jnp.bfloat16)).astype(f32)
    grad_weights = jnp.einsum('bid,bjd->bij', grad_blocks, near_values)
    row_dot = jnp.sum(grad_blocks * attended, axis=-1, keepdims=True)
    grad_scores = weights * (grad_weights - row_dot)
    grad_scores = lax.optimization_barrier(grad_scores.astype(jnp.bfloat16)).astype(f32)
    grad_query = jnp.einsum('bij,bjd->bid', grad_scores, near_keys) * score_scale
    key_terms = jnp.einsum('bij,bid->bjd', grad_scores, query_blocks) * score_scale
    value_terms = jnp.einsum('bij,bid->bjd', weights_low, grad_blocks)
    flat_blocks = near_blocks.reshape(qblocks * MAXNB).astype(jnp.int32)
    key_terms = key_terms.reshape(qblocks * MAXNB, BLOCK, HEAD_DIM)
    value_terms = value_terms.reshape(qblocks * MAXNB, BLOCK, HEAD_DIM)
    empty = jnp.zeros((qblocks, BLOCK, HEAD_DIM), f32)
    grad_keys = empty.at[flat_blocks].add(key_terms)
    grad_values = empty.at[flat_blocks].add(value_terms)
    return (grad_query.reshape(SEQ_LEN, HEAD_DIM), grad_keys.reshape(SEQ_LEN, HEAD_DIM),
            grad_values.reshape(SEQ_LEN, HEAD_DIM), attended.reshape(SEQ_LEN, HEAD_DIM).astype(jnp.bfloat16))


def reference(layer_input, handoff, qkv_weight, out_weight, neighbours, counts):
    f32 = jnp.float32
    inputs_all = []
    qkv_grads = []
    out_grads = []
    for section_index in range(SECTIONS):
        inputs = layer_input[section_index]
        grad_out = handoff[(section_index + 1) % SECTIONS]
        weight_in = qkv_weight[section_index]
        weight_out = out_weight[section_index]
        projected = jnp.dot(inputs, weight_in, preferred_element_type=f32).astype(jnp.bfloat16)
        grad_attn = jnp.dot(grad_out, weight_out.T, preferred_element_type=f32).astype(jnp.bfloat16)
        heads_view = projected.reshape(SEQ_LEN, HEADS, 3, HEAD_DIM).transpose(1, 2, 0, 3)
        grad_view = grad_attn.reshape(SEQ_LEN, HEADS, HEAD_DIM).transpose(1, 0, 2)

        def one_head(pieces):
            return head_pass(pieces[0], pieces[1], pieces[2], pieces[3], pieces[4], pieces[5])

        grad_query, grad_keys, grad_values, attended = lax.map(
            one_head, (heads_view[:, 0], heads_view[:, 1], heads_view[:, 2], grad_view,
                       neighbours[section_index], counts[section_index]))
        grad_qkv = jnp.stack([grad_query, grad_keys, grad_values], axis=1)
        grad_qkv = grad_qkv.transpose(2, 0, 1, 3).reshape(SEQ_LEN, 3 * D).astype(jnp.bfloat16)
        attended = attended.transpose(1, 0, 2).reshape(SEQ_LEN, D)
        out_grads.append(jnp.dot(attended.T, grad_out, preferred_element_type=f32))
        qkv_grads.append(jnp.dot(grad_qkv.T, inputs, preferred_element_type=f32))
        back = grad_out.astype(f32) + jnp.dot(grad_qkv, weight_in.T, preferred_element_type=f32)
        inputs_all.append(back.astype(jnp.bfloat16))
    return jnp.stack(inputs_all), jnp.stack(qkv_grads), jnp.stack(out_grads)
```

```python
import functools
import jax, jax.numpy as jnp
from jax import lax
from jax.experimental import pallas as pl
from jax.experimental.pallas import tpu as pltpu
from jax.sharding import PartitionSpec as P
HEAD_DIM=64; BLOCK=128; MAXNB=8; QB=64; GROUP=4
f32=jnp.float32; bf16=jnp.bfloat16

def attn_body(order, nb, cnt, hq, qd, gqa, acc, kvt, group, i, slots):
    scale = HEAD_DIM ** -0.5
    half_row = lax.broadcasted_iota(jnp.int32, (BLOCK, BLOCK), 0) < HEAD_DIM
    half_lane = lax.broadcasted_iota(jnp.int32, (BLOCK, BLOCK), 1) < HEAD_DIM
    zero = jnp.zeros((BLOCK, BLOCK), bf16)
    dn = (((1,), (0,)), ((), ()))
    mm = lambda a, b: lax.dot_general(a, b, dn, preferred_element_type=f32)
    chains = []
    for g in range(group):
        b = order[i * group + g]
        chains.append((b, cnt[b], [nb[b, j] for j in range(slots)]))
    st = []
    for b, c, ns in chains:
        own = qd[b]
        own_t = own.T
        q_t = jnp.where(half_row, own_t * jnp.asarray(scale, bf16), zero)
        d_t = jnp.where(half_row, zero, own_t)
        right = jnp.concatenate([q_t, d_t], axis=1)
        scores, dps = [], []
        for j in range(slots):
            keys = hq[key_rows(ns[j]), :]
            both = mm(keys, right)
            s = both[:, :BLOCK]
            if j > 0:
                s = jnp.where(j < c, s, -jnp.inf)
            scores.append(s); dps.append(both[:, BLOCK:])
        st.append((own, own_t, scores, dps))
    st2 = []
    for (b, c, ns), (own, own_t, scores, dps) in zip(chains, st):
        top = scores[0]
        for s in scores[1:]:
            top = jnp.maximum(top, s)
        top = jnp.max(top, axis=0, keepdims=True)
        es = [jnp.exp(s - top) for s in scores]
        tot = es[0]
        for e in es[1:]:
            tot = tot + e
        inv = 1.0 / jnp.sum(tot, axis=0, keepdims=True)
        ps = [e * inv for e in es]
        st2.append((own, own_t, dps, ps))
    for (b, c, ns), (own, own_t, dps, ps) in zip(chains, st2):
        low = [p.astype(bf16) for p in ps]
        att_t = jnp.zeros((HEAD_DIM, BLOCK), f32)
        for j in range(slots):
            att_t = att_t + mm(kvt[ns[j], HEAD_DIM:, :], low[j])
        att_t = att_t.astype(bf16)
        dot = jnp.sum(own_t[HEAD_DIM:, :].astype(f32) * att_t.astype(f32), axis=0, keepdims=True)
        ds = [(p * (dp - dot)).astype(bf16) for p, dp in zip(ps, dps)]
        left = jnp.concatenate([jnp.where(half_lane, own * jnp.asarray(scale, bf16), zero), jnp.where(half_lane, zero, own)], axis=0)
        gq_t = jnp.zeros((HEAD_DIM, BLOCK), f32)
        for j in range(slots):
            gq_t = gq_t + mm(kvt[ns[j], :HEAD_DIM, :], ds[j])
            acc[ns[j]] += mm(jnp.concatenate([ds[j], low[j]], axis=1), left)
        gq_t = (gq_t * scale).astype(bf16)
        gqa[b] = jnp.concatenate([gq_t, att_t], axis=0).T

def key_rows(n):
    return pl.ds(pl.multiple_of((n // 2) * 512 + (n % 2) * BLOCK, BLOCK), BLOCK)


def attn_kernel(order, nb, cnt, hq, hg, acc, kvt, qd, gqa, *, group, switch):
    def prep(u, carry):
        base = pl.multiple_of(u * 512, 512)
        for e in range(2):
            acc[2 * u + e] = jnp.zeros((BLOCK, BLOCK), f32)
            kvt[2 * u + e] = hq[pl.ds(base + e * BLOCK, BLOCK), :].T
        q = hq[pl.ds(base + 256, BLOCK), :]
        d = hq[pl.ds(base + 384, BLOCK), :]
        qd[2 * u] = jnp.concatenate([q[:, :HEAD_DIM], d[:, :HEAD_DIM]], axis=1)
        qd[2 * u + 1] = jnp.concatenate([q[:, HEAD_DIM:], d[:, HEAD_DIM:]], axis=1)
        return carry
    lax.fori_loop(0, QB // 2, prep, 0, unroll=2)
    def step(i, carry):
        if switch:
            most = cnt[order[i * group]]
            for g in range(1, group):
                most = jnp.maximum(most, cnt[order[i * group + g]])
            for slots in range(1, MAXNB + 1):
                @pl.when(most == slots)
                def run():
                    attn_body(order, nb, cnt, hq, qd, gqa, acc, kvt, group, i, slots)
        else:
            attn_body(order, nb, cnt, hq, qd, gqa, acc, kvt, group, i, MAXNB)
        return carry
    lax.fori_loop(0, QB // group, step, 0)
    def fin(u, carry):
        base = pl.multiple_of(u * 512, 512)
        for e in range(2):
            hg[pl.ds(base + e * BLOCK, BLOCK), :] = acc[2 * u + e].astype(bf16)
        a, b = gqa[2 * u], gqa[2 * u + 1]
        hg[pl.ds(base + 256, BLOCK), :] = jnp.concatenate([a[:, :HEAD_DIM], b[:, :HEAD_DIM]], axis=1)
        hg[pl.ds(base + 384, BLOCK), :] = jnp.concatenate([a[:, HEAD_DIM:], b[:, HEAD_DIM:]], axis=1)
        return carry
    lax.fori_loop(0, QB // 2, fin, 0, unroll=2)


def attention(hq, nb, cnt, group=GROUP, switch=True):
    order = jnp.argsort(cnt).astype(jnp.int32) if switch else jnp.arange(QB, dtype=jnp.int32)
    sm = pl.BlockSpec(memory_space=pltpu.SMEM)
    vm = pl.BlockSpec(memory_space=pltpu.VMEM)
    return pl.pallas_call(functools.partial(attn_kernel, group=group, switch=switch),
        out_shape=jax.ShapeDtypeStruct((32 * 512, 128), bf16),
        in_specs=[sm, sm, sm, vm], out_specs=vm,
        scratch_shapes=[pltpu.VMEM((QB, BLOCK, 128), f32), pltpu.VMEM((QB, 128, 128), bf16), pltpu.VMEM((QB, 128, 128), bf16), pltpu.VMEM((QB, 128, 128), bf16)],
        compiler_params=pltpu.CompilerParams(vmem_limit_bytes=56*2**20),
        cost_estimate=pl.CostEstimate(flops=2*512*128*128*64*6, bytes_accessed=2**23, transcendentals=512*128*128))(order, nb, cnt, hq)


def passed_along(block, axis, distance):
    devices = range(lax.axis_size(axis))
    route = [((i - distance) % len(devices), i) for i in devices]
    return lax.ppermute(block, axis, route)


def local(layer_input, handoff, qkv_weight, out_weight, neighbours, counts):
    inputs = layer_input[0]
    grad_out = passed_along(handoff, "pipe", -1)[0]
    weight_in = qkv_weight[0]
    weight_out = out_weight[0]
    projected = jnp.dot(inputs, weight_in, preferred_element_type=f32).astype(bf16)
    grad_attn = jnp.dot(grad_out, weight_out.T, preferred_element_type=f32).astype(bf16)
    p = projected.reshape(2, 2, 128, 16, 192)
    kv = p[..., 64:].reshape(2, 256, 16, 128).transpose(2, 0, 1, 3)
    q = p[..., :64].transpose(3, 0, 2, 1, 4).reshape(16, 2, 128, 128)
    d = grad_attn.reshape(2, 2, 128, 16, 64).transpose(3, 0, 2, 1, 4).reshape(16, 2, 128, 128)
    packed = jnp.concatenate([kv, q, d], axis=2)
    hq = lax.all_to_all(packed, "seq", split_axis=0, concat_axis=0, tiled=True)
    hg = attention(hq.reshape(32 * 512, 128), neighbours[0, 0], counts[0, 0])
    back = lax.all_to_all(hg.reshape(16, 2, 512, 128), "seq", split_axis=0, concat_axis=0, tiled=True)
    gkv = back[:, :, :256].reshape(16, 512, 128)
    unpair = lambda a: a.reshape(16, 2, 128, 2, 64).transpose(0, 1, 3, 2, 4).reshape(16, 512, 64)
    gq = unpair(back[:, :, 256:384])
    att = unpair(back[:, :, 384:])
    grad_qkv = jnp.concatenate([gq, gkv], axis=2).transpose(1, 0, 2).reshape(512, 3072)
    attended = att.transpose(1, 0, 2).reshape(512, 1024)
    total = grad_out.astype(f32) + jnp.dot(grad_qkv, weight_in.T, preferred_element_type=f32)
    grad_input = total.astype(bf16)
    dims = (((0,), (0,)), ((), ()))
    grad_out_weight = lax.psum_scatter(
        lax.dot_general(attended, grad_out, dims, preferred_element_type=f32),
        "seq", scatter_dimension=0, tiled=True)
    grad_qkv_weight = lax.psum_scatter(
        lax.dot_general(grad_qkv, inputs, dims, preferred_element_type=f32),
        "seq", scatter_dimension=0, tiled=True)
    return (grad_input[None], grad_qkv_weight[None], grad_out_weight[None])


def solution(mesh):
    placed = (
        P("pipe", "seq", None),
        P("pipe", "seq", None),
        P("pipe", None, None),
        P("pipe", None, None),
        P("pipe", "seq", None, None),
        P("pipe", "seq", None),
    )
    return jax.shard_map(
        local,
        mesh=mesh,
        in_specs=placed,
        out_specs=(P("pipe", "seq", None), P("pipe", "seq", None), P("pipe", "seq", None)),
        check_vma=False,
    )
```

```python
import functools
import jax, jax.numpy as jnp
from jax import lax
from jax.experimental import pallas as pl
from jax.experimental.pallas import tpu as pltpu
from jax.sharding import PartitionSpec as P
HEAD_DIM=64; BLOCK=128; MAXNB=8; QB=64; GROUP=4
f32=jnp.float32; bf16=jnp.bfloat16

def attn_body(order, nb, cnt, hq, qd, gqa, acc, kvt, group, i, slots):
    scale = HEAD_DIM ** -0.5
    half_row = lax.broadcasted_iota(jnp.int32, (BLOCK, BLOCK), 0) < HEAD_DIM
    half_lane = lax.broadcasted_iota(jnp.int32, (BLOCK, BLOCK), 1) < HEAD_DIM
    zero = jnp.zeros((BLOCK, BLOCK), bf16)
    dn = (((1,), (0,)), ((), ()))
    mm = lambda a, b: lax.dot_general(a, b, dn, preferred_element_type=f32)
    chains = []
    for g in range(group):
        b = order[i * group + g]
        chains.append((b, cnt[b], [nb[b, j] for j in range(slots)]))
    st = []
    for b, c, ns in chains:
        own = qd[b]
        own_t = own.T
        q_t = jnp.where(half_row, own_t * jnp.asarray(scale, bf16), zero)
        d_t = jnp.where(half_row, zero, own_t)
        right = jnp.concatenate([q_t, d_t], axis=1)
        scores, dps = [], []
        for j in range(slots):
            keys = load_keys(hq, ns[j])
            both = mm(keys, right)
            s = both[:, :BLOCK]
            if j > 0:
                s = jnp.where(j < c, s, -jnp.inf)
            scores.append(s); dps.append(both[:, BLOCK:])
        st.append((own, own_t, scores, dps))
    st2 = []
    for (b, c, ns), (own, own_t, scores, dps) in zip(chains, st):
        top = scores[0]
        for s in scores[1:]:
            top = jnp.maximum(top, s)
        top = jnp.max(top, axis=0, keepdims=True)
        es = [jnp.exp(s - top) for s in scores]
        tot = es[0]
        for e in es[1:]:
            tot = tot + e
        inv = 1.0 / jnp.sum(tot, axis=0, keepdims=True)
        ps = [e * inv for e in es]
        st2.append((own, own_t, dps, ps))
    for (b, c, ns), (own, own_t, dps, ps) in zip(chains, st2):
        low = [p.astype(bf16) for p in ps]
        att_t = jnp.zeros((HEAD_DIM, BLOCK), f32)
        for j in range(slots):
            att_t = att_t + mm(kvt[ns[j], HEAD_DIM:, :], low[j])
        att_t = att_t.astype(bf16)
        dot = jnp.sum(own_t[HEAD_DIM:, :].astype(f32) * att_t.astype(f32), axis=0, keepdims=True)
        ds = [(p * (dp - dot)).astype(bf16) for p, dp in zip(ps, dps)]
        left = jnp.concatenate([jnp.where(half_lane, own * jnp.asarray(scale, bf16), zero), jnp.where(half_lane, zero, own)], axis=0)
        gq_t = jnp.zeros((HEAD_DIM, BLOCK), f32)
        for j in range(slots):
            gq_t = gq_t + mm(kvt[ns[j], :HEAD_DIM, :], ds[j])
            acc[ns[j]] += mm(jnp.concatenate([ds[j], low[j]], axis=1), left)
        gq_t = (gq_t * scale).astype(bf16)
        gqa[b] = jnp.concatenate([gq_t, att_t], axis=0).T

def load_keys(hq, n):
    half, rows = key_rows(n)
    return hq[half, rows, :]


def key_rows(n):
    return n // 2, pl.ds(pl.multiple_of((n % 2) * BLOCK, BLOCK), BLOCK)


def attn_kernel(order, nb, cnt, hq, hd, hg, ha, acc, kvt, qd, gqa, *, group):
    def prep(u, carry):
        for e in range(2):
            acc[2 * u + e] = jnp.zeros((BLOCK, BLOCK), f32)
            kvt[2 * u + e] = hq[u, pl.ds(e * BLOCK, BLOCK), :].T
        q = hq[u, pl.ds(256, BLOCK), :]
        d = hd[u]
        qd[2 * u] = jnp.concatenate([q[:, :HEAD_DIM], d[:, :HEAD_DIM]], axis=1)
        qd[2 * u + 1] = jnp.concatenate([q[:, HEAD_DIM:], d[:, HEAD_DIM:]], axis=1)
        return carry
    lax.fori_loop(0, QB // 2, prep, 0, unroll=2)

    def step(i, carry):
        most = cnt[order[i * group]]
        for g in range(1, group):
            most = jnp.maximum(most, cnt[order[i * group + g]])
        for slots in range(1, MAXNB + 1):
            @pl.when(most == slots)
            def run():
                attn_body(order, nb, cnt, hq, qd, gqa, acc, kvt, group, i, slots)
        return carry
    lax.fori_loop(0, QB // group, step, 0)

    def fin(u, carry):
        for e in range(2):
            hg[u, pl.ds(e * BLOCK, BLOCK), :] = acc[2 * u + e].astype(bf16)
        a, b = gqa[2 * u], gqa[2 * u + 1]
        hg[u, pl.ds(256, BLOCK), :] = jnp.concatenate([a[:, :HEAD_DIM], b[:, :HEAD_DIM]], axis=1)
        ha[u] = jnp.concatenate([a[:, HEAD_DIM:], b[:, HEAD_DIM:]], axis=1)
        return carry
    lax.fori_loop(0, QB // 2, fin, 0, unroll=2)


def attention(hq, hd, nb, cnt, group=GROUP):
    order = jnp.argsort(cnt).astype(jnp.int32)
    sm = pl.BlockSpec(memory_space=pltpu.SMEM)
    vm = pl.BlockSpec(memory_space=pltpu.VMEM)
    return pl.pallas_call(
        functools.partial(attn_kernel, group=group),
        out_shape=[jax.ShapeDtypeStruct((QB // 2, 384, 128), bf16), jax.ShapeDtypeStruct((QB // 2, 128, 128), bf16)],
        in_specs=[sm, sm, sm, vm, vm],
        out_specs=[vm, vm],
        scratch_shapes=[
            pltpu.VMEM((QB, BLOCK, 128), f32),
            pltpu.VMEM((QB, 128, 128), bf16),
            pltpu.VMEM((QB, 128, 128), bf16),
            pltpu.VMEM((QB, 128, 128), bf16),
        ],
        compiler_params=pltpu.CompilerParams(vmem_limit_bytes=56 * 2**20),
        cost_estimate=pl.CostEstimate(flops=2 * 512 * 128 * 128 * 64 * 6, bytes_accessed=2**23, transcendentals=512 * 128 * 128),
    )(order, nb, cnt, hq, hd)


MESH = pl.DeviceIdType.MESH

def cat_tokens(dst, row, col, pair):
    turned = pair.T
    dst[pl.ds(row, HEAD_DIM), pl.ds(col, 128)] = turned[:HEAD_DIM]
    dst[pl.ds(row, HEAD_DIM), pl.ds(col + 128, 128)] = turned[HEAD_DIM:]

def finish_kernel(gqkv, att, lg, gz, w, gin, gqw, gow,
                  rv, fv, at, lv, gv, wv, xt, mt, acc, pqs, pqr, pos, por,
                  loc, zs, zr, xs, xr, as_, ar, qs, qr, os_, or_):
    pipe = lax.axis_index("pipe")
    me = lax.axis_index("seq")
    z, x = me // 4, me % 4
    zr4 = lambda d: (z + d) % 4
    xr4 = lambda d: (x + d) % 4
    def to_z(d): return (pipe, zr4(d) * 4 + x)
    def to_x(d): return (pipe, z * 4 + xr4(d))
    barrier = pltpu.get_barrier_semaphore()
    for d in (1, 2, 3):
        pl.semaphore_signal(barrier, inc=1, device_id=to_z(d), device_id_type=MESH)
        pl.semaphore_signal(barrier, inc=1, device_id=to_x(d), device_id_type=MESH)
    loads = [pltpu.make_async_copy(gqkv.at[z], rv.at[z], loc.at[0]),
             pltpu.make_async_copy(lg, lv, loc.at[1]),
             pltpu.make_async_copy(att.at[:, x], at.at[x], loc.at[2]),
             pltpu.make_async_copy(gz, gv, loc.at[3]),
             pltpu.make_async_copy(w, wv, loc.at[4])]
    for c in loads:
        c.start()
    pl.semaphore_wait(barrier, 6)

    def remote(src, dst, ss, rs, dev):
        return pltpu.make_async_remote_copy(src_ref=src, dst_ref=dst, send_sem=ss, recv_sem=rs, device_id=dev, device_id_type=MESH)

    ZORDER = [(d, j) for j in (1, 3, 2, 0) for d in (1, 3)] + [(2, j) for j in (1, 3, 2, 0)]
    zc = {}
    for d, j in ZORDER:
        zc[d, j] = remote(gqkv.at[zr4(d), xr4(j)], rv.at[z, xr4(j)], zs.at[d - 1, j], zr.at[d - 1, j], to_z(d))
    xc, ac = {}, {}
    for d in (1, 3, 2):
        xc[0, d] = remote(gqkv.at[z, xr4(d)], fv.at[z, x], xs.at[0, d - 1], xr.at[0, d - 1], to_x(d))
        ac[d] = remote(att.at[:, xr4(d)], at.at[x], as_.at[d - 1], ar.at[d - 1], to_x(d))
        for e in (1, 3, 2):
            xc[e, d] = remote(rv.at[zr4(-e), xr4(d)], fv.at[zr4(-e), x], xs.at[e, d - 1], xr.at[e, d - 1], to_x(d))
    for key in ZORDER:
        zc[key].start()
    for d in (1, 3, 2):
        xc[0, d].start()
    for d in (1, 3, 2):
        ac[d].start()

    def weight_part(zh, out_at):
        def turn(u, carry):
            xi, half = u // 2, u % 2
            col = pl.multiple_of(u * 256, 256)
            xt[pl.ds(64, 128), pl.ds(col, 256)] = rv[zh, xi, half, pl.ds(0, 256), :].T
            cat_tokens(xt, 0, col, rv[zh, xi, half, pl.ds(256, 128), :])
            return carry
        lax.fori_loop(0, 8, turn, 0)
        def tile(n, carry):
            cols = pl.ds(pl.multiple_of(n * 256, 256), 256)
            total = jnp.zeros((192, 256), f32)
            for k in range(4):
                total += jnp.dot(xt[pl.ds(0, 192), pl.ds(k * 512, 512)], lv[k, :, cols], preferred_element_type=f32)
            out_at(cols, total)
            return carry
        lax.fori_loop(0, 4, tile, 0)

    def own_out(cols, total):
        gqw[:, cols] = total

    def sent_out(slot):
        def put(cols, total):
            pqs[slot, :, cols] = total.astype(bf16)
        return put

    def input_part(zh, first=False):
        def build(u, carry):
            half, e = u // 2, u % 2
            rows = pl.ds(pl.multiple_of(u * 128, 128), 128)
            krows = pl.ds(pl.multiple_of(e * 128, 128), 128)
            for p in range(2):
                a, b = 2 * p, 2 * p + 1
                qa = fv[zh, a, half, pl.ds(256, 128), :]
                qb = fv[zh, b, half, pl.ds(256, 128), :]
                low = e == 0
                qa = jnp.where(low, qa[:, :64], qa[:, 64:])
                qb = jnp.where(low, qb[:, :64], qb[:, 64:])
                mt[rows, pl.ds(p * 384, 384)] = jnp.concatenate(
                    [qa, fv[zh, a, half, krows, :], qb, fv[zh, b, half, krows, :]], axis=1)
            return carry
        lax.fori_loop(0, 4, build, 0)
        def tile(n, carry):
            cols = pl.ds(pl.multiple_of(n * 256, 256), 256)
            part = lax.dot_general(mt[...], wv[cols, pl.ds(pl.multiple_of(zh * 768, 128), 768)],
                                   (((1,), (1,)), ((), ())), preferred_element_type=f32)
            if first:
                acc[:, cols] = gv[z, :, cols].astype(f32) + part
            else:
                acc[:, cols] += part
            return carry
        lax.fori_loop(0, 4, tile, 0)

    loads[0].wait()
    loads[1].wait()
    own = pltpu.make_async_copy(rv.at[z, x], fv.at[z, x], loc.at[5])
    own.start()
    weight_part(z, own_out)

    loads[2].wait()
    loads[3].wait()
    loads[4].wait()

    def arrive(d, j):
        zc[d, j].wait_recv()
        if j:
            xc[d, j].start()

    for d, j in ZORDER[:4]:
        arrive(d, j)
    for d in (1, 3, 2):
        ac[d].wait_recv()
    def turn_att(u, carry):
        zi, half = u // 2, u % 2
        col = pl.multiple_of(u * 256, 256)
        for xh in range(4):
            cat_tokens(xt, xh * 64, col, at[xh, zi, half])
        return carry
    lax.fori_loop(0, 8, turn_att, 0)
    def att_tile(n, carry):
        cols = pl.ds(pl.multiple_of(n * 256, 256), 256)
        total = jnp.zeros((256, 256), f32)
        for k in range(4):
            total += jnp.dot(xt[:, pl.ds(k * 512, 512)], gv[k, :, cols], preferred_element_type=f32)
        for xh in range(4):
            pos[xh, :, cols] = total[xh * 64:(xh + 1) * 64]
        return carry
    lax.fori_loop(0, 4, att_tile, 0)
    gow[...] = pos[x]
    oc = {}
    for d in (1, 3, 2):
        oc[d] = remote(pos.at[xr4(d)], por.at[d - 1], os_.at[d - 1], or_.at[d - 1], to_x(d))
        oc[d].start()
    for d, j in ZORDER[4:8]:
        arrive(d, j)
    locals_ = {}
    def take_own(e):
        locals_[e] = pltpu.make_async_copy(rv.at[zr4(-e), x], fv.at[zr4(-e), x], loc.at[5 + e])
        locals_[e].start()
    qc = {}
    def send_part(e):
        weight_part(zr4(-e), sent_out(e - 1))
        qc[e] = remote(pqs.at[e - 1], pqr.at[e - 1], qs.at[e - 1], qr.at[e - 1], to_z(-e))
        qc[e].start()
    for e in (1, 3):
        take_own(e)
        send_part(e)
    for d in (1, 3, 2):
        xc[0, d].wait_recv()
    own.wait()
    input_part(z, first=True)
    for d, j in ZORDER[8:]:
        arrive(d, j)
    take_own(2)
    send_part(2)
    for e in (1, 3, 2):
        for d in (1, 3, 2):
            xc[e, d].wait_recv()
        locals_[e].wait()
        input_part(zr4(-e))
    gin[...] = acc[...].astype(bf16)
    for d in (1, 3, 2):
        oc[d].wait_recv()
        gow[...] += por[d - 1].astype(f32)
    for d in (1, 3, 2):
        qc[d].wait_recv()
        gqw[...] += pqr[d - 1].astype(f32)
    for c in [*zc.values(), *xc.values(), *ac.values(), *oc.values(), *qc.values()]:
        c.wait_send()

def finish(gqkv, att, lg, gz, w, cid=1):
    anys = pl.BlockSpec(memory_space=pl.ANY)
    vm = pl.BlockSpec(memory_space=pltpu.VMEM)
    D = pltpu.SemaphoreType.DMA
    return pl.pallas_call(finish_kernel,
        out_shape=[jax.ShapeDtypeStruct((512, 1024), bf16), jax.ShapeDtypeStruct((192, 1024), f32), jax.ShapeDtypeStruct((64, 1024), f32)],
        in_specs=[anys] * 5, out_specs=[vm] * 3,
        scratch_shapes=[
            pltpu.VMEM((4, 4, 2, 384, 128), bf16), pltpu.VMEM((4, 4, 2, 384, 128), bf16), pltpu.VMEM((4, 4, 2, 128, 128), bf16),
            pltpu.VMEM((4, 512, 1024), bf16), pltpu.VMEM((4, 512, 1024), bf16), pltpu.VMEM((1024, 3072), bf16),
            pltpu.VMEM((256, 2048), bf16), pltpu.VMEM((512, 768), bf16), pltpu.VMEM((512, 1024), f32),
            pltpu.VMEM((3, 192, 1024), bf16), pltpu.VMEM((3, 192, 1024), bf16),
            pltpu.VMEM((4, 64, 1024), f32), pltpu.VMEM((3, 64, 1024), f32),
            D((9,)), D((3, 4)), D((3, 4)), D((4, 3)), D((4, 3)), D((3,)), D((3,)), D((3,)), D((3,)), D((3,)), D((3,))],
        compiler_params=pltpu.CompilerParams(collective_id=cid, has_side_effects=True, vmem_limit_bytes=56 * 2**20),
        cost_estimate=pl.CostEstimate(flops=8 * 10**9, bytes_accessed=2 * 10**7, transcendentals=0),
    )(gqkv.reshape(4, 4, 2, 384, 128), att.reshape(4, 4, 2, 128, 128), lg, gz, w)


def passed_along(block, axis, distance):
    devices = range(lax.axis_size(axis))
    route = [((i - distance) % len(devices), i) for i in devices]
    return lax.ppermute(block, axis, route)


def local(layer_input, handoff, qkv_weight, out_weight, neighbours, counts):
    inputs = layer_input[0]
    grad_out = passed_along(handoff, "pipe", -1)[0]
    weight_in = qkv_weight[0]
    weight_out = out_weight[0]
    projected = jnp.dot(inputs, weight_in, preferred_element_type=f32).astype(bf16)
    grad_attn = jnp.dot(grad_out, weight_out.T, preferred_element_type=f32).astype(bf16)
    p = projected.reshape(2, 2, 128, 16, 192)
    kv = p[..., 64:].reshape(2, 256, 16, 128).transpose(2, 0, 1, 3)
    q = p[..., :64].transpose(3, 0, 2, 1, 4).reshape(16, 2, 128, 128)
    d = grad_attn.reshape(2, 2, 128, 16, 64).transpose(3, 0, 2, 1, 4).reshape(16, 2, 128, 128)
    packed = jnp.concatenate([kv, q], axis=2)
    hq = lax.all_to_all(packed, "seq", split_axis=0, concat_axis=0, tiled=True)
    hd = lax.all_to_all(d, "seq", split_axis=0, concat_axis=0, tiled=True)
    gqkv, att = attention(hq.reshape(32, 384, 128), hd.reshape(32, 128, 128), neighbours[0, 0], counts[0, 0])
    along_x = [[4 * a + b for b in range(4)] for a in range(4)]
    along_z = [[4 * b + a for b in range(4)] for a in range(4)]
    lg = lax.all_gather(inputs, "seq", axis_index_groups=along_x)
    gz = lax.all_gather(grad_out, "seq", axis_index_groups=along_z)
    grad_input, grad_qkv_weight, grad_out_weight = finish(gqkv, att, lg, gz, weight_in)
    return (grad_input[None], grad_qkv_weight[None], grad_out_weight[None])


def solution(mesh):
    placed = (
        P("pipe", "seq", None),
        P("pipe", "seq", None),
        P("pipe", None, None),
        P("pipe", None, None),
        P("pipe", "seq", None, None),
        P("pipe", "seq", None),
    )
    return jax.shard_map(
        local,
        mesh=mesh,
        in_specs=placed,
        out_specs=(P("pipe", "seq", None), P("pipe", "seq", None), P("pipe", "seq", None)),
        check_vma=False,
    )
```

```python
import functools
import jax, jax.numpy as jnp
from jax import lax
from jax.experimental import pallas as pl
from jax.experimental.pallas import tpu as pltpu
from jax.sharding import PartitionSpec as P
HEAD_DIM=64; BLOCK=128; MAXNB=8; QB=64; GROUP=4
f32=jnp.float32; bf16=jnp.bfloat16

def attn_body(order, nb, cnt, hq, qd, gqa, acc, kvt, group, i, slots):
    scale = HEAD_DIM ** -0.5
    half_row = lax.broadcasted_iota(jnp.int32, (BLOCK, BLOCK), 0) < HEAD_DIM
    half_lane = lax.broadcasted_iota(jnp.int32, (BLOCK, BLOCK), 1) < HEAD_DIM
    zero = jnp.zeros((BLOCK, BLOCK), bf16)
    dn = (((1,), (0,)), ((), ()))
    mm = lambda a, b: lax.dot_general(a, b, dn, preferred_element_type=f32)
    chains = []
    for g in range(group):
        b = order[i * group + g]
        chains.append((b, cnt[b], [nb[b, j] for j in range(slots)]))
    st = []
    for b, c, ns in chains:
        own = qd[b]
        own_t = own.T
        q_t = jnp.where(half_row, own_t * jnp.asarray(scale, bf16), zero)
        d_t = jnp.where(half_row, zero, own_t)
        right = jnp.concatenate([q_t, d_t], axis=1)
        scores, dps = [], []
        for j in range(slots):
            keys = load_keys(hq, ns[j])
            both = mm(keys, right)
            s = both[:, :BLOCK]
            if j > 0:
                s = jnp.where(j < c, s, -jnp.inf)
            scores.append(s); dps.append(both[:, BLOCK:])
        st.append((own, own_t, scores, dps))
    st2 = []
    for (b, c, ns), (own, own_t, scores, dps) in zip(chains, st):
        top = scores[0]
        for s in scores[1:]:
            top = jnp.maximum(top, s)
        top = jnp.max(top, axis=0, keepdims=True)
        es = [jnp.exp(s - top) for s in scores]
        tot = es[0]
        for e in es[1:]:
            tot = tot + e
        inv = 1.0 / jnp.sum(tot, axis=0, keepdims=True)
        ps = [e * inv for e in es]
        st2.append((own, own_t, dps, ps))
    for (b, c, ns), (own, own_t, dps, ps) in zip(chains, st2):
        low = [p.astype(bf16) for p in ps]
        att_t = jnp.zeros((HEAD_DIM, BLOCK), f32)
        for j in range(slots):
            att_t = att_t + mm(kvt[ns[j], HEAD_DIM:, :], low[j])
        att_t = att_t.astype(bf16)
        dot = jnp.sum(own_t[HEAD_DIM:, :].astype(f32) * att_t.astype(f32), axis=0, keepdims=True)
        ds = [(p * (dp - dot)).astype(bf16) for p, dp in zip(ps, dps)]
        left = jnp.concatenate([jnp.where(half_lane, own * jnp.asarray(scale, bf16), zero), jnp.where(half_lane, zero, own)], axis=0)
        gq_t = jnp.zeros((HEAD_DIM, BLOCK), f32)
        for j in range(slots):
            gq_t = gq_t + mm(kvt[ns[j], :HEAD_DIM, :], ds[j])
            acc[ns[j]] += mm(jnp.concatenate([ds[j], low[j]], axis=1), left)
        gq_t = (gq_t * scale).astype(bf16)
        gqa[b] = jnp.concatenate([gq_t, att_t], axis=0).T

def load_keys(hq, n):
    half, rows = key_rows(n)
    return hq[half, rows, :]


def key_rows(n):
    return n // 2, pl.ds(pl.multiple_of((n % 2) * BLOCK, BLOCK), BLOCK)


def attn_kernel(order, nb, cnt, hq, hd, hg, ha, acc, kvt, qd, gqa, *, group):
    def prep(u, carry):
        for e in range(2):
            acc[2 * u + e] = jnp.zeros((BLOCK, BLOCK), f32)
            kvt[2 * u + e] = hq[u, pl.ds(e * BLOCK, BLOCK), :].T
        q = hq[u, pl.ds(256, BLOCK), :]
        d = hd[u]
        qd[2 * u] = jnp.concatenate([q[:, :HEAD_DIM], d[:, :HEAD_DIM]], axis=1)
        qd[2 * u + 1] = jnp.concatenate([q[:, HEAD_DIM:], d[:, HEAD_DIM:]], axis=1)
        return carry
    lax.fori_loop(0, QB // 2, prep, 0, unroll=2)

    def step(i, carry):
        most = cnt[order[i * group]]
        for g in range(1, group):
            most = jnp.maximum(most, cnt[order[i * group + g]])
        for slots in range(1, MAXNB + 1):
            @pl.when(most == slots)
            def run():
                attn_body(order, nb, cnt, hq, qd, gqa, acc, kvt, group, i, slots)
        return carry
    lax.fori_loop(0, QB // group, step, 0)

    def fin(u, carry):
        for e in range(2):
            hg[u, pl.ds(e * BLOCK, BLOCK), :] = acc[2 * u + e].astype(bf16)
        a, b = gqa[2 * u], gqa[2 * u + 1]
        hg[u, pl.ds(256, BLOCK), :] = jnp.concatenate([a[:, :HEAD_DIM], b[:, :HEAD_DIM]], axis=1)
        ha[u] = jnp.concatenate([a[:, HEAD_DIM:], b[:, HEAD_DIM:]], axis=1)
        return carry
    lax.fori_loop(0, QB // 2, fin, 0, unroll=2)


def attention(hq, hd, nb, cnt, group=GROUP):
    order = jnp.argsort(cnt).astype(jnp.int32)
    sm = pl.BlockSpec(memory_space=pltpu.SMEM)
    vm = pl.BlockSpec(memory_space=pltpu.VMEM)
    return pl.pallas_call(
        functools.partial(attn_kernel, group=group),
        out_shape=[jax.ShapeDtypeStruct((QB // 2, 384, 128), bf16), jax.ShapeDtypeStruct((QB // 2, 128, 128), bf16)],
        in_specs=[sm, sm, sm, vm, vm],
        out_specs=[vm, vm],
        scratch_shapes=[
            pltpu.VMEM((QB, BLOCK, 128), f32),
            pltpu.VMEM((QB, 128, 128), bf16),
            pltpu.VMEM((QB, 128, 128), bf16),
            pltpu.VMEM((QB, 128, 128), bf16),
        ],
        compiler_params=pltpu.CompilerParams(vmem_limit_bytes=56 * 2**20),
        cost_estimate=pl.CostEstimate(flops=2 * 512 * 128 * 128 * 64 * 6, bytes_accessed=2**23, transcendentals=512 * 128 * 128),
    )(order, nb, cnt, hq, hd)


MESH = pl.DeviceIdType.MESH

def cat_tokens(dst, row, col, pair):
    turned = pair.T
    dst[pl.ds(row, HEAD_DIM), pl.ds(col, 128)] = turned[:HEAD_DIM]
    dst[pl.ds(row, HEAD_DIM), pl.ds(col + 128, 128)] = turned[HEAD_DIM:]

def finish_kernel(gqkv, att, lg, gz, w, gin, gqw, gow,
                  rv, fv, at, lv, gv, wv, xt, mt, acc, pqs, pqr, pos, por,
                  loc, zs, zr, xs, xr, as_, ar, qs, qr, os_, or_):
    pipe = lax.axis_index("pipe")
    me = lax.axis_index("seq")
    z, x = me // 4, me % 4
    zr4 = lambda d: (z + d) % 4
    xr4 = lambda d: (x + d) % 4
    def to_z(d): return (pipe, zr4(d) * 4 + x)
    def to_x(d): return (pipe, z * 4 + xr4(d))
    barrier = pltpu.get_barrier_semaphore()
    for d in (1, 2, 3):
        pl.semaphore_signal(barrier, inc=1, device_id=to_z(d), device_id_type=MESH)
        pl.semaphore_signal(barrier, inc=1, device_id=to_x(d), device_id_type=MESH)
    loads = [pltpu.make_async_copy(gqkv.at[z], rv.at[z], loc.at[0]),
             pltpu.make_async_copy(lg, lv, loc.at[1]),
             pltpu.make_async_copy(att.at[:, x], at.at[x], loc.at[2]),
             pltpu.make_async_copy(gz, gv, loc.at[3]),
             pltpu.make_async_copy(w, wv, loc.at[4])]
    for c in loads:
        c.start()
    pl.semaphore_wait(barrier, 6)

    def remote(src, dst, ss, rs, dev):
        return pltpu.make_async_remote_copy(src_ref=src, dst_ref=dst, send_sem=ss, recv_sem=rs, device_id=dev, device_id_type=MESH)

    ZORDER = [(d, j) for j in (1, 3, 2, 0) for d in (1, 3)] + [(2, j) for j in (1, 3, 2, 0)]
    zc = {}
    for d, j in ZORDER:
        zc[d, j] = remote(gqkv.at[zr4(d), xr4(j)], rv.at[z, xr4(j)], zs.at[d - 1, j], zr.at[d - 1, j], to_z(d))
    xc, ac = {}, {}
    for d in (1, 3, 2):
        xc[0, d] = remote(gqkv.at[z, xr4(d)], fv.at[z, x], xs.at[0, d - 1], xr.at[0, d - 1], to_x(d))
        ac[d] = remote(att.at[:, xr4(d)], at.at[x], as_.at[d - 1], ar.at[d - 1], to_x(d))
        for e in (1, 3, 2):
            xc[e, d] = remote(rv.at[zr4(-e), xr4(d)], fv.at[zr4(-e), x], xs.at[e, d - 1], xr.at[e, d - 1], to_x(d))
    for key in ZORDER:
        zc[key].start()
    for d in (1, 3, 2):
        xc[0, d].start()
    for d in (1, 3, 2):
        ac[d].start()

    def weight_part(zh, out_at):
        def turn(u, carry):
            xi, half = u // 2, u % 2
            col = pl.multiple_of(u * 256, 256)
            xt[pl.ds(64, 128), pl.ds(col, 256)] = rv[zh, xi, half, pl.ds(0, 256), :].T
            cat_tokens(xt, 0, col, rv[zh, xi, half, pl.ds(256, 128), :])
            return carry
        lax.fori_loop(0, 8, turn, 0)
        def tile(n, carry):
            cols = pl.ds(pl.multiple_of(n * 256, 256), 256)
            total = jnp.zeros((192, 256), f32)
            for k in range(4):
                total += jnp.dot(xt[pl.ds(0, 192), pl.ds(k * 512, 512)], lv[k, :, cols], preferred_element_type=f32)
            out_at(cols, total)
            return carry
        lax.fori_loop(0, 4, tile, 0)

    def own_out(cols, total):
        gqw[:, cols] = total

    def sent_out(slot):
        def put(cols, total):
            pqs[slot, :, cols] = total.astype(bf16)
        return put

    def input_part(zh, first=False):
        def build(u, carry):
            half, e = u // 2, u % 2
            rows = pl.ds(pl.multiple_of(u * 128, 128), 128)
            krows = pl.ds(pl.multiple_of(e * 128, 128), 128)
            for p in range(2):
                a, b = 2 * p, 2 * p + 1
                qa = fv[zh, a, half, pl.ds(256, 128), :]
                qb = fv[zh, b, half, pl.ds(256, 128), :]
                low = e == 0
                qa = jnp.where(low, qa[:, :64], qa[:, 64:])
                qb = jnp.where(low, qb[:, :64], qb[:, 64:])
                mt[rows, pl.ds(p * 384, 384)] = jnp.concatenate(
                    [qa, fv[zh, a, half, krows, :], qb, fv[zh, b, half, krows, :]], axis=1)
            return carry
        lax.fori_loop(0, 4, build, 0)
        def tile(n, carry):
            cols = pl.ds(pl.multiple_of(n * 256, 256), 256)
            part = lax.dot_general(mt[...], wv[cols, pl.ds(pl.multiple_of(zh * 768, 128), 768)],
                                   (((1,), (1,)), ((), ())), preferred_element_type=f32)
            if first:
                acc[:, cols] = gv[z, :, cols].astype(f32) + part
            else:
                acc[:, cols] += part
            return carry
        lax.fori_loop(0, 4, tile, 0)

    loads[0].wait()
    loads[1].wait()
    own = pltpu.make_async_copy(rv.at[z, x], fv.at[z, x], loc.at[5])
    own.start()
    weight_part(z, own_out)

    loads[2].wait()
    loads[3].wait()
    loads[4].wait()

    def arrive(d, j):
        zc[d, j].wait_recv()
        if j:
            xc[d, j].start()

    for d, j in ZORDER[:4]:
        arrive(d, j)
    for d in (1, 3, 2):
        ac[d].wait_recv()
    def turn_att(u, carry):
        zi, half = u // 2, u % 2
        col = pl.multiple_of(u * 256, 256)
        for xh in range(4):
            cat_tokens(xt, xh * 64, col, at[xh, zi, half])
        return carry
    lax.fori_loop(0, 8, turn_att, 0)
    def att_tile(n, carry):
        cols = pl.ds(pl.multiple_of(n * 256, 256), 256)
        total = jnp.zeros((256, 256), f32)
        for k in range(4):
            total += jnp.dot(xt[:, pl.ds(k * 512, 512)], gv[k, :, cols], preferred_element_type=f32)
        for xh in range(4):
            pos[xh, :, cols] = total[xh * 64:(xh + 1) * 64]
        return carry
    lax.fori_loop(0, 4, att_tile, 0)
    gow[...] = pos[x]
    oc = {}
    for d in (1, 3, 2):
        oc[d] = remote(pos.at[xr4(d)], por.at[d - 1], os_.at[d - 1], or_.at[d - 1], to_x(d))
        oc[d].start()
    for d, j in ZORDER[4:8]:
        arrive(d, j)
    locals_ = {}
    def take_own(e):
        locals_[e] = pltpu.make_async_copy(rv.at[zr4(-e), x], fv.at[zr4(-e), x], loc.at[5 + e])
        locals_[e].start()
    qc = {}
    def send_part(e):
        weight_part(zr4(-e), sent_out(e - 1))
        qc[e] = remote(pqs.at[e - 1], pqr.at[e - 1], qs.at[e - 1], qr.at[e - 1], to_z(-e))
        qc[e].start()
    for e in (1, 3):
        take_own(e)
        send_part(e)
    for d in (1, 3, 2):
        xc[0, d].wait_recv()
    own.wait()
    input_part(z, first=True)
    for d, j in ZORDER[8:]:
        arrive(d, j)
    take_own(2)
    send_part(2)
    for e in (1, 3, 2):
        for d in (1, 3, 2):
            xc[e, d].wait_recv()
        locals_[e].wait()
        input_part(zr4(-e))
    gin[...] = acc[...].astype(bf16)
    for d in (1, 3, 2):
        oc[d].wait_recv()
        gow[...] += por[d - 1].astype(f32)
    for d in (1, 3, 2):
        qc[d].wait_recv()
        gqw[...] += pqr[d - 1].astype(f32)
    for c in [*zc.values(), *xc.values(), *ac.values(), *oc.values(), *qc.values()]:
        c.wait_send()

def finish(gqkv, att, lg, gz, w, cid=1):
    anys = pl.BlockSpec(memory_space=pl.ANY)
    vm = pl.BlockSpec(memory_space=pltpu.VMEM)
    D = pltpu.SemaphoreType.DMA
    return pl.pallas_call(finish_kernel,
        out_shape=[jax.ShapeDtypeStruct((512, 1024), bf16), jax.ShapeDtypeStruct((192, 1024), f32), jax.ShapeDtypeStruct((64, 1024), f32)],
        in_specs=[anys] * 5, out_specs=[vm] * 3,
        scratch_shapes=[
            pltpu.VMEM((4, 4, 2, 384, 128), bf16), pltpu.VMEM((4, 4, 2, 384, 128), bf16), pltpu.VMEM((4, 4, 2, 128, 128), bf16),
            pltpu.VMEM((4, 512, 1024), bf16), pltpu.VMEM((4, 512, 1024), bf16), pltpu.VMEM((1024, 3072), bf16),
            pltpu.VMEM((256, 2048), bf16), pltpu.VMEM((512, 768), bf16), pltpu.VMEM((512, 1024), f32),
            pltpu.VMEM((3, 192, 1024), bf16), pltpu.VMEM((3, 192, 1024), bf16),
            pltpu.VMEM((4, 64, 1024), f32), pltpu.VMEM((3, 64, 1024), f32),
            D((9,)), D((3, 4)), D((3, 4)), D((4, 3)), D((4, 3)), D((3,)), D((3,)), D((3,)), D((3,)), D((3,)), D((3,))],
        compiler_params=pltpu.CompilerParams(collective_id=cid, has_side_effects=True, vmem_limit_bytes=56 * 2**20),
        cost_estimate=pl.CostEstimate(flops=8 * 10**9, bytes_accessed=2 * 10**7, transcendentals=0),
    )(gqkv.reshape(4, 4, 2, 384, 128), att.reshape(4, 4, 2, 128, 128), lg, gz, w)


def begin_kernel(lin, hand, w, wo, hqkv, hd, lg, g,
                 lv, gv, w4, wov, sq, sd,
                 loc, hs, hr, gs, gr, zs, zr, ds_, dr):
    pipe = lax.axis_index("pipe")
    me = lax.axis_index("seq")
    z, x = me // 4, me % 4
    zr4 = lambda d: (z + d) % 4
    xr4 = lambda d: (x + d) % 4
    def to_z(d): return (pipe, zr4(d) * 4 + x)
    def to_x(d): return (pipe, z * 4 + xr4(d))
    barrier = pltpu.get_barrier_semaphore()
    for d in range(1, 16):
        pl.semaphore_signal(barrier, inc=1, device_id=(pipe, (me + d) % 16), device_id_type=MESH)
    pl.semaphore_signal(barrier, inc=1, device_id=((pipe + 1) % 8, me), device_id_type=MESH)

    def here(src, dst, sem):
        return pltpu.make_async_copy(src, dst, sem)

    def remote(src, dst, ss, rs, dev):
        return pltpu.make_async_remote_copy(src_ref=src, dst_ref=dst, send_sem=ss, recv_sem=rs, device_id=dev, device_id_type=MESH)

    load_l = here(lin, lv.at[x], loc.at[0])
    load_l.start()
    load_w = []
    for zh in range(4):
        first = pl.multiple_of(((12 * zh + 3 * x) // 2) * 128, 128)
        load_w.append(here(w.at[:, pl.ds(first, 256)], w4.at[zh], loc.at[1 + zh]))
        load_w[-1].start()
    load_wo = here(wo, wov, loc.at[5])
    load_wo.start()
    pl.semaphore_wait(barrier, 16)

    given = remote(hand, gv, hs, hr, ((pipe + 7) % 8, me))
    right = {h: remote(lin.at[h], lv.at[x, h], gs.at[0, h], gr.at[0, h], to_x(1)) for h in (0, 1)}
    left = {h: remote(lin.at[h], lv.at[x, h], gs.at[1, h], gr.at[1, h], to_x(3)) for h in (0, 1)}
    right[2] = remote(lv.at[xr4(3), 0], lv.at[xr4(3), 0], gs.at[0, 2], gr.at[0, 2], to_x(1))
    left[2] = remote(lv.at[xr4(1), 1], lv.at[xr4(1), 1], gs.at[1, 2], gr.at[1, 2], to_x(3))
    right[0].start()
    left[1].start()
    given.start()
    right[1].start()
    left[0].start()

    zc, own, kept = {}, [], []

    def project(r, h):
        xs = xr4(r)
        def head(zh, carry):
            part = jnp.dot(lv[xs, h], w4[zh], preferred_element_type=f32).astype(bf16)
            part = jnp.where(x % 2 == 1, jnp.concatenate([part[:, 64:], part[:, :64]], axis=1), part)
            sq[xs, zh, h, pl.ds(0, 256), :] = part[:, 64:192]
            sq[xs, zh, h, pl.ds(256, 128), :] = jnp.concatenate([part[:128, :64], part[128:, :64]], axis=1)
            return carry
        lax.fori_loop(0, 4, head, 0)
        for d in (1, 3, 2):
            zc[d, r, h] = remote(sq.at[xs, zr4(d), h], hqkv.at[z, xs, h], zs.at[d - 1, r, h], zr.at[d - 1, r, h], to_z(d))
            zc[d, r, h].start()
        own.append(here(sq.at[xs, z, h], hqkv.at[z, xs, h], loc.at[6 + 2 * r + h]))
        own[-1].start()

    load_l.wait()
    for c in load_w:
        c.wait()
    project(0, 0)
    project(0, 1)
    right[0].wait_recv()
    right[2].start()
    project(3, 0)
    left[1].wait_recv()
    left[2].start()
    project(1, 1)

    given.wait_recv()
    load_wo.wait()
    own.append(here(gv, g, loc.at[14]))
    own[-1].start()
    def heads(n, carry):
        rows = pl.ds(pl.multiple_of(n * 256, 256), 256)
        part = lax.dot_general(gv[...], wov[rows, :], (((1,), (1,)), ((), ())), preferred_element_type=f32).astype(bf16)
        for i in range(4):
            cols = part[:, i * 64:(i + 1) * 64]
            for h in range(2):
                sd[n * 4 + i, h] = jnp.concatenate([cols[h * 256:h * 256 + 128], cols[h * 256 + 128:h * 256 + 256]], axis=1)
        return carry
    lax.fori_loop(0, 4, heads, 0)
    dc = {}
    for d in (1, 15, 4, 12, 5, 11, 3, 13, 2, 14, 8, 6, 10, 7, 9):
        dc[d] = remote(sd.at[(me + d) % 16], hd.at[z, x], ds_.at[d - 1], dr.at[d - 1], (pipe, (me + d) % 16))
        dc[d].start()
    own.append(here(sd.at[me], hd.at[z, x], loc.at[15]))
    own[-1].start()

    right[1].wait_recv()
    project(3, 1)
    left[0].wait_recv()
    project(1, 0)
    right[2].wait_recv()
    project(2, 0)
    left[2].wait_recv()
    project(2, 1)
    store = here(lv, lg, loc.at[16])
    store.start()
    for c in [*zc.values(), *dc.values()]:
        c.wait_recv()
    for c in own:
        c.wait()
    store.wait()
    given.wait_send()
    for c in [*right.values(), *left.values(), *zc.values(), *dc.values()]:
        c.wait_send()


def begin(lin, hand, w, wo, cid=2):
    anys = pl.BlockSpec(memory_space=pl.ANY)
    D = pltpu.SemaphoreType.DMA
    return pl.pallas_call(
        begin_kernel,
        out_shape=[
            jax.ShapeDtypeStruct((4, 4, 2, 384, 128), bf16),
            jax.ShapeDtypeStruct((4, 4, 2, 128, 128), bf16),
            jax.ShapeDtypeStruct((4, 2, 256, 1024), bf16),
            jax.ShapeDtypeStruct((512, 1024), bf16),
        ],
        in_specs=[anys] * 4,
        out_specs=[anys] * 4,
        scratch_shapes=[
            pltpu.VMEM((4, 2, 256, 1024), bf16), pltpu.VMEM((512, 1024), bf16),
            pltpu.VMEM((4, 1024, 256), bf16), pltpu.VMEM((1024, 1024), bf16),
            pltpu.VMEM((4, 4, 2, 384, 128), bf16), pltpu.VMEM((16, 2, 128, 128), bf16),
            D((17,)), D, D, D((2, 3)), D((2, 3)), D((3, 4, 2)), D((3, 4, 2)), D((15,)), D((15,)),
        ],
        compiler_params=pltpu.CompilerParams(collective_id=cid, has_side_effects=True, vmem_limit_bytes=48 * 2**20),
        cost_estimate=pl.CostEstimate(flops=4 * 10**9, bytes_accessed=2 * 10**7, transcendentals=0),
    )(lin.reshape(2, 256, 1024), hand, w, wo)


def local(layer_input, handoff, qkv_weight, out_weight, neighbours, counts):
    weight_in = qkv_weight[0]
    hqkv, hd, lg, grad_out = begin(layer_input[0], handoff[0], weight_in, out_weight[0])
    along_z = [[4 * b + a for b in range(4)] for a in range(4)]
    gz = lax.all_gather(grad_out, "seq", axis_index_groups=along_z)
    gqkv, att = attention(hqkv.reshape(32, 384, 128), hd.reshape(32, 128, 128), neighbours[0, 0], counts[0, 0])
    grad_input, grad_qkv_weight, grad_out_weight = finish(gqkv, att, lg.reshape(4, 512, 1024), gz, weight_in)
    return (grad_input[None], grad_qkv_weight[None], grad_out_weight[None])


def solution(mesh):
    placed = (
        P("pipe", "seq", None),
        P("pipe", "seq", None),
        P("pipe", None, None),
        P("pipe", None, None),
        P("pipe", "seq", None, None),
        P("pipe", "seq", None),
    )
    return jax.shard_map(
        local,
        mesh=mesh,
        in_specs=placed,
        out_specs=(P("pipe", "seq", None), P("pipe", "seq", None), P("pipe", "seq", None)),
        check_vma=False,
    )
```

```python
import functools
import jax, jax.numpy as jnp
from jax import lax
from jax.experimental import pallas as pl
from jax.experimental.pallas import tpu as pltpu
from jax.sharding import PartitionSpec as P
HEAD_DIM=64; BLOCK=128; MAXNB=8; QB=64; GROUP=8
f32=jnp.float32; bf16=jnp.bfloat16

def attn_body(order, nb, cnt, hq, qd, gqa, acc, kvt, group, i, slots):
    scale = HEAD_DIM ** -0.5
    half_row = lax.broadcasted_iota(jnp.int32, (BLOCK, BLOCK), 0) < HEAD_DIM
    half_lane = lax.broadcasted_iota(jnp.int32, (BLOCK, BLOCK), 1) < HEAD_DIM
    zero = jnp.zeros((BLOCK, BLOCK), bf16)
    dn = (((1,), (0,)), ((), ()))
    mm = lambda a, b: lax.dot_general(a, b, dn, preferred_element_type=f32)
    chains = []
    for g in range(group):
        b = order[i * group + g]
        chains.append((b, cnt[b], [nb[j, b] for j in range(slots)]))
    st = []
    for b, c, ns in chains:
        own = qd[b]
        own_t = own.T
        q_t = jnp.where(half_row, own_t * jnp.asarray(scale, bf16), zero)
        d_t = jnp.where(half_row, zero, own_t)
        right = jnp.concatenate([q_t, d_t], axis=1)
        scores, dps = [], []
        every = mm(jnp.concatenate([load_keys(hq, ns[j]) for j in range(slots)], axis=0), right)
        for j in range(slots):
            both = every[j * BLOCK:(j + 1) * BLOCK]
            s = both[:, :BLOCK]
            if j > 0:
                s = jnp.where(j < c, s, -jnp.inf)
            scores.append(s); dps.append(both[:, BLOCK:])
        st.append((own, own_t, scores, dps))
    st2 = []
    for (b, c, ns), (own, own_t, scores, dps) in zip(chains, st):
        top = scores[0]
        for s in scores[1:]:
            top = jnp.maximum(top, s)
        top = jnp.max(top, axis=0, keepdims=True)
        es = [jnp.exp(s - top) for s in scores]
        tot = es[0]
        for e in es[1:]:
            tot = tot + e
        inv = 1.0 / jnp.sum(tot, axis=0, keepdims=True)
        ps = [e * inv for e in es]
        st2.append((own, own_t, dps, ps))
    for (b, c, ns), (own, own_t, dps, ps) in zip(chains, st2):
        low = [p.astype(bf16) for p in ps]
        att_t = mm(jnp.concatenate([kvt[ns[j], HEAD_DIM:, :] for j in range(slots)], axis=1), jnp.concatenate(low, axis=0))
        att_t = att_t.astype(bf16)
        dot = jnp.sum(own_t[HEAD_DIM:, :].astype(f32) * att_t.astype(f32), axis=0, keepdims=True)
        ds = [(p * (dp - dot)).astype(bf16) for p, dp in zip(ps, dps)]
        left = jnp.concatenate([jnp.where(half_lane, own * jnp.asarray(scale, bf16), zero), jnp.where(half_lane, zero, own)], axis=0)
        low_all, ds_all = jnp.concatenate(low, axis=0), jnp.concatenate(ds, axis=0)
        terms = mm(jnp.concatenate([ds_all, low_all], axis=1), left)
        gq_t = mm(jnp.concatenate([kvt[ns[j], :HEAD_DIM, :] for j in range(slots)], axis=1), ds_all)
        for j in range(slots):
            acc[ns[j]] += terms[j * BLOCK:(j + 1) * BLOCK]
        gq_t = (gq_t * scale).astype(bf16)
        gqa[b] = jnp.concatenate([gq_t, att_t], axis=0).T

def load_keys(hq, n):
    half, rows = key_rows(n)
    return hq[half, rows, :]


def key_rows(n):
    return n // 2, pl.ds(pl.multiple_of((n % 2) * BLOCK, BLOCK), BLOCK)


def attn_kernel(nb, cnt, hq, hd, hg, ha, acc, kvt, qd, gqa, order, place, *, group):
    for c in range(MAXNB + 2):
        place[c] = 0

    def prep_keys(u, carry):
        for e in range(2):
            c = cnt[2 * u + e] + 1
            place[c] = place[c] + 1
            kvt[2 * u + e] = hq[u, pl.ds(e * BLOCK, BLOCK), :].T
        return carry
    lax.fori_loop(0, QB // 2, prep_keys, 0, unroll=2)
    for c in range(1, MAXNB + 1):
        place[c] = place[c] + place[c - 1]

    def prep_rows(u, carry):
        for e in range(2):
            c = cnt[2 * u + e]
            at = place[c]
            order[at] = 2 * u + e
            place[c] = at + 1
            acc[2 * u + e] = jnp.zeros((BLOCK, BLOCK), f32)
        q = hq[u, pl.ds(256, BLOCK), :]
        d = hd[u]
        qd[2 * u] = jnp.concatenate([q[:, :HEAD_DIM], d[:, :HEAD_DIM]], axis=1)
        qd[2 * u + 1] = jnp.concatenate([q[:, HEAD_DIM:], d[:, HEAD_DIM:]], axis=1)
        return carry
    lax.fori_loop(0, QB // 2, prep_rows, 0, unroll=2)

    def step(i, carry):
        most = cnt[order[i * group + group - 1]]
        for slots in range(1, MAXNB + 1):
            @pl.when(most == slots)
            def run():
                attn_body(order, nb, cnt, hq, qd, gqa, acc, kvt, group, i, slots)
        return carry
    lax.fori_loop(0, QB // group, step, 0)

    def fin(u, carry):
        for e in range(2):
            hg[u, pl.ds(e * BLOCK, BLOCK), :] = acc[2 * u + e].astype(bf16)
        a, b = gqa[2 * u], gqa[2 * u + 1]
        hg[u, pl.ds(256, BLOCK), :] = jnp.concatenate([a[:, :HEAD_DIM], b[:, :HEAD_DIM]], axis=1)
        ha[u] = jnp.concatenate([a[:, HEAD_DIM:], b[:, HEAD_DIM:]], axis=1)
        return carry
    lax.fori_loop(0, QB // 2, fin, 0, unroll=2)


def attention(hq, hd, nb, cnt, group=GROUP):
    sm = pl.BlockSpec(memory_space=pltpu.SMEM)
    vm = pl.BlockSpec(memory_space=pltpu.VMEM)
    return pl.pallas_call(
        functools.partial(attn_kernel, group=group),
        out_shape=[jax.ShapeDtypeStruct((QB // 2, 384, 128), bf16), jax.ShapeDtypeStruct((QB // 2, 128, 128), bf16)],
        in_specs=[sm, sm, vm, vm],
        out_specs=[vm, vm],
        scratch_shapes=[
            pltpu.VMEM((QB, BLOCK, 128), f32),
            pltpu.VMEM((QB, 128, 128), bf16),
            pltpu.VMEM((QB, 128, 128), bf16),
            pltpu.VMEM((QB, 128, 128), bf16),
            pltpu.SMEM((QB,), jnp.int32),
            pltpu.SMEM((MAXNB + 2,), jnp.int32),
        ],
        compiler_params=pltpu.CompilerParams(vmem_limit_bytes=56 * 2**20),
        cost_estimate=pl.CostEstimate(flops=2 * 512 * 128 * 128 * 64 * 6, bytes_accessed=2**23, transcendentals=512 * 128 * 128),
    )(nb.T, cnt, hq, hd)


MESH = pl.DeviceIdType.MESH

def cat_tokens(dst, row, col, pair):
    turned = pair.T
    dst[pl.ds(row, HEAD_DIM), pl.ds(col, 128)] = turned[:HEAD_DIM]
    dst[pl.ds(row, HEAD_DIM), pl.ds(col + 128, 128)] = turned[HEAD_DIM:]

def finish_kernel(gqkv, att, lg, gz, w, gin, gqw, gow,
                  rv, fv, at, lv, gv, wv, xt, mt, acc, pqs, pqr, pos, por, mine,
                  loc, zs, zr, xs, xr, as_, ar, qs, qr, os_, or_):
    pipe = lax.axis_index("pipe")
    me = lax.axis_index("seq")
    z, x = me // 4, me % 4
    zr4 = lambda d: (z + d) % 4
    xr4 = lambda d: (x + d) % 4
    def to_z(d): return (pipe, zr4(d) * 4 + x)
    def to_x(d): return (pipe, z * 4 + xr4(d))
    barrier = pltpu.get_barrier_semaphore()
    for d in (1, 2, 3):
        pl.semaphore_signal(barrier, inc=1, device_id=to_z(d), device_id_type=MESH)
        pl.semaphore_signal(barrier, inc=1, device_id=to_x(d), device_id_type=MESH)
    loads = [pltpu.make_async_copy(gqkv.at[z], rv.at[z], loc.at[0]),
             pltpu.make_async_copy(lg, lv, loc.at[1]),
             pltpu.make_async_copy(att.at[:, x], at.at[x], loc.at[2]),
             pltpu.make_async_copy(gz, gv, loc.at[3]),
             pltpu.make_async_copy(w, wv, loc.at[4])]
    for c in loads:
        c.start()
    pl.semaphore_wait(barrier, 6)

    def remote(src, dst, ss, rs, dev):
        return pltpu.make_async_remote_copy(src_ref=src, dst_ref=dst, send_sem=ss, recv_sem=rs, device_id=dev, device_id_type=MESH)

    ZORDER = [(d, j) for j in (1, 3, 2, 0) for d in (1, 3)] + [(2, j) for j in (1, 3, 2, 0)]
    zc = {}
    for d, j in ZORDER:
        zc[d, j] = remote(gqkv.at[zr4(d), xr4(j)], rv.at[z, xr4(j)], zs.at[d - 1, j], zr.at[d - 1, j], to_z(d))
    xc, ac = {}, {}
    for d in (1, 3, 2):
        xc[0, d] = remote(gqkv.at[z, xr4(d)], fv.at[z, x], xs.at[0, d - 1], xr.at[0, d - 1], to_x(d))
        ac[d] = remote(att.at[:, xr4(d)], at.at[x], as_.at[d - 1], ar.at[d - 1], to_x(d))
        for e in (1, 3, 2):
            xc[e, d] = remote(rv.at[zr4(-e), xr4(d)], fv.at[zr4(-e), x], xs.at[e, d - 1], xr.at[e, d - 1], to_x(d))
    for key in ZORDER:
        zc[key].start()
    for d in (1, 3, 2):
        xc[0, d].start()
    for d in (1, 3, 2):
        ac[d].start()

    def weight_part(zh, out_at):
        def turn(u, carry):
            xi, half = u // 2, u % 2
            col = pl.multiple_of(u * 256, 256)
            xt[pl.ds(64, 128), pl.ds(col, 256)] = rv[zh, xi, half, pl.ds(0, 256), :].T
            cat_tokens(xt, 0, col, rv[zh, xi, half, pl.ds(256, 128), :])
            return carry
        lax.fori_loop(0, 8, turn, 0)
        def tile(n, carry):
            cols = pl.ds(pl.multiple_of(n * 256, 256), 256)
            total = jnp.zeros((192, 256), f32)
            for k in range(4):
                total += jnp.dot(xt[pl.ds(0, 192), pl.ds(k * 512, 512)], lv[k, :, cols], preferred_element_type=f32)
            out_at(cols, total)
            return carry
        lax.fori_loop(0, 4, tile, 0)

    def own_out(cols, total):
        gqw[:, cols] = total

    def sent_out(slot):
        def put(cols, total):
            pqs[slot, :, cols] = total.astype(bf16)
        return put

    def input_part(zh, first=False):
        def build(u, carry):
            half, e = u // 2, u % 2
            rows = pl.ds(pl.multiple_of(u * 128, 128), 128)
            krows = pl.ds(pl.multiple_of(e * 128, 128), 128)
            for p in range(2):
                a, b = 2 * p, 2 * p + 1
                qa = fv[zh, a, half, pl.ds(256, 128), :]
                qb = fv[zh, b, half, pl.ds(256, 128), :]
                low = e == 0
                qa = jnp.where(low, qa[:, :64], qa[:, 64:])
                qb = jnp.where(low, qb[:, :64], qb[:, 64:])
                mt[rows, pl.ds(p * 384, 384)] = jnp.concatenate(
                    [qa, fv[zh, a, half, krows, :], qb, fv[zh, b, half, krows, :]], axis=1)
            return carry
        lax.fori_loop(0, 4, build, 0)
        def tile(n, carry):
            cols = pl.ds(pl.multiple_of(n * 256, 256), 256)
            part = lax.dot_general(mt[...], wv[cols, pl.ds(pl.multiple_of(zh * 768, 128), 768)],
                                   (((1,), (1,)), ((), ())), preferred_element_type=f32)
            if first:
                acc[:, cols] = gv[z, :, cols].astype(f32) + part
            else:
                acc[:, cols] += part
            return carry
        lax.fori_loop(0, 4, tile, 0)

    loads[0].wait()
    loads[1].wait()
    own = pltpu.make_async_copy(rv.at[z, x], fv.at[z, x], loc.at[5])
    own.start()
    weight_part(z, own_out)

    loads[2].wait()
    loads[3].wait()
    loads[4].wait()

    def arrive(d, j):
        zc[d, j].wait_recv()
        if j:
            xc[d, j].start()

    for d, j in ZORDER[:4]:
        arrive(d, j)
    for d in (1, 3, 2):
        ac[d].wait_recv()
    def turn_att(u, carry):
        zi, half = u // 2, u % 2
        col = pl.multiple_of(u * 256, 256)
        for xh in range(4):
            cat_tokens(xt, xh * 64, col, at[xh, zi, half])
        return carry
    lax.fori_loop(0, 8, turn_att, 0)
    def att_tile(n, carry):
        cols = pl.ds(pl.multiple_of(n * 256, 256), 256)
        total = jnp.zeros((256, 256), f32)
        for k in range(4):
            total += jnp.dot(xt[:, pl.ds(k * 512, 512)], gv[k, :, cols], preferred_element_type=f32)
        mine[:, cols] = total
        for xh in range(4):
            pos[xh, :, cols] = total[xh * 64:(xh + 1) * 64].astype(bf16)
        return carry
    lax.fori_loop(0, 4, att_tile, 0)
    gow[...] = mine[pl.ds(pl.multiple_of(x * 64, 64), 64), :]
    oc = {}
    for d in (1, 3, 2):
        oc[d] = remote(pos.at[xr4(d)], por.at[d - 1], os_.at[d - 1], or_.at[d - 1], to_x(d))
        oc[d].start()
    for d, j in ZORDER[4:8]:
        arrive(d, j)
    locals_ = {}
    def take_own(e):
        locals_[e] = pltpu.make_async_copy(rv.at[zr4(-e), x], fv.at[zr4(-e), x], loc.at[5 + e])
        locals_[e].start()
    qc = {}
    def send_part(e):
        weight_part(zr4(-e), sent_out(e - 1))
        qc[e] = remote(pqs.at[e - 1], pqr.at[e - 1], qs.at[e - 1], qr.at[e - 1], to_z(-e))
        qc[e].start()
    for e in (1, 3):
        take_own(e)
        send_part(e)
    for d in (1, 3, 2):
        xc[0, d].wait_recv()
    own.wait()
    input_part(z, first=True)
    for d, j in ZORDER[8:]:
        arrive(d, j)
    take_own(2)
    send_part(2)
    for e in (1, 3, 2):
        for d in (1, 3, 2):
            xc[e, d].wait_recv()
        locals_[e].wait()
        input_part(zr4(-e))
    gin[...] = acc[...].astype(bf16)
    for d in (1, 3, 2):
        oc[d].wait_recv()
        gow[...] += por[d - 1].astype(f32)
    for d in (1, 3, 2):
        qc[d].wait_recv()
        gqw[...] += pqr[d - 1].astype(f32)
    for c in [*zc.values(), *xc.values(), *ac.values(), *oc.values(), *qc.values()]:
        c.wait_send()

def finish(gqkv, att, lg, gz, w, cid=1):
    anys = pl.BlockSpec(memory_space=pl.ANY)
    vm = pl.BlockSpec(memory_space=pltpu.VMEM)
    D = pltpu.SemaphoreType.DMA
    return pl.pallas_call(finish_kernel,
        out_shape=[jax.ShapeDtypeStruct((512, 1024), bf16), jax.ShapeDtypeStruct((192, 1024), f32), jax.ShapeDtypeStruct((64, 1024), f32)],
        in_specs=[anys] * 5, out_specs=[vm] * 3,
        scratch_shapes=[
            pltpu.VMEM((4, 4, 2, 384, 128), bf16), pltpu.VMEM((4, 4, 2, 384, 128), bf16), pltpu.VMEM((4, 4, 2, 128, 128), bf16),
            pltpu.VMEM((4, 512, 1024), bf16), pltpu.VMEM((4, 512, 1024), bf16), pltpu.VMEM((1024, 3072), bf16),
            pltpu.VMEM((256, 2048), bf16), pltpu.VMEM((512, 768), bf16), pltpu.VMEM((512, 1024), f32),
            pltpu.VMEM((3, 192, 1024), bf16), pltpu.VMEM((3, 192, 1024), bf16),
            pltpu.VMEM((4, 64, 1024), bf16), pltpu.VMEM((3, 64, 1024), bf16), pltpu.VMEM((256, 1024), f32),
            D((9,)), D((3, 4)), D((3, 4)), D((4, 3)), D((4, 3)), D((3,)), D((3,)), D((3,)), D((3,)), D((3,)), D((3,))],
        compiler_params=pltpu.CompilerParams(collective_id=cid, has_side_effects=True, vmem_limit_bytes=56 * 2**20),
        cost_estimate=pl.CostEstimate(flops=8 * 10**9, bytes_accessed=2 * 10**7, transcendentals=0),
    )(gqkv.reshape(4, 4, 2, 384, 128), att.reshape(4, 4, 2, 128, 128), lg, gz, w)


def begin_kernel(lin, hand, w, wo, hqkv, hd, lg, g,
                 lv, gv, w4, wov, sq, sd, dv,
                 loc, hs, hr, gs, gr, zs, zr, ds_, dr, es, er):
    pipe = lax.axis_index("pipe")
    me = lax.axis_index("seq")
    z, x = me // 4, me % 4
    zr4 = lambda d: (z + d) % 4
    xr4 = lambda d: (x + d) % 4
    def to_z(d): return (pipe, zr4(d) * 4 + x)
    def to_x(d): return (pipe, z * 4 + xr4(d))
    barrier = pltpu.get_barrier_semaphore()
    for d in (1, 2, 3):
        pl.semaphore_signal(barrier, inc=1, device_id=to_z(d), device_id_type=MESH)
        pl.semaphore_signal(barrier, inc=1, device_id=to_x(d), device_id_type=MESH)
    pl.semaphore_signal(barrier, inc=1, device_id=((pipe + 1) % 8, me), device_id_type=MESH)

    def here(src, dst, sem):
        return pltpu.make_async_copy(src, dst, sem)

    def remote(src, dst, ss, rs, dev):
        return pltpu.make_async_remote_copy(src_ref=src, dst_ref=dst, send_sem=ss, recv_sem=rs, device_id=dev, device_id_type=MESH)

    load_l = here(lin, lv.at[x], loc.at[0])
    load_l.start()
    load_w = []
    for zh in range(4):
        first = pl.multiple_of(((12 * zh + 3 * x) // 2) * 128, 128)
        load_w.append(here(w.at[:, pl.ds(first, 256)], w4.at[zh], loc.at[1 + zh]))
        load_w[-1].start()
    load_wo = here(wo, wov, loc.at[5])
    load_wo.start()
    pl.semaphore_wait(barrier, 7)

    given = remote(hand, gv, hs, hr, ((pipe + 7) % 8, me))
    right = {h: remote(lin.at[h], lv.at[x, h], gs.at[0, h], gr.at[0, h], to_x(1)) for h in (0, 1)}
    left = {h: remote(lin.at[h], lv.at[x, h], gs.at[1, h], gr.at[1, h], to_x(3)) for h in (0, 1)}
    right[2] = remote(lv.at[xr4(3), 0], lv.at[xr4(3), 0], gs.at[0, 2], gr.at[0, 2], to_x(1))
    left[2] = remote(lv.at[xr4(1), 1], lv.at[xr4(1), 1], gs.at[1, 2], gr.at[1, 2], to_x(3))
    right[0].start()
    left[1].start()
    given.start()
    right[1].start()
    left[0].start()

    zc, own, kept = {}, [], []

    def project(r, h):
        xs = xr4(r)
        def head(zh, carry):
            part = jnp.dot(lv[xs, h], w4[zh], preferred_element_type=f32).astype(bf16)
            part = jnp.where(x % 2 == 1, jnp.concatenate([part[:, 64:], part[:, :64]], axis=1), part)
            sq[xs, zh, h, pl.ds(0, 256), :] = part[:, 64:192]
            sq[xs, zh, h, pl.ds(256, 128), :] = jnp.concatenate([part[:128, :64], part[128:, :64]], axis=1)
            return carry
        lax.fori_loop(0, 4, head, 0)
        for d in (1, 3, 2):
            zc[d, r, h] = remote(sq.at[xs, zr4(d), h], hqkv.at[z, xs, h], zs.at[d - 1, r, h], zr.at[d - 1, r, h], to_z(d))
            zc[d, r, h].start()
        own.append(here(sq.at[xs, z, h], hqkv.at[z, xs, h], loc.at[6 + 2 * r + h]))
        own[-1].start()

    load_l.wait()
    for c in load_w:
        c.wait()
    project(0, 0)
    project(0, 1)
    right[0].wait_recv()
    right[2].start()
    project(3, 0)
    left[1].wait_recv()
    left[2].start()
    project(1, 1)

    given.wait_recv()
    load_wo.wait()
    own.append(here(gv, g, loc.at[14]))
    own[-1].start()
    def heads(n, carry):
        rows = pl.ds(pl.multiple_of(n * 256, 256), 256)
        part = lax.dot_general(gv[...], wov[rows, :], (((1,), (1,)), ((), ())), preferred_element_type=f32).astype(bf16)
        for i in range(4):
            cols = part[:, i * 64:(i + 1) * 64]
            for h in range(2):
                sd[n, i, h] = jnp.concatenate([cols[h * 256:h * 256 + 128], cols[h * 256 + 128:h * 256 + 256]], axis=1)
        return carry
    lax.fori_loop(0, 4, heads, 0)
    dz, dx = {}, {}
    for d in (1, 3, 2):
        dz[d] = remote(sd.at[zr4(d)], dv.at[z], ds_.at[d - 1], dr.at[d - 1], to_z(d))
        dz[d].start()
    own.append(here(sd.at[z, x], hd.at[z, x], loc.at[15]))
    own[-1].start()
    for d in (1, 3, 2):
        dx[0, d] = remote(sd.at[z, xr4(d)], hd.at[z, x], es.at[0, d - 1], er.at[0, d - 1], to_x(d))

    right[1].wait_recv()
    project(3, 1)
    left[0].wait_recv()
    project(1, 0)
    right[2].wait_recv()
    left[2].wait_recv()
    for d in (1, 3, 2):
        dx[0, d].start()
    project(2, 0)
    project(2, 1)
    for e in (1, 3, 2):
        dz[e].wait_recv()
        for d in (1, 3, 2):
            dx[e, d] = remote(dv.at[zr4(-e), xr4(d)], hd.at[zr4(-e), x], es.at[e, d - 1], er.at[e, d - 1], to_x(d))
            dx[e, d].start()
        own.append(here(dv.at[zr4(-e), x], hd.at[zr4(-e), x], loc.at[16 + e]))
        own[-1].start()
    store = here(lv, lg, loc.at[16])
    store.start()
    for c in [*zc.values(), *dx.values()]:
        c.wait_recv()
    for c in own:
        c.wait()
    store.wait()
    given.wait_send()
    for c in [*right.values(), *left.values(), *zc.values(), *dz.values(), *dx.values()]:
        c.wait_send()


def begin(lin, hand, w, wo, cid=2):
    anys = pl.BlockSpec(memory_space=pl.ANY)
    D = pltpu.SemaphoreType.DMA
    return pl.pallas_call(
        begin_kernel,
        out_shape=[
            jax.ShapeDtypeStruct((4, 4, 2, 384, 128), bf16),
            jax.ShapeDtypeStruct((4, 4, 2, 128, 128), bf16),
            jax.ShapeDtypeStruct((4, 2, 256, 1024), bf16),
            jax.ShapeDtypeStruct((512, 1024), bf16),
        ],
        in_specs=[anys] * 4,
        out_specs=[anys] * 4,
        scratch_shapes=[
            pltpu.VMEM((4, 2, 256, 1024), bf16), pltpu.VMEM((512, 1024), bf16),
            pltpu.VMEM((4, 1024, 256), bf16), pltpu.VMEM((1024, 1024), bf16),
            pltpu.VMEM((4, 4, 2, 384, 128), bf16), pltpu.VMEM((4, 4, 2, 128, 128), bf16), pltpu.VMEM((4, 4, 2, 128, 128), bf16),
            D((20,)), D, D, D((2, 3)), D((2, 3)), D((3, 4, 2)), D((3, 4, 2)), D((3,)), D((3,)), D((4, 3)), D((4, 3)),
        ],
        compiler_params=pltpu.CompilerParams(collective_id=cid, has_side_effects=True, vmem_limit_bytes=62 * 2**20),
        cost_estimate=pl.CostEstimate(flops=4 * 10**9, bytes_accessed=2 * 10**7, transcendentals=0),
    )(lin.reshape(2, 256, 1024), hand, w, wo)


def settle_kernel(a, b, c, oa, ob, oc, ha, hb, hc, ins, outs):
    loads, stores = [], []
    for src, held, dst, parts in ((a, ha, oa, 4), (b, hb, ob, 3), (c, hc, oc, 1)):
        rows = src.shape[0] // parts
        for p in range(parts):
            cut, n = pl.ds(p * rows, rows), len(loads)
            loads.append(pltpu.make_async_copy(src.at[cut], held.at[cut], ins.at[n]))
            stores.append(pltpu.make_async_copy(held.at[cut], dst.at[cut], outs.at[n]))
            loads[-1].start()
    for load, store in zip(loads, stores):
        load.wait()
        store.start()
    for store in stores:
        store.wait()


def settle(*arrays):
    anys = pl.BlockSpec(memory_space=pl.ANY)
    return pl.pallas_call(
        settle_kernel,
        out_shape=[jax.ShapeDtypeStruct(a.shape, a.dtype) for a in arrays],
        in_specs=[anys] * 3,
        out_specs=[anys] * 3,
        scratch_shapes=[pltpu.VMEM(a.shape, a.dtype) for a in arrays]
        + [pltpu.SemaphoreType.DMA((8,)), pltpu.SemaphoreType.DMA((8,))],
        compiler_params=pltpu.CompilerParams(has_side_effects=True, vmem_limit_bytes=62 * 2**20),
    )(*arrays)


def local(layer_input, handoff, qkv_weight, out_weight, neighbours, counts):
    weight_in = qkv_weight[0]
    hqkv, hd, lg, grad_out = begin(layer_input[0], handoff[0], weight_in, out_weight[0])
    along_z = [[4 * b + a for b in range(4)] for a in range(4)]
    gz = lax.all_gather(grad_out, "seq", axis_index_groups=along_z)
    gqkv, att = attention(hqkv.reshape(32, 384, 128), hd.reshape(32, 128, 128), neighbours[0, 0], counts[0, 0])
    grad_input, grad_qkv_weight, grad_out_weight = finish(gqkv, att, lg.reshape(4, 512, 1024), gz, weight_in)
    grad_input, grad_qkv_weight, grad_out_weight = settle(grad_input, grad_qkv_weight, grad_out_weight)
    return (grad_input[None], grad_qkv_weight[None], grad_out_weight[None])


def solution(mesh):
    placed = (
        P("pipe", "seq", None),
        P("pipe", "seq", None),
        P("pipe", None, None),
        P("pipe", None, None),
        P("pipe", "seq", None, None),
        P("pipe", "seq", None),
    )
    return jax.shard_map(
        local,
        mesh=mesh,
        in_specs=placed,
        out_specs=(P("pipe", "seq", None), P("pipe", "seq", None), P("pipe", "seq", None)),
        check_vma=False,
    )
```

```python
import functools
import jax, jax.numpy as jnp
from jax import lax
from jax.experimental import pallas as pl
from jax.experimental.pallas import tpu as pltpu
from jax.sharding import PartitionSpec as P
HEAD_DIM=64; BLOCK=128; MAXNB=8; QB=64; GROUP=8
f32=jnp.float32; bf16=jnp.bfloat16

def attn_body(order, nb, cnt, hq, qd, gqa, acc, kvt, group, i, slots):
    scale = HEAD_DIM ** -0.5
    half_row = lax.broadcasted_iota(jnp.int32, (BLOCK, BLOCK), 0) < HEAD_DIM
    half_lane = lax.broadcasted_iota(jnp.int32, (BLOCK, BLOCK), 1) < HEAD_DIM
    zero = jnp.zeros((BLOCK, BLOCK), bf16)
    dn = (((1,), (0,)), ((), ()))
    mm = lambda a, b: lax.dot_general(a, b, dn, preferred_element_type=f32)
    chains = []
    for g in range(group):
        b = order[i * group + g]
        chains.append((b, cnt[b], [nb[j, b] for j in range(slots)]))
    st = []
    for b, c, ns in chains:
        own = qd[b]
        own_t = own.T
        q_t = jnp.where(half_row, own_t * jnp.asarray(scale, bf16), zero)
        d_t = jnp.where(half_row, zero, own_t)
        right = jnp.concatenate([q_t, d_t], axis=1)
        scores, dps = [], []
        every = mm(jnp.concatenate([load_keys(hq, ns[j]) for j in range(slots)], axis=0), right)
        for j in range(slots):
            both = every[j * BLOCK:(j + 1) * BLOCK]
            s = both[:, :BLOCK]
            if j > 0:
                s = jnp.where(j < c, s, -jnp.inf)
            scores.append(s); dps.append(both[:, BLOCK:])
        st.append((own, own_t, scores, dps))
    st2 = []
    for (b, c, ns), (own, own_t, scores, dps) in zip(chains, st):
        top = scores[0]
        for s in scores[1:]:
            top = jnp.maximum(top, s)
        top = jnp.max(top, axis=0, keepdims=True)
        es = [jnp.exp(s - top) for s in scores]
        tot = es[0]
        for e in es[1:]:
            tot = tot + e
        inv = 1.0 / jnp.sum(tot, axis=0, keepdims=True)
        ps = [e * inv for e in es]
        st2.append((own, own_t, dps, ps))
    for (b, c, ns), (own, own_t, dps, ps) in zip(chains, st2):
        low = [p.astype(bf16) for p in ps]
        att_t = mm(jnp.concatenate([kvt[ns[j], HEAD_DIM:, :] for j in range(slots)], axis=1), jnp.concatenate(low, axis=0))
        att_t = att_t.astype(bf16)
        dot = jnp.sum(own_t[HEAD_DIM:, :].astype(f32) * att_t.astype(f32), axis=0, keepdims=True)
        ds = [(p * (dp - dot)).astype(bf16) for p, dp in zip(ps, dps)]
        left = jnp.concatenate([jnp.where(half_lane, own * jnp.asarray(scale, bf16), zero), jnp.where(half_lane, zero, own)], axis=0)
        low_all, ds_all = jnp.concatenate(low, axis=0), jnp.concatenate(ds, axis=0)
        terms = mm(jnp.concatenate([ds_all, low_all], axis=1), left)
        gq_t = mm(jnp.concatenate([kvt[ns[j], :HEAD_DIM, :] for j in range(slots)], axis=1), ds_all)
        for j in range(slots):
            acc[ns[j]] += terms[j * BLOCK:(j + 1) * BLOCK]
        gq_t = (gq_t * scale).astype(bf16)
        gqa[b] = jnp.concatenate([gq_t, att_t], axis=0).T

def load_keys(hq, n):
    half, rows = key_rows(n)
    return hq[half, rows, :]


def key_rows(n):
    return n // 2, pl.ds(pl.multiple_of((n % 2) * BLOCK, BLOCK), BLOCK)


def attn_kernel(nb, cnt, hq, hd, hg, ha, acc, kvt, qd, gqa, order, place, *, group):
    for c in range(MAXNB + 2):
        place[c] = 0

    def prep_keys(u, carry):
        for e in range(2):
            c = cnt[2 * u + e] + 1
            place[c] = place[c] + 1
            kvt[2 * u + e] = hq[u, pl.ds(e * BLOCK, BLOCK), :].T
        return carry
    lax.fori_loop(0, QB // 2, prep_keys, 0, unroll=2)
    for c in range(1, MAXNB + 1):
        place[c] = place[c] + place[c - 1]

    def prep_rows(u, carry):
        for e in range(2):
            c = cnt[2 * u + e]
            at = place[c]
            order[at] = 2 * u + e
            place[c] = at + 1
            acc[2 * u + e] = jnp.zeros((BLOCK, BLOCK), f32)
        q = hq[u, pl.ds(256, BLOCK), :]
        d = hd[u]
        qd[2 * u] = jnp.concatenate([q[:, :HEAD_DIM], d[:, :HEAD_DIM]], axis=1)
        qd[2 * u + 1] = jnp.concatenate([q[:, HEAD_DIM:], d[:, HEAD_DIM:]], axis=1)
        return carry
    lax.fori_loop(0, QB // 2, prep_rows, 0, unroll=2)

    def step(i, carry):
        most = cnt[order[i * group + group - 1]]
        for slots in range(1, MAXNB + 1):
            @pl.when(most == slots)
            def run():
                attn_body(order, nb, cnt, hq, qd, gqa, acc, kvt, group, i, slots)
        return carry
    lax.fori_loop(0, QB // group, step, 0)

    def fin(u, carry):
        for e in range(2):
            hg[u, pl.ds(e * BLOCK, BLOCK), :] = acc[2 * u + e].astype(bf16)
        a, b = gqa[2 * u], gqa[2 * u + 1]
        hg[u, pl.ds(256, BLOCK), :] = jnp.concatenate([a[:, :HEAD_DIM], b[:, :HEAD_DIM]], axis=1)
        ha[u] = jnp.concatenate([a[:, HEAD_DIM:], b[:, HEAD_DIM:]], axis=1)
        return carry
    lax.fori_loop(0, QB // 2, fin, 0, unroll=2)


def attention(hq, hd, nb, cnt, group=GROUP):
    sm = pl.BlockSpec(memory_space=pltpu.SMEM)
    vm = pl.BlockSpec(memory_space=pltpu.VMEM)
    return pl.pallas_call(
        functools.partial(attn_kernel, group=group),
        out_shape=[jax.ShapeDtypeStruct((QB // 2, 384, 128), bf16), jax.ShapeDtypeStruct((QB // 2, 128, 128), bf16)],
        in_specs=[sm, sm, vm, vm],
        out_specs=[vm, vm],
        scratch_shapes=[
            pltpu.VMEM((QB, BLOCK, 128), f32),
            pltpu.VMEM((QB, 128, 128), bf16),
            pltpu.VMEM((QB, 128, 128), bf16),
            pltpu.VMEM((QB, 128, 128), bf16),
            pltpu.SMEM((QB,), jnp.int32),
            pltpu.SMEM((MAXNB + 2,), jnp.int32),
        ],
        compiler_params=pltpu.CompilerParams(vmem_limit_bytes=56 * 2**20),
        cost_estimate=pl.CostEstimate(flops=2 * 512 * 128 * 128 * 64 * 6, bytes_accessed=2**23, transcendentals=512 * 128 * 128),
    )(nb.T, cnt, hq, hd)


MESH = pl.DeviceIdType.MESH

def cat_tokens(dst, row, col, pair):
    turned = pair.T
    dst[pl.ds(row, HEAD_DIM), pl.ds(col, 128)] = turned[:HEAD_DIM]
    dst[pl.ds(row, HEAD_DIM), pl.ds(col + 128, 128)] = turned[HEAD_DIM:]

def finish_kernel(gqkv, att, lg, g0, g1, g3, g2, w, gin, gqw, gow,
                  rv, fv, at, lv, gv, wv, xt, mt, acc, pqs, pqr, pos, por, mine,
                  loc, zs, zr, xs, xr, as_, ar, qs, qr, os_, or_):
    pipe = lax.axis_index("pipe")
    me = lax.axis_index("seq")
    z, x = me // 4, me % 4
    zr4 = lambda d: (z + d) % 4
    xr4 = lambda d: (x + d) % 4
    def to_z(d): return (pipe, zr4(d) * 4 + x)
    def to_x(d): return (pipe, z * 4 + xr4(d))
    barrier = pltpu.get_barrier_semaphore()
    for d in (1, 2, 3):
        pl.semaphore_signal(barrier, inc=1, device_id=to_z(d), device_id_type=MESH)
        pl.semaphore_signal(barrier, inc=1, device_id=to_x(d), device_id_type=MESH)
    loads = [pltpu.make_async_copy(gqkv.at[z], rv.at[z], loc.at[0]),
             pltpu.make_async_copy(lg, lv, loc.at[1]),
             pltpu.make_async_copy(att.at[:, x], at.at[x], loc.at[2]),
             pltpu.make_async_copy(g0, gv.at[z], loc.at[3]),
             pltpu.make_async_copy(g1, gv.at[zr4(-1)], loc.at[9]),
             pltpu.make_async_copy(g3, gv.at[zr4(-3)], loc.at[10]),
             pltpu.make_async_copy(g2, gv.at[zr4(-2)], loc.at[11]),
             pltpu.make_async_copy(w, wv, loc.at[4])]
    for c in loads:
        c.start()
    pl.semaphore_wait(barrier, 6)

    def remote(src, dst, ss, rs, dev):
        return pltpu.make_async_remote_copy(src_ref=src, dst_ref=dst, send_sem=ss, recv_sem=rs, device_id=dev, device_id_type=MESH)

    ZORDER = [(d, j) for j in (1, 3, 2, 0) for d in (1, 3)] + [(2, j) for j in (1, 3, 2, 0)]
    zc = {}
    for d, j in ZORDER:
        zc[d, j] = remote(gqkv.at[zr4(d), xr4(j)], rv.at[z, xr4(j)], zs.at[d - 1, j], zr.at[d - 1, j], to_z(d))
    xc, ac = {}, {}
    for d in (1, 3, 2):
        xc[0, d] = remote(gqkv.at[z, xr4(d)], fv.at[z, x], xs.at[0, d - 1], xr.at[0, d - 1], to_x(d))
        ac[d] = remote(att.at[:, xr4(d)], at.at[x], as_.at[d - 1], ar.at[d - 1], to_x(d))
        for e in (1, 3, 2):
            xc[e, d] = remote(rv.at[zr4(-e), xr4(d)], fv.at[zr4(-e), x], xs.at[e, d - 1], xr.at[e, d - 1], to_x(d))
    for key in ZORDER:
        zc[key].start()
    for d in (1, 3, 2):
        xc[0, d].start()
    for d in (1, 3, 2):
        ac[d].start()

    def weight_part(zh, out_at):
        def turn(u, carry):
            xi, half = u // 2, u % 2
            col = pl.multiple_of(u * 256, 256)
            xt[pl.ds(64, 128), pl.ds(col, 256)] = rv[zh, xi, half, pl.ds(0, 256), :].T
            cat_tokens(xt, 0, col, rv[zh, xi, half, pl.ds(256, 128), :])
            return carry
        lax.fori_loop(0, 8, turn, 0)
        def tile(n, carry):
            cols = pl.ds(pl.multiple_of(n * 256, 256), 256)
            total = jnp.zeros((192, 256), f32)
            for k in range(4):
                total += jnp.dot(xt[pl.ds(0, 192), pl.ds(k * 512, 512)], lv[k, :, cols], preferred_element_type=f32)
            out_at(cols, total)
            return carry
        lax.fori_loop(0, 4, tile, 0)

    def own_out(cols, total):
        gqw[:, cols] = total

    def sent_out(slot):
        def put(cols, total):
            pqs[slot, :, cols] = total.astype(bf16)
        return put

    def input_part(zh, first=False):
        def build(u, carry):
            half, e = u // 2, u % 2
            rows = pl.ds(pl.multiple_of(u * 128, 128), 128)
            krows = pl.ds(pl.multiple_of(e * 128, 128), 128)
            for p in range(2):
                a, b = 2 * p, 2 * p + 1
                qa = fv[zh, a, half, pl.ds(256, 128), :]
                qb = fv[zh, b, half, pl.ds(256, 128), :]
                low = e == 0
                qa = jnp.where(low, qa[:, :64], qa[:, 64:])
                qb = jnp.where(low, qb[:, :64], qb[:, 64:])
                mt[rows, pl.ds(p * 384, 384)] = jnp.concatenate(
                    [qa, fv[zh, a, half, krows, :], qb, fv[zh, b, half, krows, :]], axis=1)
            return carry
        lax.fori_loop(0, 4, build, 0)
        def tile(n, carry):
            cols = pl.ds(pl.multiple_of(n * 256, 256), 256)
            part = lax.dot_general(mt[...], wv[cols, pl.ds(pl.multiple_of(zh * 768, 128), 768)],
                                   (((1,), (1,)), ((), ())), preferred_element_type=f32)
            if first:
                acc[:, cols] = gv[z, :, cols].astype(f32) + part
            else:
                acc[:, cols] += part
            return carry
        lax.fori_loop(0, 4, tile, 0)

    loads[0].wait()
    loads[1].wait()
    own = pltpu.make_async_copy(rv.at[z, x], fv.at[z, x], loc.at[5])
    own.start()
    weight_part(z, own_out)

    for c in loads[2:]:
        c.wait()

    def arrive(d, j):
        zc[d, j].wait_recv()
        if j:
            xc[d, j].start()

    for d, j in ZORDER[:4]:
        arrive(d, j)
    for d in (1, 3, 2):
        ac[d].wait_recv()
    def turn_att(u, carry):
        zi, half = u // 2, u % 2
        col = pl.multiple_of(u * 256, 256)
        for xh in range(4):
            cat_tokens(xt, xh * 64, col, at[xh, zi, half])
        return carry
    lax.fori_loop(0, 8, turn_att, 0)
    def att_tile(n, carry):
        cols = pl.ds(pl.multiple_of(n * 256, 256), 256)
        total = jnp.zeros((256, 256), f32)
        for k in range(4):
            total += jnp.dot(xt[:, pl.ds(k * 512, 512)], gv[k, :, cols], preferred_element_type=f32)
        mine[:, cols] = total
        for xh in range(4):
            pos[xh, :, cols] = total[xh * 64:(xh + 1) * 64].astype(bf16)
        return carry
    lax.fori_loop(0, 4, att_tile, 0)
    gow[...] = mine[pl.ds(pl.multiple_of(x * 64, 64), 64), :]
    oc = {}
    for d in (1, 3, 2):
        oc[d] = remote(pos.at[xr4(d)], por.at[d - 1], os_.at[d - 1], or_.at[d - 1], to_x(d))
        oc[d].start()
    for d, j in ZORDER[4:8]:
        arrive(d, j)
    locals_ = {}
    def take_own(e):
        locals_[e] = pltpu.make_async_copy(rv.at[zr4(-e), x], fv.at[zr4(-e), x], loc.at[5 + e])
        locals_[e].start()
    qc = {}
    def send_part(e):
        weight_part(zr4(-e), sent_out(e - 1))
        qc[e] = remote(pqs.at[e - 1], pqr.at[e - 1], qs.at[e - 1], qr.at[e - 1], to_z(-e))
        qc[e].start()
    for e in (1, 3):
        take_own(e)
        send_part(e)
    for d in (1, 3, 2):
        xc[0, d].wait_recv()
    own.wait()
    input_part(z, first=True)
    for d, j in ZORDER[8:]:
        arrive(d, j)
    take_own(2)
    send_part(2)
    for e in (1, 3, 2):
        for d in (1, 3, 2):
            xc[e, d].wait_recv()
        locals_[e].wait()
        input_part(zr4(-e))
    gin[...] = acc[...].astype(bf16)
    for d in (1, 3, 2):
        oc[d].wait_recv()
        gow[...] += por[d - 1].astype(f32)
    for d in (1, 3, 2):
        qc[d].wait_recv()
        gqw[...] += pqr[d - 1].astype(f32)
    for c in [*zc.values(), *xc.values(), *ac.values(), *oc.values(), *qc.values()]:
        c.wait_send()

def finish(gqkv, att, lg, g0, g1, g3, g2, w, cid=1):
    anys = pl.BlockSpec(memory_space=pl.ANY)
    vm = pl.BlockSpec(memory_space=pltpu.VMEM)
    D = pltpu.SemaphoreType.DMA
    return pl.pallas_call(finish_kernel,
        out_shape=[jax.ShapeDtypeStruct((512, 1024), bf16), jax.ShapeDtypeStruct((192, 1024), f32), jax.ShapeDtypeStruct((64, 1024), f32)],
        in_specs=[anys] * 8, out_specs=[vm] * 3,
        scratch_shapes=[
            pltpu.VMEM((4, 4, 2, 384, 128), bf16), pltpu.VMEM((4, 4, 2, 384, 128), bf16), pltpu.VMEM((4, 4, 2, 128, 128), bf16),
            pltpu.VMEM((4, 512, 1024), bf16), pltpu.VMEM((4, 512, 1024), bf16), pltpu.VMEM((1024, 3072), bf16),
            pltpu.VMEM((256, 2048), bf16), pltpu.VMEM((512, 768), bf16), pltpu.VMEM((512, 1024), f32),
            pltpu.VMEM((3, 192, 1024), bf16), pltpu.VMEM((3, 192, 1024), bf16),
            pltpu.VMEM((4, 64, 1024), bf16), pltpu.VMEM((3, 64, 1024), bf16), pltpu.VMEM((256, 1024), f32),
            D((12,)), D((3, 4)), D((3, 4)), D((4, 3)), D((4, 3)), D((3,)), D((3,)), D((3,)), D((3,)), D((3,)), D((3,))],
        compiler_params=pltpu.CompilerParams(collective_id=cid, has_side_effects=True, vmem_limit_bytes=56 * 2**20),
        cost_estimate=pl.CostEstimate(flops=8 * 10**9, bytes_accessed=2 * 10**7, transcendentals=0),
    )(gqkv.reshape(4, 4, 2, 384, 128), att.reshape(4, 4, 2, 128, 128), lg, g0, g1, g3, g2, w)


def begin_kernel(lin, hand, w, wo, hqkv, hd, lg, g,
                 lv, gv, w4, wov, sq, sd, dv,
                 loc, hs, hr, gs, gr, zs, zr, ds_, dr, es, er):
    pipe = lax.axis_index("pipe")
    me = lax.axis_index("seq")
    z, x = me // 4, me % 4
    zr4 = lambda d: (z + d) % 4
    xr4 = lambda d: (x + d) % 4
    def to_z(d): return (pipe, zr4(d) * 4 + x)
    def to_x(d): return (pipe, z * 4 + xr4(d))
    barrier = pltpu.get_barrier_semaphore()
    for d in (1, 2, 3):
        pl.semaphore_signal(barrier, inc=1, device_id=to_z(d), device_id_type=MESH)
        pl.semaphore_signal(barrier, inc=1, device_id=to_x(d), device_id_type=MESH)
    pl.semaphore_signal(barrier, inc=1, device_id=((pipe + 1) % 8, me), device_id_type=MESH)

    def here(src, dst, sem):
        return pltpu.make_async_copy(src, dst, sem)

    def remote(src, dst, ss, rs, dev):
        return pltpu.make_async_remote_copy(src_ref=src, dst_ref=dst, send_sem=ss, recv_sem=rs, device_id=dev, device_id_type=MESH)

    load_l = here(lin, lv.at[x], loc.at[0])
    load_l.start()
    load_w = []
    for zh in range(4):
        first = pl.multiple_of(((12 * zh + 3 * x) // 2) * 128, 128)
        load_w.append(here(w.at[:, pl.ds(first, 256)], w4.at[zh], loc.at[1 + zh]))
        load_w[-1].start()
    load_wo = here(wo, wov, loc.at[5])
    load_wo.start()
    pl.semaphore_wait(barrier, 7)

    given = remote(hand, gv, hs, hr, ((pipe + 7) % 8, me))
    right = {h: remote(lin.at[h], lv.at[x, h], gs.at[0, h], gr.at[0, h], to_x(1)) for h in (0, 1)}
    left = {h: remote(lin.at[h], lv.at[x, h], gs.at[1, h], gr.at[1, h], to_x(3)) for h in (0, 1)}
    right[2] = remote(lv.at[xr4(3), 0], lv.at[xr4(3), 0], gs.at[0, 2], gr.at[0, 2], to_x(1))
    left[2] = remote(lv.at[xr4(1), 1], lv.at[xr4(1), 1], gs.at[1, 2], gr.at[1, 2], to_x(3))
    right[0].start()
    left[1].start()
    given.start()
    right[1].start()
    left[0].start()

    zc, own, kept = {}, [], []

    def project(r, h):
        xs = xr4(r)
        def head(zh, carry):
            part = jnp.dot(lv[xs, h], w4[zh], preferred_element_type=f32).astype(bf16)
            part = jnp.where(x % 2 == 1, jnp.concatenate([part[:, 64:], part[:, :64]], axis=1), part)
            sq[xs, zh, h, pl.ds(0, 256), :] = part[:, 64:192]
            sq[xs, zh, h, pl.ds(256, 128), :] = jnp.concatenate([part[:128, :64], part[128:, :64]], axis=1)
            return carry
        lax.fori_loop(0, 4, head, 0)
        for d in (1, 3, 2):
            zc[d, r, h] = remote(sq.at[xs, zr4(d), h], hqkv.at[z, xs, h], zs.at[d - 1, r, h], zr.at[d - 1, r, h], to_z(d))
            zc[d, r, h].start()
        own.append(here(sq.at[xs, z, h], hqkv.at[z, xs, h], loc.at[6 + 2 * r + h]))
        own[-1].start()

    load_l.wait()
    for c in load_w:
        c.wait()
    project(0, 0)
    project(0, 1)
    right[0].wait_recv()
    right[2].start()
    project(3, 0)
    left[1].wait_recv()
    left[2].start()
    project(1, 1)

    given.wait_recv()
    load_wo.wait()
    own.append(here(gv, g, loc.at[14]))
    own[-1].start()
    def heads(n, carry):
        rows = pl.ds(pl.multiple_of(n * 256, 256), 256)
        part = lax.dot_general(gv[...], wov[rows, :], (((1,), (1,)), ((), ())), preferred_element_type=f32).astype(bf16)
        for i in range(4):
            cols = part[:, i * 64:(i + 1) * 64]
            for h in range(2):
                sd[n, i, h] = jnp.concatenate([cols[h * 256:h * 256 + 128], cols[h * 256 + 128:h * 256 + 256]], axis=1)
        return carry
    lax.fori_loop(0, 4, heads, 0)
    dz, dx = {}, {}
    for d in (1, 3, 2):
        dz[d] = remote(sd.at[zr4(d)], dv.at[z], ds_.at[d - 1], dr.at[d - 1], to_z(d))
        dz[d].start()
    own.append(here(sd.at[z, x], hd.at[z, x], loc.at[15]))
    own[-1].start()
    for d in (1, 3, 2):
        dx[0, d] = remote(sd.at[z, xr4(d)], hd.at[z, x], es.at[0, d - 1], er.at[0, d - 1], to_x(d))

    right[1].wait_recv()
    project(3, 1)
    left[0].wait_recv()
    project(1, 0)
    right[2].wait_recv()
    left[2].wait_recv()
    for d in (1, 3, 2):
        dx[0, d].start()
    project(2, 0)
    project(2, 1)
    for e in (1, 3, 2):
        dz[e].wait_recv()
        for d in (1, 3, 2):
            dx[e, d] = remote(dv.at[zr4(-e), xr4(d)], hd.at[zr4(-e), x], es.at[e, d - 1], er.at[e, d - 1], to_x(d))
            dx[e, d].start()
        own.append(here(dv.at[zr4(-e), x], hd.at[zr4(-e), x], loc.at[16 + e]))
        own[-1].start()
    store = here(lv, lg, loc.at[16])
    store.start()
    for c in [*zc.values(), *dx.values()]:
        c.wait_recv()
    for c in own:
        c.wait()
    store.wait()
    given.wait_send()
    for c in [*right.values(), *left.values(), *zc.values(), *dz.values(), *dx.values()]:
        c.wait_send()


def begin(lin, hand, w, wo, cid=2):
    anys = pl.BlockSpec(memory_space=pl.ANY)
    D = pltpu.SemaphoreType.DMA
    return pl.pallas_call(
        begin_kernel,
        out_shape=[
            jax.ShapeDtypeStruct((4, 4, 2, 384, 128), bf16),
            jax.ShapeDtypeStruct((4, 4, 2, 128, 128), bf16),
            jax.ShapeDtypeStruct((4, 2, 256, 1024), bf16),
            jax.ShapeDtypeStruct((512, 1024), bf16),
        ],
        in_specs=[anys] * 4,
        out_specs=[anys] * 4,
        scratch_shapes=[
            pltpu.VMEM((4, 2, 256, 1024), bf16), pltpu.VMEM((512, 1024), bf16),
            pltpu.VMEM((4, 1024, 256), bf16), pltpu.VMEM((1024, 1024), bf16),
            pltpu.VMEM((4, 4, 2, 384, 128), bf16), pltpu.VMEM((4, 4, 2, 128, 128), bf16), pltpu.VMEM((4, 4, 2, 128, 128), bf16),
            D((20,)), D, D, D((2, 3)), D((2, 3)), D((3, 4, 2)), D((3, 4, 2)), D((3,)), D((3,)), D((4, 3)), D((4, 3)),
        ],
        compiler_params=pltpu.CompilerParams(collective_id=cid, has_side_effects=True, vmem_limit_bytes=62 * 2**20),
        cost_estimate=pl.CostEstimate(flops=4 * 10**9, bytes_accessed=2 * 10**7, transcendentals=0),
    )(lin.reshape(2, 256, 1024), hand, w, wo)


def settle_kernel(a, b, c, oa, ob, oc, ha, hb, hc, ins, outs):
    loads, stores = [], []
    for src, held, dst, parts in ((a, ha, oa, 4), (b, hb, ob, 3), (c, hc, oc, 1)):
        rows = src.shape[0] // parts
        for p in range(parts):
            cut, n = pl.ds(p * rows, rows), len(loads)
            loads.append(pltpu.make_async_copy(src.at[cut], held.at[cut], ins.at[n]))
            stores.append(pltpu.make_async_copy(held.at[cut], dst.at[cut], outs.at[n]))
            loads[-1].start()
    for load, store in zip(loads, stores):
        load.wait()
        store.start()
    for store in stores:
        store.wait()


def settle(*arrays):
    anys = pl.BlockSpec(memory_space=pl.ANY)
    return pl.pallas_call(
        settle_kernel,
        out_shape=[jax.ShapeDtypeStruct(a.shape, a.dtype) for a in arrays],
        in_specs=[anys] * 3,
        out_specs=[anys] * 3,
        scratch_shapes=[pltpu.VMEM(a.shape, a.dtype) for a in arrays]
        + [pltpu.SemaphoreType.DMA((8,)), pltpu.SemaphoreType.DMA((8,))],
        compiler_params=pltpu.CompilerParams(has_side_effects=True, vmem_limit_bytes=62 * 2**20),
    )(*arrays)


def local(layer_input, handoff, qkv_weight, out_weight, neighbours, counts):
    weight_in = qkv_weight[0]
    hqkv, hd, lg, grad_out = begin(layer_input[0], handoff[0], weight_in, out_weight[0])
    around = [lax.ppermute(grad_out, "seq", [(i, (i + 4 * d) % 16) for i in range(16)]) for d in (1, 3, 2)]
    gqkv, att = attention(hqkv.reshape(32, 384, 128), hd.reshape(32, 128, 128), neighbours[0, 0], counts[0, 0])
    grad_input, grad_qkv_weight, grad_out_weight = finish(gqkv, att, lg.reshape(4, 512, 1024), grad_out, *around, weight_in)
    grad_input, grad_qkv_weight, grad_out_weight = settle(grad_input, grad_qkv_weight, grad_out_weight)
    return (grad_input[None], grad_qkv_weight[None], grad_out_weight[None])


def solution(mesh):
    placed = (
        P("pipe", "seq", None),
        P("pipe", "seq", None),
        P("pipe", None, None),
        P("pipe", None, None),
        P("pipe", "seq", None, None),
        P("pipe", "seq", None),
    )
    return jax.shard_map(
        local,
        mesh=mesh,
        in_specs=placed,
        out_specs=(P("pipe", "seq", None), P("pipe", "seq", None), P("pipe", "seq", None)),
        check_vma=False,
    )
```

```python
import functools
import jax, jax.numpy as jnp
from jax import lax
from jax.experimental import pallas as pl
from jax.experimental.pallas import tpu as pltpu
from jax.sharding import PartitionSpec as P
HEAD_DIM=64; BLOCK=128; MAXNB=8; QB=64; GROUP=8
f32=jnp.float32; bf16=jnp.bfloat16

def attn_body(order, nb, cnt, hq, qd, gqa, acc, kvt, group, i, slots):
    scale = HEAD_DIM ** -0.5
    half_row = lax.broadcasted_iota(jnp.int32, (BLOCK, BLOCK), 0) < HEAD_DIM
    half_lane = lax.broadcasted_iota(jnp.int32, (BLOCK, BLOCK), 1) < HEAD_DIM
    zero = jnp.zeros((BLOCK, BLOCK), bf16)
    dn = (((1,), (0,)), ((), ()))
    mm = lambda a, b: lax.dot_general(a, b, dn, preferred_element_type=f32)
    chains = []
    for g in range(group):
        b = order[i * group + g]
        chains.append((b, cnt[b], [nb[j, b] for j in range(slots)]))
    def first(g):
        b, c, ns = chains[g]
        own = qd[b]
        own_t = own.T
        q_t = jnp.where(half_row, own_t * jnp.asarray(scale, bf16), zero)
        d_t = jnp.where(half_row, zero, own_t)
        right = jnp.concatenate([q_t, d_t], axis=1)
        scores, dps = [], []
        every = mm(jnp.concatenate([load_keys(hq, ns[j]) for j in range(slots)], axis=0), right)
        for j in range(slots):
            both = every[j * BLOCK:(j + 1) * BLOCK]
            s = both[:, :BLOCK]
            if j > 0:
                s = jnp.where(j < c, s, -jnp.inf)
            scores.append(s)
            dps.append(both[:, BLOCK:])
        return own, own_t, scores, dps

    def second(g, own, own_t, scores, dps):
        top = scores[0]
        for s in scores[1:]:
            top = jnp.maximum(top, s)
        top = jnp.max(top, axis=0, keepdims=True)
        es = [jnp.exp(s - top) for s in scores]
        tot = es[0]
        for e in es[1:]:
            tot = tot + e
        inv = 1.0 / jnp.sum(tot, axis=0, keepdims=True)
        ps = [e * inv for e in es]
        b, c, ns = chains[g]
        low_all = jnp.concatenate([p.astype(bf16) for p in ps], axis=0)
        att_t = mm(jnp.concatenate([kvt[ns[j], HEAD_DIM:, :] for j in range(slots)], axis=1), low_all)
        return own, own_t, dps, ps, low_all, att_t.astype(bf16)

    def third(g, own, own_t, dps, ps, low_all, att_t):
        b, c, ns = chains[g]
        dot = jnp.sum(own_t[HEAD_DIM:, :].astype(f32) * att_t.astype(f32), axis=0, keepdims=True)
        ds_all = jnp.concatenate([(p * (dp - dot)).astype(bf16) for p, dp in zip(ps, dps)], axis=0)
        left = jnp.concatenate([jnp.where(half_lane, own * jnp.asarray(scale, bf16), zero), jnp.where(half_lane, zero, own)], axis=0)
        terms = mm(jnp.concatenate([ds_all, low_all], axis=1), left)
        gq_t = mm(jnp.concatenate([kvt[ns[j], :HEAD_DIM, :] for j in range(slots)], axis=1), ds_all)
        for j in range(slots):
            acc[ns[j]] += terms[j * BLOCK:(j + 1) * BLOCK]
        gq_t = (gq_t * scale).astype(bf16)
        gqa[b] = jnp.concatenate([gq_t, att_t], axis=0).T

    ones, twos = {}, {}
    for t in range(group + 2):
        if t < group:
            ones[t] = first(t)
        if 0 <= t - 1 < group:
            twos[t - 1] = second(t - 1, *ones.pop(t - 1))
        if 0 <= t - 2 < group:
            third(t - 2, *twos.pop(t - 2))


def load_keys(hq, n):
    half, rows = key_rows(n)
    return hq[half, rows, :]


def key_rows(n):
    return n // 2, pl.ds(pl.multiple_of((n % 2) * BLOCK, BLOCK), BLOCK)


def attn_kernel(nb, cnt, hq, hd, hg, ha, acc, kvt, qd, gqa, order, place, *, group):
    for c in range(MAXNB + 2):
        place[c] = 0

    def prep_keys(u, carry):
        for e in range(2):
            c = cnt[2 * u + e] + 1
            place[c] = place[c] + 1
            kvt[2 * u + e] = hq[u, pl.ds(e * BLOCK, BLOCK), :].T
        return carry
    lax.fori_loop(0, QB // 2, prep_keys, 0, unroll=2)
    for c in range(1, MAXNB + 1):
        place[c] = place[c] + place[c - 1]

    def prep_rows(u, carry):
        for e in range(2):
            c = cnt[2 * u + e]
            at = place[c]
            order[at] = 2 * u + e
            place[c] = at + 1
            acc[2 * u + e] = jnp.zeros((BLOCK, BLOCK), f32)
        q = hq[u, pl.ds(256, BLOCK), :]
        d = hd[u]
        qd[2 * u] = jnp.concatenate([q[:, :HEAD_DIM], d[:, :HEAD_DIM]], axis=1)
        qd[2 * u + 1] = jnp.concatenate([q[:, HEAD_DIM:], d[:, HEAD_DIM:]], axis=1)
        return carry
    lax.fori_loop(0, QB // 2, prep_rows, 0, unroll=2)

    def step(i, carry):
        most = cnt[order[i * group + group - 1]]
        for slots in range(1, MAXNB + 1):
            @pl.when(most == slots)
            def run():
                attn_body(order, nb, cnt, hq, qd, gqa, acc, kvt, group, i, slots)
        return carry
    lax.fori_loop(0, QB // group, step, 0)

    def fin(u, carry):
        for e in range(2):
            hg[u, pl.ds(e * BLOCK, BLOCK), :] = acc[2 * u + e].astype(bf16)
        a, b = gqa[2 * u], gqa[2 * u + 1]
        hg[u, pl.ds(256, BLOCK), :] = jnp.concatenate([a[:, :HEAD_DIM], b[:, :HEAD_DIM]], axis=1)
        ha[u] = jnp.concatenate([a[:, HEAD_DIM:], b[:, HEAD_DIM:]], axis=1)
        return carry
    lax.fori_loop(0, QB // 2, fin, 0, unroll=2)


def attention(hq, hd, nb, cnt, group=GROUP):
    sm = pl.BlockSpec(memory_space=pltpu.SMEM)
    vm = pl.BlockSpec(memory_space=pltpu.VMEM)
    return pl.pallas_call(
        functools.partial(attn_kernel, group=group),
        out_shape=[jax.ShapeDtypeStruct((QB // 2, 384, 128), bf16), jax.ShapeDtypeStruct((QB // 2, 128, 128), bf16)],
        in_specs=[sm, sm, vm, vm],
        out_specs=[vm, vm],
        scratch_shapes=[
            pltpu.VMEM((QB, BLOCK, 128), f32),
            pltpu.VMEM((QB, 128, 128), bf16),
            pltpu.VMEM((QB, 128, 128), bf16),
            pltpu.VMEM((QB, 128, 128), bf16),
            pltpu.SMEM((QB,), jnp.int32),
            pltpu.SMEM((MAXNB + 2,), jnp.int32),
        ],
        compiler_params=pltpu.CompilerParams(vmem_limit_bytes=62 * 2**20),
        cost_estimate=pl.CostEstimate(flops=2 * 512 * 128 * 128 * 64 * 6, bytes_accessed=2**23, transcendentals=512 * 128 * 128),
    )(nb.T, cnt, hq, hd)


MESH = pl.DeviceIdType.MESH

def cat_tokens(dst, row, col, pair):
    turned = pair.T
    dst[pl.ds(row, HEAD_DIM), pl.ds(col, 128)] = turned[:HEAD_DIM]
    dst[pl.ds(row, HEAD_DIM), pl.ds(col + 128, 128)] = turned[HEAD_DIM:]

def finish_kernel(gqkv, att, lg, g0, g1, g3, g2, w, gin, gqw, gow,
                  rv, fv, at, lv, gv, wv, xt, mt, acc, pqs, pqr, pos, por, mine,
                  loc, zs, zr, xs, xr, as_, ar, qs, qr, os_, or_):
    pipe = lax.axis_index("pipe")
    me = lax.axis_index("seq")
    z, x = me // 4, me % 4
    zr4 = lambda d: (z + d) % 4
    xr4 = lambda d: (x + d) % 4
    def to_z(d): return (pipe, zr4(d) * 4 + x)
    def to_x(d): return (pipe, z * 4 + xr4(d))
    barrier = pltpu.get_barrier_semaphore()
    for d in (1, 2, 3):
        pl.semaphore_signal(barrier, inc=1, device_id=to_z(d), device_id_type=MESH)
        pl.semaphore_signal(barrier, inc=1, device_id=to_x(d), device_id_type=MESH)
    loads = [pltpu.make_async_copy(gqkv.at[z], rv.at[z], loc.at[0]),
             pltpu.make_async_copy(lg, lv, loc.at[1]),
             pltpu.make_async_copy(att.at[:, x], at.at[x], loc.at[2]),
             pltpu.make_async_copy(g0, gv.at[z], loc.at[3]),
             pltpu.make_async_copy(g1, gv.at[zr4(-1)], loc.at[9]),
             pltpu.make_async_copy(g3, gv.at[zr4(-3)], loc.at[10]),
             pltpu.make_async_copy(g2, gv.at[zr4(-2)], loc.at[11]),
             pltpu.make_async_copy(w, wv, loc.at[4])]
    for c in loads:
        c.start()
    pl.semaphore_wait(barrier, 6)

    def remote(src, dst, ss, rs, dev):
        return pltpu.make_async_remote_copy(src_ref=src, dst_ref=dst, send_sem=ss, recv_sem=rs, device_id=dev, device_id_type=MESH)

    ZORDER = [(d, j) for j in (1, 3, 2, 0) for d in (1, 3)] + [(2, j) for j in (1, 3, 2, 0)]
    zc = {}
    for d, j in ZORDER:
        zc[d, j] = remote(gqkv.at[zr4(d), xr4(j)], rv.at[z, xr4(j)], zs.at[d - 1, j], zr.at[d - 1, j], to_z(d))
    xc, ac = {}, {}
    for d in (1, 3, 2):
        xc[0, d] = remote(gqkv.at[z, xr4(d)], fv.at[z, x], xs.at[0, d - 1], xr.at[0, d - 1], to_x(d))
        ac[d] = remote(att.at[:, xr4(d)], at.at[x], as_.at[d - 1], ar.at[d - 1], to_x(d))
        for e in (1, 3, 2):
            xc[e, d] = remote(rv.at[zr4(-e), xr4(d)], fv.at[zr4(-e), x], xs.at[e, d - 1], xr.at[e, d - 1], to_x(d))
    for key in ZORDER:
        zc[key].start()
    for d in (1, 3, 2):
        xc[0, d].start()
    for d in (1, 3, 2):
        ac[d].start()

    def weight_part(zh, out_at):
        def turn(u, carry):
            xi, half = u // 2, u % 2
            col = pl.multiple_of(u * 256, 256)
            xt[pl.ds(64, 128), pl.ds(col, 256)] = rv[zh, xi, half, pl.ds(0, 256), :].T
            cat_tokens(xt, 0, col, rv[zh, xi, half, pl.ds(256, 128), :])
            return carry
        lax.fori_loop(0, 8, turn, 0)
        def tile(n, carry):
            cols = pl.ds(pl.multiple_of(n * 256, 256), 256)
            total = jnp.zeros((192, 256), f32)
            for k in range(4):
                total += jnp.dot(xt[pl.ds(0, 192), pl.ds(k * 512, 512)], lv[k, :, cols], preferred_element_type=f32)
            out_at(cols, total)
            return carry
        lax.fori_loop(0, 4, tile, 0)

    def own_out(cols, total):
        gqw[:, cols] = total

    def sent_out(slot):
        def put(cols, total):
            pqs[slot, :, cols] = total.astype(bf16)
        return put

    def input_part(zh, first=False):
        def build(u, carry):
            half, e = u // 2, u % 2
            rows = pl.ds(pl.multiple_of(u * 128, 128), 128)
            krows = pl.ds(pl.multiple_of(e * 128, 128), 128)
            for p in range(2):
                a, b = 2 * p, 2 * p + 1
                qa = fv[zh, a, half, pl.ds(256, 128), :]
                qb = fv[zh, b, half, pl.ds(256, 128), :]
                low = e == 0
                qa = jnp.where(low, qa[:, :64], qa[:, 64:])
                qb = jnp.where(low, qb[:, :64], qb[:, 64:])
                mt[rows, pl.ds(p * 384, 384)] = jnp.concatenate(
                    [qa, fv[zh, a, half, krows, :], qb, fv[zh, b, half, krows, :]], axis=1)
            return carry
        lax.fori_loop(0, 4, build, 0)
        def tile(n, carry):
            cols = pl.ds(pl.multiple_of(n * 256, 256), 256)
            part = lax.dot_general(mt[...], wv[cols, pl.ds(pl.multiple_of(zh * 768, 128), 768)],
                                   (((1,), (1,)), ((), ())), preferred_element_type=f32)
            if first:
                acc[:, cols] = gv[z, :, cols].astype(f32) + part
            else:
                acc[:, cols] += part
            return carry
        lax.fori_loop(0, 4, tile, 0)

    loads[0].wait()
    loads[1].wait()
    here = pltpu.make_async_copy
    own = here(rv.at[z, x], fv.at[z, x], loc.at[5])
    own.start()
    weight_part(z, own_out)

    for c in loads[2:]:
        c.wait()

    def arrive(d, j):
        zc[d, j].wait_recv()
        if j:
            xc[d, j].start()

    locals_, qc, oc = {}, {}, {}

    def make_part(e):
        weight_part(zr4(-e), sent_out(e - 1))
        qc[e] = remote(pqs.at[e - 1], pqr.at[e - 1], qs.at[e - 1], qr.at[e - 1], to_z(-e))

    def take_own(e):
        locals_[e] = here(rv.at[zr4(-e), x], fv.at[zr4(-e), x], loc.at[5 + e])
        locals_[e].start()

    def turn_att(u, carry):
        zi, half = u // 2, u % 2
        col = pl.multiple_of(u * 256, 256)
        for xh in range(4):
            cat_tokens(xt, xh * 64, col, at[xh, zi, half])
        return carry

    def att_tile(n, carry):
        cols = pl.ds(pl.multiple_of(n * 256, 256), 256)
        total = jnp.zeros((256, 256), f32)
        for k in range(4):
            total += jnp.dot(xt[:, pl.ds(k * 512, 512)], gv[k, :, cols], preferred_element_type=f32)
        mine[:, cols] = total
        for xh in range(4):
            pos[xh, :, cols] = total[xh * 64:(xh + 1) * 64].astype(bf16)
        return carry

    for d, j in ZORDER[:8]:
        arrive(d, j)
    take_own(1)
    take_own(3)
    make_part(1)
    for d, j in ZORDER[8:10]:
        arrive(d, j)
    make_part(3)
    for d, j in ZORDER[10:]:
        arrive(d, j)
    take_own(2)
    qc[1].start()
    qc[3].start()
    make_part(2)
    qc[2].start()
    for d in (1, 3, 2):
        ac[d].wait_recv()
    lax.fori_loop(0, 8, turn_att, 0)
    lax.fori_loop(0, 4, att_tile, 0)
    gow[...] = mine[pl.ds(pl.multiple_of(x * 64, 64), 64), :]
    for d in (1, 3, 2):
        oc[d] = remote(pos.at[xr4(d)], por.at[d - 1], os_.at[d - 1], or_.at[d - 1], to_x(d))
        oc[d].start()
    for d in (1, 3, 2):
        xc[0, d].wait_recv()
    own.wait()
    input_part(z, first=True)
    for e in (1, 3, 2):
        for d in (1, 3, 2):
            xc[e, d].wait_recv()
        locals_[e].wait()
        input_part(zr4(-e))
    gin[...] = acc[...].astype(bf16)
    for d in (1, 3, 2):
        oc[d].wait_recv()
        gow[...] += por[d - 1].astype(f32)
    for d in (1, 3, 2):
        qc[d].wait_recv()
        gqw[...] += pqr[d - 1].astype(f32)
    for c in [*zc.values(), *xc.values(), *ac.values(), *oc.values(), *qc.values()]:
        c.wait_send()

def finish(gqkv, att, lg, g0, g1, g3, g2, w, cid=1):
    anys = pl.BlockSpec(memory_space=pl.ANY)
    vm = pl.BlockSpec(memory_space=pltpu.VMEM)
    D = pltpu.SemaphoreType.DMA
    return pl.pallas_call(finish_kernel,
        out_shape=[jax.ShapeDtypeStruct((512, 1024), bf16), jax.ShapeDtypeStruct((192, 1024), f32), jax.ShapeDtypeStruct((64, 1024), f32)],
        in_specs=[anys] * 8, out_specs=[vm] * 3,
        scratch_shapes=[
            pltpu.VMEM((4, 4, 2, 384, 128), bf16), pltpu.VMEM((4, 4, 2, 384, 128), bf16), pltpu.VMEM((4, 4, 2, 128, 128), bf16),
            pltpu.VMEM((4, 512, 1024), bf16), pltpu.VMEM((4, 512, 1024), bf16), pltpu.VMEM((1024, 3072), bf16),
            pltpu.VMEM((256, 2048), bf16), pltpu.VMEM((512, 768), bf16), pltpu.VMEM((512, 1024), f32),
            pltpu.VMEM((3, 192, 1024), bf16), pltpu.VMEM((3, 192, 1024), bf16),
            pltpu.VMEM((4, 64, 1024), bf16), pltpu.VMEM((3, 64, 1024), bf16), pltpu.VMEM((256, 1024), f32),
            D((12,)), D((3, 4)), D((3, 4)), D((4, 3)), D((4, 3)), D((3,)), D((3,)), D((3,)), D((3,)), D((3,)), D((3,))],
        compiler_params=pltpu.CompilerParams(collective_id=cid, has_side_effects=True, vmem_limit_bytes=62 * 2**20),
        cost_estimate=pl.CostEstimate(flops=8 * 10**9, bytes_accessed=2 * 10**7, transcendentals=0),
    )(gqkv.reshape(4, 4, 2, 384, 128), att.reshape(4, 4, 2, 128, 128), lg, g0, g1, g3, g2, w)


def begin_kernel(lin, hand, w, wo, hqkv, hd, lg, g,
                 lv, gv, w4, wov, sq, sd, dv,
                 loc, hs, hr, gs, gr, zs, zr, ds_, dr, es, er):
    pipe = lax.axis_index("pipe")
    me = lax.axis_index("seq")
    z, x = me // 4, me % 4
    zr4 = lambda d: (z + d) % 4
    xr4 = lambda d: (x + d) % 4
    def to_z(d): return (pipe, zr4(d) * 4 + x)
    def to_x(d): return (pipe, z * 4 + xr4(d))
    barrier = pltpu.get_barrier_semaphore()
    for d in (1, 2, 3):
        pl.semaphore_signal(barrier, inc=1, device_id=to_z(d), device_id_type=MESH)
        pl.semaphore_signal(barrier, inc=1, device_id=to_x(d), device_id_type=MESH)
    pl.semaphore_signal(barrier, inc=1, device_id=((pipe + 1) % 8, me), device_id_type=MESH)

    def here(src, dst, sem):
        return pltpu.make_async_copy(src, dst, sem)

    def remote(src, dst, ss, rs, dev):
        return pltpu.make_async_remote_copy(src_ref=src, dst_ref=dst, send_sem=ss, recv_sem=rs, device_id=dev, device_id_type=MESH)

    load_l = here(lin, lv.at[x], loc.at[0])
    load_l.start()
    load_w = []
    for zh in range(4):
        first = pl.multiple_of(((12 * zh + 3 * x) // 2) * 128, 128)
        load_w.append(here(w.at[:, pl.ds(first, 256)], w4.at[zh], loc.at[1 + zh]))
        load_w[-1].start()
    load_wo = here(wo, wov, loc.at[5])
    load_wo.start()
    pl.semaphore_wait(barrier, 7)

    given = remote(hand, gv, hs, hr, ((pipe + 7) % 8, me))
    right = {h: remote(lin.at[h], lv.at[x, h], gs.at[0, h], gr.at[0, h], to_x(1)) for h in (0, 1)}
    left = {h: remote(lin.at[h], lv.at[x, h], gs.at[1, h], gr.at[1, h], to_x(3)) for h in (0, 1)}
    right[2] = remote(lv.at[xr4(3), 0], lv.at[xr4(3), 0], gs.at[0, 2], gr.at[0, 2], to_x(1))
    left[2] = remote(lv.at[xr4(1), 1], lv.at[xr4(1), 1], gs.at[1, 2], gr.at[1, 2], to_x(3))
    right[0].start()
    left[1].start()
    given.start()
    right[1].start()
    left[0].start()

    zc, own, kept = {}, [], []

    def project(r, h):
        xs = xr4(r)
        def head(zh, carry):
            part = jnp.dot(lv[xs, h], w4[zh], preferred_element_type=f32).astype(bf16)
            part = jnp.where(x % 2 == 1, jnp.concatenate([part[:, 64:], part[:, :64]], axis=1), part)
            sq[xs, zh, h, pl.ds(0, 256), :] = part[:, 64:192]
            sq[xs, zh, h, pl.ds(256, 128), :] = jnp.concatenate([part[:128, :64], part[128:, :64]], axis=1)
            return carry
        lax.fori_loop(0, 4, head, 0)
        for d in (1, 3, 2):
            zc[d, r, h] = remote(sq.at[xs, zr4(d), h], hqkv.at[z, xs, h], zs.at[d - 1, r, h], zr.at[d - 1, r, h], to_z(d))
            zc[d, r, h].start()
        own.append(here(sq.at[xs, z, h], hqkv.at[z, xs, h], loc.at[6 + 2 * r + h]))
        own[-1].start()

    load_l.wait()
    for c in load_w:
        c.wait()
    project(0, 0)
    project(0, 1)
    right[0].wait_recv()
    right[2].start()
    project(3, 0)
    left[1].wait_recv()
    left[2].start()
    project(1, 1)

    given.wait_recv()
    load_wo.wait()
    own.append(here(gv, g, loc.at[14]))
    own[-1].start()
    def heads(n, carry):
        rows = pl.ds(pl.multiple_of(n * 256, 256), 256)
        part = lax.dot_general(gv[...], wov[rows, :], (((1,), (1,)), ((), ())), preferred_element_type=f32).astype(bf16)
        for i in range(4):
            cols = part[:, i * 64:(i + 1) * 64]
            for h in range(2):
                sd[n, i, h] = jnp.concatenate([cols[h * 256:h * 256 + 128], cols[h * 256 + 128:h * 256 + 256]], axis=1)
        return carry
    lax.fori_loop(0, 4, heads, 0)
    dz, dx = {}, {}
    for d in (1, 3, 2):
        dz[d] = remote(sd.at[zr4(d)], dv.at[z], ds_.at[d - 1], dr.at[d - 1], to_z(d))
        dz[d].start()
    own.append(here(sd.at[z, x], hd.at[z, x], loc.at[15]))
    own[-1].start()
    for d in (1, 3, 2):
        dx[0, d] = remote(sd.at[z, xr4(d)], hd.at[z, x], es.at[0, d - 1], er.at[0, d - 1], to_x(d))

    right[1].wait_recv()
    project(3, 1)
    left[0].wait_recv()
    project(1, 0)
    right[2].wait_recv()
    left[2].wait_recv()
    for d in (1, 3, 2):
        dx[0, d].start()
    project(2, 0)
    project(2, 1)
    for e in (1, 3, 2):
        dz[e].wait_recv()
        for d in (1, 3, 2):
            dx[e, d] = remote(dv.at[zr4(-e), xr4(d)], hd.at[zr4(-e), x], es.at[e, d - 1], er.at[e, d - 1], to_x(d))
            dx[e, d].start()
        own.append(here(dv.at[zr4(-e), x], hd.at[zr4(-e), x], loc.at[16 + e]))
        own[-1].start()
    store = here(lv, lg, loc.at[16])
    store.start()
    for c in [*zc.values(), *dx.values()]:
        c.wait_recv()
    for c in own:
        c.wait()
    store.wait()
    given.wait_send()
    for c in [*right.values(), *left.values(), *zc.values(), *dz.values(), *dx.values()]:
        c.wait_send()


def begin(lin, hand, w, wo, cid=2):
    anys = pl.BlockSpec(memory_space=pl.ANY)
    D = pltpu.SemaphoreType.DMA
    return pl.pallas_call(
        begin_kernel,
        out_shape=[
            jax.ShapeDtypeStruct((4, 4, 2, 384, 128), bf16),
            jax.ShapeDtypeStruct((4, 4, 2, 128, 128), bf16),
            jax.ShapeDtypeStruct((4, 2, 256, 1024), bf16),
            jax.ShapeDtypeStruct((512, 1024), bf16),
        ],
        in_specs=[anys] * 4,
        out_specs=[anys] * 4,
        scratch_shapes=[
            pltpu.VMEM((4, 2, 256, 1024), bf16), pltpu.VMEM((512, 1024), bf16),
            pltpu.VMEM((4, 1024, 256), bf16), pltpu.VMEM((1024, 1024), bf16),
            pltpu.VMEM((4, 4, 2, 384, 128), bf16), pltpu.VMEM((4, 4, 2, 128, 128), bf16), pltpu.VMEM((4, 4, 2, 128, 128), bf16),
            D((20,)), D, D, D((2, 3)), D((2, 3)), D((3, 4, 2)), D((3, 4, 2)), D((3,)), D((3,)), D((4, 3)), D((4, 3)),
        ],
        compiler_params=pltpu.CompilerParams(collective_id=cid, has_side_effects=True, vmem_limit_bytes=62 * 2**20),
        cost_estimate=pl.CostEstimate(flops=4 * 10**9, bytes_accessed=2 * 10**7, transcendentals=0),
    )(lin.reshape(2, 256, 1024), hand, w, wo)


def settle_kernel(a, b, c, oa, ob, oc, ha, hb, hc, ins, outs):
    loads, stores = [], []
    for src, held, dst, parts in ((a, ha, oa, 4), (b, hb, ob, 3), (c, hc, oc, 1)):
        rows = src.shape[0] // parts
        for p in range(parts):
            cut, n = pl.ds(p * rows, rows), len(loads)
            loads.append(pltpu.make_async_copy(src.at[cut], held.at[cut], ins.at[n]))
            stores.append(pltpu.make_async_copy(held.at[cut], dst.at[cut], outs.at[n]))
            loads[-1].start()
    for load, store in zip(loads, stores):
        load.wait()
        store.start()
    for store in stores:
        store.wait()


def settle(*arrays):
    anys = pl.BlockSpec(memory_space=pl.ANY)
    return pl.pallas_call(
        settle_kernel,
        out_shape=[jax.ShapeDtypeStruct(a.shape, a.dtype) for a in arrays],
        in_specs=[anys] * 3,
        out_specs=[anys] * 3,
        scratch_shapes=[pltpu.VMEM(a.shape, a.dtype) for a in arrays]
        + [pltpu.SemaphoreType.DMA((8,)), pltpu.SemaphoreType.DMA((8,))],
        compiler_params=pltpu.CompilerParams(has_side_effects=True, vmem_limit_bytes=62 * 2**20),
    )(*arrays)


def local(layer_input, handoff, qkv_weight, out_weight, neighbours, counts):
    weight_in = qkv_weight[0]
    hqkv, hd, lg, grad_out = begin(layer_input[0], handoff[0], weight_in, out_weight[0])
    around = [lax.ppermute(grad_out, "seq", [(i, (i + 4 * d) % 16) for i in range(16)]) for d in (1, 3, 2)]
    gqkv, att = attention(hqkv.reshape(32, 384, 128), hd.reshape(32, 128, 128), neighbours[0, 0], counts[0, 0])
    grad_input, grad_qkv_weight, grad_out_weight = finish(gqkv, att, lg.reshape(4, 512, 1024), grad_out, *around, weight_in)
    grad_input, grad_qkv_weight, grad_out_weight = settle(grad_input, grad_qkv_weight, grad_out_weight)
    return (grad_input[None], grad_qkv_weight[None], grad_out_weight[None])


def solution(mesh):
    placed = (
        P("pipe", "seq", None),
        P("pipe", "seq", None),
        P("pipe", None, None),
        P("pipe", None, None),
        P("pipe", "seq", None, None),
        P("pipe", "seq", None),
    )
    return jax.shard_map(
        local,
        mesh=mesh,
        in_specs=placed,
        out_specs=(P("pipe", "seq", None), P("pipe", "seq", None), P("pipe", "seq", None)),
        check_vma=False,
    )
```

```python
import functools
import jax, jax.numpy as jnp
from jax import lax
from jax.experimental import pallas as pl
from jax.experimental.pallas import tpu as pltpu
from jax.sharding import PartitionSpec as P
HEAD_DIM=64; BLOCK=128; MAXNB=8; QB=64; GROUP=8
NEAR = 384
HALF = (512 - NEAR) // 2
f32=jnp.float32; bf16=jnp.bfloat16

def attn_body(order, nb, cnt, hq, qd, gqa, acc, kvt, group, i, slots):
    scale = HEAD_DIM ** -0.5
    half_row = lax.broadcasted_iota(jnp.int32, (BLOCK, BLOCK), 0) < HEAD_DIM
    half_lane = lax.broadcasted_iota(jnp.int32, (BLOCK, BLOCK), 1) < HEAD_DIM
    zero = jnp.zeros((BLOCK, BLOCK), bf16)
    dn = (((1,), (0,)), ((), ()))
    mm = lambda a, b: lax.dot_general(a, b, dn, preferred_element_type=f32)
    chains = []
    for g in range(group):
        b = order[i * group + g]
        chains.append((b, cnt[b], [nb[j, b] for j in range(slots)]))
    def first(g):
        b, c, ns = chains[g]
        own = qd[b]
        own_t = own.T
        q_t = jnp.where(half_row, own_t * jnp.asarray(scale, bf16), zero)
        d_t = jnp.where(half_row, zero, own_t)
        right = jnp.concatenate([q_t, d_t], axis=1)
        scores, dps = [], []
        every = mm(jnp.concatenate([load_keys(hq, ns[j]) for j in range(slots)], axis=0), right)
        for j in range(slots):
            both = every[j * BLOCK:(j + 1) * BLOCK]
            s = both[:, :BLOCK]
            if j > 0:
                s = jnp.where(j < c, s, -jnp.inf)
            scores.append(s)
            dps.append(both[:, BLOCK:])
        return own, own_t, scores, dps

    def second(g, own, own_t, scores, dps):
        top = scores[0]
        for s in scores[1:]:
            top = jnp.maximum(top, s)
        top = jnp.max(top, axis=0, keepdims=True)
        es = [jnp.exp(s - top) for s in scores]
        tot = es[0]
        for e in es[1:]:
            tot = tot + e
        inv = 1.0 / jnp.sum(tot, axis=0, keepdims=True)
        ps = [e * inv for e in es]
        b, c, ns = chains[g]
        low_all = jnp.concatenate([p.astype(bf16) for p in ps], axis=0)
        att_t = mm(jnp.concatenate([kvt[ns[j], HEAD_DIM:, :] for j in range(slots)], axis=1), low_all)
        return own, own_t, dps, ps, low_all, att_t.astype(bf16)

    def third(g, own, own_t, dps, ps, low_all, att_t):
        b, c, ns = chains[g]
        dot = jnp.sum(own_t[HEAD_DIM:, :].astype(f32) * att_t.astype(f32), axis=0, keepdims=True)
        ds_all = jnp.concatenate([(p * (dp - dot)).astype(bf16) for p, dp in zip(ps, dps)], axis=0)
        left = jnp.concatenate([jnp.where(half_lane, own * jnp.asarray(scale, bf16), zero), jnp.where(half_lane, zero, own)], axis=0)
        terms = mm(jnp.concatenate([ds_all, low_all], axis=1), left)
        gq_t = mm(jnp.concatenate([kvt[ns[j], :HEAD_DIM, :] for j in range(slots)], axis=1), ds_all)
        for j in range(slots):
            acc[ns[j]] += terms[j * BLOCK:(j + 1) * BLOCK]
        gq_t = (gq_t * scale).astype(bf16)
        gqa[b] = jnp.concatenate([gq_t, att_t], axis=0).T

    ones, twos = {}, {}
    for t in range(group + 2):
        if t < group:
            ones[t] = first(t)
        if 0 <= t - 1 < group:
            twos[t - 1] = second(t - 1, *ones.pop(t - 1))
        if 0 <= t - 2 < group:
            third(t - 2, *twos.pop(t - 2))


def load_keys(hq, n):
    half, rows = key_rows(n)
    return hq[half, rows, :]


def key_rows(n):
    return n // 2, pl.ds(pl.multiple_of((n % 2) * BLOCK, BLOCK), BLOCK)


def attn_kernel(nb, cnt, hq, hd, hg, ha, acc, kvt, qd, gqa, order, place, *, group):
    for c in range(MAXNB + 2):
        place[c] = 0

    def prep_keys(u, carry):
        for e in range(2):
            c = cnt[2 * u + e] + 1
            place[c] = place[c] + 1
            kvt[2 * u + e] = hq[u, pl.ds(e * BLOCK, BLOCK), :].T
        return carry
    lax.fori_loop(0, QB // 2, prep_keys, 0, unroll=2)
    for c in range(1, MAXNB + 1):
        place[c] = place[c] + place[c - 1]

    def prep_rows(u, carry):
        for e in range(2):
            c = cnt[2 * u + e]
            at = place[c]
            order[at] = 2 * u + e
            place[c] = at + 1
            acc[2 * u + e] = jnp.zeros((BLOCK, BLOCK), f32)
        q = hq[u, pl.ds(256, BLOCK), :]
        d = hd[u]
        qd[2 * u] = jnp.concatenate([q[:, :HEAD_DIM], d[:, :HEAD_DIM]], axis=1)
        qd[2 * u + 1] = jnp.concatenate([q[:, HEAD_DIM:], d[:, HEAD_DIM:]], axis=1)
        return carry
    lax.fori_loop(0, QB // 2, prep_rows, 0, unroll=2)

    def step(i, carry):
        most = cnt[order[i * group + group - 1]]
        for slots in range(1, MAXNB + 1):
            @pl.when(most == slots)
            def run():
                attn_body(order, nb, cnt, hq, qd, gqa, acc, kvt, group, i, slots)
        return carry
    lax.fori_loop(0, QB // group, step, 0)

    def fin(u, carry):
        for e in range(2):
            hg[u, pl.ds(e * BLOCK, BLOCK), :] = acc[2 * u + e].astype(bf16)
        a, b = gqa[2 * u], gqa[2 * u + 1]
        hg[u, pl.ds(256, BLOCK), :] = jnp.concatenate([a[:, :HEAD_DIM], b[:, :HEAD_DIM]], axis=1)
        ha[u] = jnp.concatenate([a[:, HEAD_DIM:], b[:, HEAD_DIM:]], axis=1)
        return carry
    lax.fori_loop(0, QB // 2, fin, 0, unroll=2)


def attention(hq, hd, nb, cnt, group=GROUP):
    sm = pl.BlockSpec(memory_space=pltpu.SMEM)
    vm = pl.BlockSpec(memory_space=pltpu.VMEM)
    return pl.pallas_call(
        functools.partial(attn_kernel, group=group),
        out_shape=[jax.ShapeDtypeStruct((QB // 2, 384, 128), bf16), jax.ShapeDtypeStruct((QB // 2, 128, 128), bf16)],
        in_specs=[sm, sm, vm, vm],
        out_specs=[vm, vm],
        scratch_shapes=[
            pltpu.VMEM((QB, BLOCK, 128), f32),
            pltpu.VMEM((QB, 128, 128), bf16),
            pltpu.VMEM((QB, 128, 128), bf16),
            pltpu.VMEM((QB, 128, 128), bf16),
            pltpu.SMEM((QB,), jnp.int32),
            pltpu.SMEM((MAXNB + 2,), jnp.int32),
        ],
        compiler_params=pltpu.CompilerParams(vmem_limit_bytes=62 * 2**20),
        cost_estimate=pl.CostEstimate(flops=2 * 512 * 128 * 128 * 64 * 6, bytes_accessed=2**23, transcendentals=512 * 128 * 128),
    )(nb.T, cnt, hq, hd)


MESH = pl.DeviceIdType.MESH

def cat_tokens(dst, row, col, pair):
    turned = pair.T
    dst[pl.ds(row, HEAD_DIM), pl.ds(col, 128)] = turned[:HEAD_DIM]
    dst[pl.ds(row, HEAD_DIM), pl.ds(col + 128, 128)] = turned[HEAD_DIM:]

def finish_kernel(gqkv, att, lg, g0, g1, g3, g2, w, gin, gqw, gow,
                  rv, fv, at, lv, gv, wv, xt, mt, acc, pqs, pqr, pos, por, mine,
                  loc, zs, zr, xs, xr, as_, ar, qs, qr, os_, or_, fs, fr):
    pipe = lax.axis_index("pipe")
    me = lax.axis_index("seq")
    z, x = me // 4, me % 4
    zr4 = lambda d: (z + d) % 4
    xr4 = lambda d: (x + d) % 4
    def to_z(d): return (pipe, zr4(d) * 4 + x)
    def to_x(d): return (pipe, z * 4 + xr4(d))
    barrier = pltpu.get_barrier_semaphore()
    for d in (1, 2, 3):
        pl.semaphore_signal(barrier, inc=1, device_id=to_z(d), device_id_type=MESH)
        pl.semaphore_signal(barrier, inc=1, device_id=to_x(d), device_id_type=MESH)
    loads = [pltpu.make_async_copy(gqkv.at[z], rv.at[z], loc.at[0]),
             pltpu.make_async_copy(lg, lv, loc.at[1]),
             pltpu.make_async_copy(att.at[:, x], at.at[x], loc.at[2]),
             pltpu.make_async_copy(g0, gv.at[z], loc.at[3]),
             pltpu.make_async_copy(g1, gv.at[zr4(-1)], loc.at[9]),
             pltpu.make_async_copy(g3, gv.at[zr4(-3)], loc.at[10]),
             pltpu.make_async_copy(g2, gv.at[zr4(-2), pl.ds(0, NEAR)], loc.at[11]),
             pltpu.make_async_copy(w, wv, loc.at[4])]
    for c in loads:
        c.start()
    pl.semaphore_wait(barrier, 6)

    def remote(src, dst, ss, rs, dev):
        return pltpu.make_async_remote_copy(src_ref=src, dst_ref=dst, send_sem=ss, recv_sem=rs, device_id=dev, device_id_type=MESH)

    ZORDER = [(d, j) for j in (1, 3, 2, 0) for d in (1, 3)] + [(2, j) for j in (1, 3, 2, 0)]
    zc = {}
    for d, j in ZORDER:
        zc[d, j] = remote(gqkv.at[zr4(d), xr4(j)], rv.at[z, xr4(j)], zs.at[d - 1, j], zr.at[d - 1, j], to_z(d))
    xc, ac = {}, {}
    for d in (1, 3, 2):
        xc[0, d] = remote(gqkv.at[z, xr4(d)], fv.at[z, x], xs.at[0, d - 1], xr.at[0, d - 1], to_x(d))
        ac[d] = remote(att.at[:, xr4(d)], at.at[x], as_.at[d - 1], ar.at[d - 1], to_x(d))
        for e in (1, 3, 2):
            xc[e, d] = remote(rv.at[zr4(-e), xr4(d)], fv.at[zr4(-e), x], xs.at[e, d - 1], xr.at[e, d - 1], to_x(d))
    onward = [remote(g1.at[pl.ds(NEAR, HALF)], gv.at[zr4(-1), pl.ds(NEAR, HALF)], fs.at[0], fr.at[0], to_z(1)),
              remote(g3.at[pl.ds(NEAR + HALF, HALF)], gv.at[zr4(1), pl.ds(NEAR + HALF, HALF)], fs.at[1], fr.at[1], to_z(3))]
    for key in ZORDER:
        zc[key].start()
    for c in onward:
        c.start()
    for d in (1, 3, 2):
        xc[0, d].start()
    for d in (1, 3, 2):
        ac[d].start()

    def weight_part(zh, out_at):
        def turn(u, carry):
            xi, half = u // 2, u % 2
            col = pl.multiple_of(u * 256, 256)
            xt[pl.ds(64, 128), pl.ds(col, 256)] = rv[zh, xi, half, pl.ds(0, 256), :].T
            cat_tokens(xt, 0, col, rv[zh, xi, half, pl.ds(256, 128), :])
            return carry
        lax.fori_loop(0, 8, turn, 0)
        def tile(n, carry):
            cols = pl.ds(pl.multiple_of(n * 256, 256), 256)
            total = jnp.zeros((192, 256), f32)
            for k in range(4):
                total += jnp.dot(xt[pl.ds(0, 192), pl.ds(k * 512, 512)], lv[k, :, cols], preferred_element_type=f32)
            out_at(cols, total)
            return carry
        lax.fori_loop(0, 4, tile, 0)

    def own_out(cols, total):
        gqw[:, cols] = total

    def sent_out(slot):
        def put(cols, total):
            pqs[slot, :, cols] = total.astype(bf16)
        return put

    def input_part(zh, first=False):
        def build(u, carry):
            half, e = u // 2, u % 2
            rows = pl.ds(pl.multiple_of(u * 128, 128), 128)
            krows = pl.ds(pl.multiple_of(e * 128, 128), 128)
            for p in range(2):
                a, b = 2 * p, 2 * p + 1
                qa = fv[zh, a, half, pl.ds(256, 128), :]
                qb = fv[zh, b, half, pl.ds(256, 128), :]
                low = e == 0
                qa = jnp.where(low, qa[:, :64], qa[:, 64:])
                qb = jnp.where(low, qb[:, :64], qb[:, 64:])
                mt[rows, pl.ds(p * 384, 384)] = jnp.concatenate(
                    [qa, fv[zh, a, half, krows, :], qb, fv[zh, b, half, krows, :]], axis=1)
            return carry
        lax.fori_loop(0, 4, build, 0)
        def tile(n, carry):
            cols = pl.ds(pl.multiple_of(n * 256, 256), 256)
            part = lax.dot_general(mt[...], wv[cols, pl.ds(pl.multiple_of(zh * 768, 128), 768)],
                                   (((1,), (1,)), ((), ())), preferred_element_type=f32)
            if first:
                acc[:, cols] = gv[z, :, cols].astype(f32) + part
            else:
                acc[:, cols] += part
            return carry
        lax.fori_loop(0, 4, tile, 0)

    loads[0].wait()
    loads[1].wait()
    here = pltpu.make_async_copy
    own = here(rv.at[z, x], fv.at[z, x], loc.at[5])
    own.start()
    weight_part(z, own_out)

    for c in loads[2:]:
        c.wait()

    def arrive(d, j):
        zc[d, j].wait_recv()
        if j:
            xc[d, j].start()

    locals_, qc, oc = {}, {}, {}

    def make_part(e):
        weight_part(zr4(-e), sent_out(e - 1))
        qc[e] = remote(pqs.at[e - 1], pqr.at[e - 1], qs.at[e - 1], qr.at[e - 1], to_z(-e))

    def take_own(e):
        locals_[e] = here(rv.at[zr4(-e), x], fv.at[zr4(-e), x], loc.at[5 + e])
        locals_[e].start()

    def turn_att(u, carry):
        zi, half = u // 2, u % 2
        col = pl.multiple_of(u * 256, 256)
        for xh in range(4):
            cat_tokens(xt, xh * 64, col, at[xh, zi, half])
        return carry

    def att_tile(n, carry):
        cols = pl.ds(pl.multiple_of(n * 256, 256), 256)
        total = jnp.zeros((256, 256), f32)
        for k in range(4):
            total += jnp.dot(xt[:, pl.ds(k * 512, 512)], gv[k, :, cols], preferred_element_type=f32)
        mine[:, cols] = total
        for xh in range(4):
            pos[xh, :, cols] = total[xh * 64:(xh + 1) * 64].astype(bf16)
        return carry

    for d, j in ZORDER[:8]:
        arrive(d, j)
    take_own(1)
    take_own(3)
    make_part(1)
    for d, j in ZORDER[8:10]:
        arrive(d, j)
    make_part(3)
    for d, j in ZORDER[10:]:
        arrive(d, j)
    take_own(2)
    qc[1].start()
    qc[3].start()
    make_part(2)
    qc[2].start()
    for d in (1, 3, 2):
        ac[d].wait_recv()
    for c in onward:
        c.wait_recv()
    lax.fori_loop(0, 8, turn_att, 0)
    lax.fori_loop(0, 4, att_tile, 0)
    gow[...] = mine[pl.ds(pl.multiple_of(x * 64, 64), 64), :]
    for d in (1, 3, 2):
        oc[d] = remote(pos.at[xr4(d)], por.at[d - 1], os_.at[d - 1], or_.at[d - 1], to_x(d))
        oc[d].start()
    for d in (1, 3, 2):
        xc[0, d].wait_recv()
    own.wait()
    input_part(z, first=True)
    for e in (1, 3, 2):
        for d in (1, 3, 2):
            xc[e, d].wait_recv()
        locals_[e].wait()
        input_part(zr4(-e))
    gin[...] = acc[...].astype(bf16)
    for d in (1, 3, 2):
        oc[d].wait_recv()
        gow[...] += por[d - 1].astype(f32)
    for d in (1, 3, 2):
        qc[d].wait_recv()
        gqw[...] += pqr[d - 1].astype(f32)
    for c in [*zc.values(), *xc.values(), *ac.values(), *oc.values(), *qc.values(), *onward]:
        c.wait_send()

def finish(gqkv, att, lg, g0, g1, g3, g2, w, cid=1):
    anys = pl.BlockSpec(memory_space=pl.ANY)
    vm = pl.BlockSpec(memory_space=pltpu.VMEM)
    D = pltpu.SemaphoreType.DMA
    return pl.pallas_call(finish_kernel,
        out_shape=[jax.ShapeDtypeStruct((512, 1024), bf16), jax.ShapeDtypeStruct((192, 1024), f32), jax.ShapeDtypeStruct((64, 1024), f32)],
        in_specs=[anys] * 8, out_specs=[vm] * 3,
        scratch_shapes=[
            pltpu.VMEM((4, 4, 2, 384, 128), bf16), pltpu.VMEM((4, 4, 2, 384, 128), bf16), pltpu.VMEM((4, 4, 2, 128, 128), bf16),
            pltpu.VMEM((4, 512, 1024), bf16), pltpu.VMEM((4, 512, 1024), bf16), pltpu.VMEM((1024, 3072), bf16),
            pltpu.VMEM((256, 2048), bf16), pltpu.VMEM((512, 768), bf16), pltpu.VMEM((512, 1024), f32),
            pltpu.VMEM((3, 192, 1024), bf16), pltpu.VMEM((3, 192, 1024), bf16),
            pltpu.VMEM((4, 64, 1024), bf16), pltpu.VMEM((3, 64, 1024), bf16), pltpu.VMEM((256, 1024), f32),
            D((12,)), D((3, 4)), D((3, 4)), D((4, 3)), D((4, 3)), D((3,)), D((3,)), D((3,)), D((3,)), D((3,)), D((3,)), D((2,)), D((2,))],
        compiler_params=pltpu.CompilerParams(collective_id=cid, has_side_effects=True, vmem_limit_bytes=62 * 2**20),
        cost_estimate=pl.CostEstimate(flops=8 * 10**9, bytes_accessed=2 * 10**7, transcendentals=0),
    )(gqkv.reshape(4, 4, 2, 384, 128), att.reshape(4, 4, 2, 128, 128), lg, g0, g1, g3, g2, w)


def begin_kernel(lin, hand, w, wo, hqkv, hd, lg, g, gt,
                 lv, gv, w4, wov, sq, sd, dv,
                 loc, hs, hr, gs, gr, zs, zr, ds_, dr, es, er):
    pipe = lax.axis_index("pipe")
    me = lax.axis_index("seq")
    z, x = me // 4, me % 4
    zr4 = lambda d: (z + d) % 4
    xr4 = lambda d: (x + d) % 4
    def to_z(d): return (pipe, zr4(d) * 4 + x)
    def to_x(d): return (pipe, z * 4 + xr4(d))
    barrier = pltpu.get_barrier_semaphore()
    for d in (1, 2, 3):
        pl.semaphore_signal(barrier, inc=1, device_id=to_z(d), device_id_type=MESH)
        pl.semaphore_signal(barrier, inc=1, device_id=to_x(d), device_id_type=MESH)
    pl.semaphore_signal(barrier, inc=1, device_id=((pipe + 1) % 8, me), device_id_type=MESH)

    def here(src, dst, sem):
        return pltpu.make_async_copy(src, dst, sem)

    def remote(src, dst, ss, rs, dev):
        return pltpu.make_async_remote_copy(src_ref=src, dst_ref=dst, send_sem=ss, recv_sem=rs, device_id=dev, device_id_type=MESH)

    load_l = here(lin, lv.at[x], loc.at[0])
    load_l.start()
    load_w = []
    for zh in range(4):
        first = pl.multiple_of(((12 * zh + 3 * x) // 2) * 128, 128)
        load_w.append(here(w.at[:, pl.ds(first, 256)], w4.at[zh], loc.at[1 + zh]))
        load_w[-1].start()
    load_wo = here(wo, wov, loc.at[5])
    load_wo.start()
    pl.semaphore_wait(barrier, 7)

    given = remote(hand, gv, hs, hr, ((pipe + 7) % 8, me))
    right = {h: remote(lin.at[h], lv.at[x, h], gs.at[0, h], gr.at[0, h], to_x(1)) for h in (0, 1)}
    left = {h: remote(lin.at[h], lv.at[x, h], gs.at[1, h], gr.at[1, h], to_x(3)) for h in (0, 1)}
    right[2] = remote(lv.at[xr4(3), 0], lv.at[xr4(3), 0], gs.at[0, 2], gr.at[0, 2], to_x(1))
    left[2] = remote(lv.at[xr4(1), 1], lv.at[xr4(1), 1], gs.at[1, 2], gr.at[1, 2], to_x(3))
    right[0].start()
    left[1].start()
    given.start()
    right[1].start()
    left[0].start()

    zc, own, kept = {}, [], []

    def project(r, h):
        xs = xr4(r)
        def head(zh, carry):
            part = jnp.dot(lv[xs, h], w4[zh], preferred_element_type=f32).astype(bf16)
            part = jnp.where(x % 2 == 1, jnp.concatenate([part[:, 64:], part[:, :64]], axis=1), part)
            sq[xs, zh, h, pl.ds(0, 256), :] = part[:, 64:192]
            sq[xs, zh, h, pl.ds(256, 128), :] = jnp.concatenate([part[:128, :64], part[128:, :64]], axis=1)
            return carry
        lax.fori_loop(0, 4, head, 0)
        for d in (1, 3, 2):
            zc[d, r, h] = remote(sq.at[xs, zr4(d), h], hqkv.at[z, xs, h], zs.at[d - 1, r, h], zr.at[d - 1, r, h], to_z(d))
            zc[d, r, h].start()
        own.append(here(sq.at[xs, z, h], hqkv.at[z, xs, h], loc.at[6 + 2 * r + h]))
        own[-1].start()

    load_l.wait()
    for c in load_w:
        c.wait()
    project(0, 0)
    project(0, 1)
    right[0].wait_recv()
    right[2].start()
    project(3, 0)
    left[1].wait_recv()
    left[2].start()
    project(1, 1)

    given.wait_recv()
    load_wo.wait()
    own.append(here(gv, g, loc.at[14]))
    own[-1].start()
    own.append(here(gv.at[pl.ds(0, NEAR)], gt, loc.at[20]))
    own[-1].start()
    def heads(n, carry):
        rows = pl.ds(pl.multiple_of(n * 256, 256), 256)
        part = lax.dot_general(gv[...], wov[rows, :], (((1,), (1,)), ((), ())), preferred_element_type=f32).astype(bf16)
        for i in range(4):
            cols = part[:, i * 64:(i + 1) * 64]
            for h in range(2):
                sd[n, i, h] = jnp.concatenate([cols[h * 256:h * 256 + 128], cols[h * 256 + 128:h * 256 + 256]], axis=1)
        return carry
    lax.fori_loop(0, 4, heads, 0)
    dz, dx = {}, {}
    for d in (1, 3, 2):
        dz[d] = remote(sd.at[zr4(d)], dv.at[z], ds_.at[d - 1], dr.at[d - 1], to_z(d))
        dz[d].start()
    own.append(here(sd.at[z, x], hd.at[z, x], loc.at[15]))
    own[-1].start()
    for d in (1, 3, 2):
        dx[0, d] = remote(sd.at[z, xr4(d)], hd.at[z, x], es.at[0, d - 1], er.at[0, d - 1], to_x(d))

    right[1].wait_recv()
    project(3, 1)
    left[0].wait_recv()
    project(1, 0)
    right[2].wait_recv()
    left[2].wait_recv()
    for d in (1, 3, 2):
        dx[0, d].start()
    project(2, 0)
    project(2, 1)
    for e in (1, 3, 2):
        dz[e].wait_recv()
        for d in (1, 3, 2):
            dx[e, d] = remote(dv.at[zr4(-e), xr4(d)], hd.at[zr4(-e), x], es.at[e, d - 1], er.at[e, d - 1], to_x(d))
            dx[e, d].start()
        own.append(here(dv.at[zr4(-e), x], hd.at[zr4(-e), x], loc.at[16 + e]))
        own[-1].start()
    store = here(lv, lg, loc.at[16])
    store.start()
    for c in [*zc.values(), *dx.values()]:
        c.wait_recv()
    for c in own:
        c.wait()
    store.wait()
    given.wait_send()
    for c in [*right.values(), *left.values(), *zc.values(), *dz.values(), *dx.values()]:
        c.wait_send()


def begin(lin, hand, w, wo, cid=2):
    anys = pl.BlockSpec(memory_space=pl.ANY)
    D = pltpu.SemaphoreType.DMA
    return pl.pallas_call(
        begin_kernel,
        out_shape=[
            jax.ShapeDtypeStruct((4, 4, 2, 384, 128), bf16),
            jax.ShapeDtypeStruct((4, 4, 2, 128, 128), bf16),
            jax.ShapeDtypeStruct((4, 2, 256, 1024), bf16),
            jax.ShapeDtypeStruct((512, 1024), bf16),
            jax.ShapeDtypeStruct((NEAR, 1024), bf16),
        ],
        in_specs=[anys] * 4,
        out_specs=[anys] * 5,
        scratch_shapes=[
            pltpu.VMEM((4, 2, 256, 1024), bf16), pltpu.VMEM((512, 1024), bf16),
            pltpu.VMEM((4, 1024, 256), bf16), pltpu.VMEM((1024, 1024), bf16),
            pltpu.VMEM((4, 4, 2, 384, 128), bf16), pltpu.VMEM((4, 4, 2, 128, 128), bf16), pltpu.VMEM((4, 4, 2, 128, 128), bf16),
            D((21,)), D, D, D((2, 3)), D((2, 3)), D((3, 4, 2)), D((3, 4, 2)), D((3,)), D((3,)), D((4, 3)), D((4, 3)),
        ],
        compiler_params=pltpu.CompilerParams(collective_id=cid, has_side_effects=True, vmem_limit_bytes=62 * 2**20),
        cost_estimate=pl.CostEstimate(flops=4 * 10**9, bytes_accessed=2 * 10**7, transcendentals=0),
    )(lin.reshape(2, 256, 1024), hand, w, wo)


def settle_kernel(a, b, c, oa, ob, oc, ha, hb, hc, ins, outs):
    loads, stores = [], []
    for src, held, dst, parts in ((a, ha, oa, 4), (b, hb, ob, 3), (c, hc, oc, 1)):
        rows = src.shape[0] // parts
        for p in range(parts):
            cut, n = pl.ds(p * rows, rows), len(loads)
            loads.append(pltpu.make_async_copy(src.at[cut], held.at[cut], ins.at[n]))
            stores.append(pltpu.make_async_copy(held.at[cut], dst.at[cut], outs.at[n]))
            loads[-1].start()
    for load, store in zip(loads, stores):
        load.wait()
        store.start()
    for store in stores:
        store.wait()


def settle(*arrays):
    anys = pl.BlockSpec(memory_space=pl.ANY)
    return pl.pallas_call(
        settle_kernel,
        out_shape=[jax.ShapeDtypeStruct(a.shape, a.dtype) for a in arrays],
        in_specs=[anys] * 3,
        out_specs=[anys] * 3,
        scratch_shapes=[pltpu.VMEM(a.shape, a.dtype) for a in arrays]
        + [pltpu.SemaphoreType.DMA((8,)), pltpu.SemaphoreType.DMA((8,))],
        compiler_params=pltpu.CompilerParams(has_side_effects=True, vmem_limit_bytes=62 * 2**20),
    )(*arrays)


def local(layer_input, handoff, qkv_weight, out_weight, neighbours, counts):
    weight_in = qkv_weight[0]
    hqkv, hd, lg, grad_out, near = begin(layer_input[0], handoff[0], weight_in, out_weight[0])
    def along(rows, d):
        return lax.ppermute(rows, "seq", [(i, (i + 4 * d) % 16) for i in range(16)])
    around = [along(grad_out, 1), along(grad_out, 3), along(near, 2)]
    gqkv, att = attention(hqkv.reshape(32, 384, 128), hd.reshape(32, 128, 128), neighbours[0, 0], counts[0, 0])
    grad_input, grad_qkv_weight, grad_out_weight = finish(gqkv, att, lg.reshape(4, 512, 1024), grad_out, *around, weight_in)
    grad_input, grad_qkv_weight, grad_out_weight = settle(grad_input, grad_qkv_weight, grad_out_weight)
    return (grad_input[None], grad_qkv_weight[None], grad_out_weight[None])


def solution(mesh):
    placed = (
        P("pipe", "seq", None),
        P("pipe", "seq", None),
        P("pipe", None, None),
        P("pipe", None, None),
        P("pipe", "seq", None, None),
        P("pipe", "seq", None),
    )
    return jax.shard_map(
        local,
        mesh=mesh,
        in_specs=placed,
        out_specs=(P("pipe", "seq", None), P("pipe", "seq", None), P("pipe", "seq", None)),
        check_vma=False,
    )
```

```python
import functools
import jax, jax.numpy as jnp
from jax import lax
from jax.experimental import pallas as pl
from jax.experimental.pallas import tpu as pltpu
from jax.sharding import PartitionSpec as P
HEAD_DIM=64; BLOCK=128; MAXNB=8; QB=64; GROUP=8
NEAR = 384
HALF = (512 - NEAR) // 2
f32=jnp.float32; bf16=jnp.bfloat16

def attn_body(order, nb, cnt, hq, qd, gqa, acc, kvt, group, i, slots):
    scale = HEAD_DIM ** -0.5
    half_row = lax.broadcasted_iota(jnp.int32, (BLOCK, BLOCK), 0) < HEAD_DIM
    half_lane = lax.broadcasted_iota(jnp.int32, (BLOCK, BLOCK), 1) < HEAD_DIM
    zero = jnp.zeros((BLOCK, BLOCK), bf16)
    dn = (((1,), (0,)), ((), ()))
    mm = lambda a, b: lax.dot_general(a, b, dn, preferred_element_type=f32)
    chains = []
    for g in range(group):
        b = order[i * group + g]
        chains.append((b, cnt[b], [nb[j, b] for j in range(slots)]))
    def first(g):
        b, c, ns = chains[g]
        own = qd[b]
        own_t = own.T
        q_t = jnp.where(half_row, own_t * jnp.asarray(scale, bf16), zero)
        d_t = jnp.where(half_row, zero, own_t)
        right = jnp.concatenate([q_t, d_t], axis=1)
        scores, dps = [], []
        every = mm(jnp.concatenate([load_keys(hq, ns[j]) for j in range(slots)], axis=0), right)
        for j in range(slots):
            both = every[j * BLOCK:(j + 1) * BLOCK]
            s = both[:, :BLOCK]
            if j > 0:
                s = jnp.where(j < c, s, -jnp.inf)
            scores.append(s)
            dps.append(both[:, BLOCK:])
        return own, own_t, scores, dps

    def second(g, own, own_t, scores, dps):
        top = scores[0]
        for s in scores[1:]:
            top = jnp.maximum(top, s)
        top = jnp.max(top, axis=0, keepdims=True)
        es = [jnp.exp(s - top) for s in scores]
        tot = es[0]
        for e in es[1:]:
            tot = tot + e
        inv = 1.0 / jnp.sum(tot, axis=0, keepdims=True)
        ps = [e * inv for e in es]
        b, c, ns = chains[g]
        low_all = jnp.concatenate([p.astype(bf16) for p in ps], axis=0)
        att_t = mm(jnp.concatenate([kvt[ns[j], HEAD_DIM:, :] for j in range(slots)], axis=1), low_all)
        return own, own_t, dps, ps, low_all, att_t.astype(bf16)

    def third(g, own, own_t, dps, ps, low_all, att_t):
        dot = jnp.sum(own_t[HEAD_DIM:, :].astype(f32) * att_t.astype(f32), axis=0, keepdims=True)
        ds_all = jnp.concatenate([(p * (dp - dot)).astype(bf16) for p, dp in zip(ps, dps)], axis=0)
        return own, low_all, ds_all, att_t

    def fourth(g, own, low_all, ds_all, att_t):
        b, c, ns = chains[g]
        left = jnp.concatenate([jnp.where(half_lane, own * jnp.asarray(scale, bf16), zero), jnp.where(half_lane, zero, own)], axis=0)
        terms = mm(jnp.concatenate([ds_all, low_all], axis=1), left)
        gq_t = mm(jnp.concatenate([kvt[ns[j], :HEAD_DIM, :] for j in range(slots)], axis=1), ds_all)
        for j in range(slots):
            acc[ns[j]] += terms[j * BLOCK:(j + 1) * BLOCK]
        gq_t = (gq_t * scale).astype(bf16)
        gqa[b] = jnp.concatenate([gq_t, att_t], axis=0).T

    ones, twos, threes = {}, {}, {}
    for t in range(group + 3):
        if t < group:
            ones[t] = first(t)
        if 0 <= t - 1 < group:
            twos[t - 1] = second(t - 1, *ones.pop(t - 1))
        if 0 <= t - 2 < group:
            threes[t - 2] = third(t - 2, *twos.pop(t - 2))
        if 0 <= t - 3 < group:
            fourth(t - 3, *threes.pop(t - 3))


def load_keys(hq, n):
    half, rows = key_rows(n)
    return hq[half, rows, :]


def key_rows(n):
    return n // 2, pl.ds(pl.multiple_of((n % 2) * BLOCK, BLOCK), BLOCK)


def attn_kernel(nb, cnt, hq, hd, hg, ha, acc, kvt, qd, gqa, order, place, *, group):
    for c in range(MAXNB + 2):
        place[c] = 0

    def prep_keys(u, carry):
        for e in range(2):
            c = cnt[2 * u + e] + 1
            place[c] = place[c] + 1
            kvt[2 * u + e] = hq[u, pl.ds(e * BLOCK, BLOCK), :].T
        return carry
    lax.fori_loop(0, QB // 2, prep_keys, 0, unroll=2)
    for c in range(1, MAXNB + 1):
        place[c] = place[c] + place[c - 1]

    def prep_rows(u, carry):
        for e in range(2):
            c = cnt[2 * u + e]
            at = place[c]
            order[at] = 2 * u + e
            place[c] = at + 1
            acc[2 * u + e] = jnp.zeros((BLOCK, BLOCK), f32)
        q = hq[u, pl.ds(256, BLOCK), :]
        d = hd[u]
        qd[2 * u] = jnp.concatenate([q[:, :HEAD_DIM], d[:, :HEAD_DIM]], axis=1)
        qd[2 * u + 1] = jnp.concatenate([q[:, HEAD_DIM:], d[:, HEAD_DIM:]], axis=1)
        return carry
    lax.fori_loop(0, QB // 2, prep_rows, 0, unroll=2)

    def step(i, carry):
        most = cnt[order[i * group + group - 1]]
        for slots in range(1, MAXNB + 1):
            @pl.when(most == slots)
            def run():
                attn_body(order, nb, cnt, hq, qd, gqa, acc, kvt, group, i, slots)
        return carry
    lax.fori_loop(0, QB // group, step, 0)

    def fin(u, carry):
        for e in range(2):
            hg[u, pl.ds(e * BLOCK, BLOCK), :] = acc[2 * u + e].astype(bf16)
        a, b = gqa[2 * u], gqa[2 * u + 1]
        hg[u, pl.ds(256, BLOCK), :] = jnp.concatenate([a[:, :HEAD_DIM], b[:, :HEAD_DIM]], axis=1)
        ha[u] = jnp.concatenate([a[:, HEAD_DIM:], b[:, HEAD_DIM:]], axis=1)
        return carry
    lax.fori_loop(0, QB // 2, fin, 0, unroll=2)


def attention(hq, hd, nb, cnt, group=GROUP):
    sm = pl.BlockSpec(memory_space=pltpu.SMEM)
    vm = pl.BlockSpec(memory_space=pltpu.VMEM)
    return pl.pallas_call(
        functools.partial(attn_kernel, group=group),
        out_shape=[jax.ShapeDtypeStruct((QB // 2, 384, 128), bf16), jax.ShapeDtypeStruct((QB // 2, 128, 128), bf16)],
        in_specs=[sm, sm, vm, vm],
        out_specs=[vm, vm],
        scratch_shapes=[
            pltpu.VMEM((QB, BLOCK, 128), f32),
            pltpu.VMEM((QB, 128, 128), bf16),
            pltpu.VMEM((QB, 128, 128), bf16),
            pltpu.VMEM((QB, 128, 128), bf16),
            pltpu.SMEM((QB,), jnp.int32),
            pltpu.SMEM((MAXNB + 2,), jnp.int32),
        ],
        compiler_params=pltpu.CompilerParams(vmem_limit_bytes=64 * 2**20 - 2**18),
        cost_estimate=pl.CostEstimate(flops=2 * 512 * 128 * 128 * 64 * 6, bytes_accessed=2**23, transcendentals=512 * 128 * 128),
    )(nb.T, cnt, hq, hd)


MESH = pl.DeviceIdType.MESH

def cat_tokens(dst, row, col, pair):
    turned = pair.T
    dst[pl.ds(row, HEAD_DIM), pl.ds(col, 128)] = turned[:HEAD_DIM]
    dst[pl.ds(row, HEAD_DIM), pl.ds(col + 128, 128)] = turned[HEAD_DIM:]

def finish_kernel(gqkv, att, lg, g0, g1, g3, g2, w, gin, gqw, gow,
                  rv, fv, at, lv, gv, wv, xt, mt, acc, pqs, pqr, pos, por, mine,
                  loc, zs, zr, xs, xr, as_, ar, qs, qr, os_, or_, fs, fr):
    pipe = lax.axis_index("pipe")
    me = lax.axis_index("seq")
    z, x = me // 4, me % 4
    zr4 = lambda d: (z + d) % 4
    xr4 = lambda d: (x + d) % 4
    def to_z(d): return (pipe, zr4(d) * 4 + x)
    def to_x(d): return (pipe, z * 4 + xr4(d))
    barrier = pltpu.get_barrier_semaphore()
    for d in (1, 2, 3):
        pl.semaphore_signal(barrier, inc=1, device_id=to_z(d), device_id_type=MESH)
        pl.semaphore_signal(barrier, inc=1, device_id=to_x(d), device_id_type=MESH)
    loads = [pltpu.make_async_copy(gqkv.at[z], rv.at[z], loc.at[0]),
             pltpu.make_async_copy(lg, lv, loc.at[1]),
             pltpu.make_async_copy(att.at[:, x], at.at[x], loc.at[2]),
             pltpu.make_async_copy(g0, gv.at[z], loc.at[3]),
             pltpu.make_async_copy(g1, gv.at[zr4(-1)], loc.at[9]),
             pltpu.make_async_copy(g3, gv.at[zr4(-3)], loc.at[10]),
             pltpu.make_async_copy(g2, gv.at[zr4(-2), pl.ds(0, NEAR)], loc.at[11]),
             pltpu.make_async_copy(w, wv, loc.at[4])]
    for c in loads:
        c.start()
    pl.semaphore_wait(barrier, 6)

    def remote(src, dst, ss, rs, dev):
        return pltpu.make_async_remote_copy(src_ref=src, dst_ref=dst, send_sem=ss, recv_sem=rs, device_id=dev, device_id_type=MESH)

    ZORDER = [(d, j) for j in (1, 3, 2, 0) for d in (1, 3)] + [(2, j) for j in (1, 3, 2, 0)]
    zc = {}
    for d, j in ZORDER:
        zc[d, j] = remote(gqkv.at[zr4(d), xr4(j)], rv.at[z, xr4(j)], zs.at[d - 1, j], zr.at[d - 1, j], to_z(d))
    xc, ac = {}, {}
    for d in (1, 3, 2):
        xc[0, d] = remote(gqkv.at[z, xr4(d)], fv.at[z, x], xs.at[0, d - 1], xr.at[0, d - 1], to_x(d))
        ac[d] = remote(att.at[:, xr4(d)], at.at[x], as_.at[d - 1], ar.at[d - 1], to_x(d))
        for e in (1, 3, 2):
            xc[e, d] = remote(rv.at[zr4(-e), xr4(d)], fv.at[zr4(-e), x], xs.at[e, d - 1], xr.at[e, d - 1], to_x(d))
    onward = [remote(g1.at[pl.ds(NEAR, HALF)], gv.at[zr4(-1), pl.ds(NEAR, HALF)], fs.at[0], fr.at[0], to_z(1)),
              remote(g3.at[pl.ds(NEAR + HALF, HALF)], gv.at[zr4(1), pl.ds(NEAR + HALF, HALF)], fs.at[1], fr.at[1], to_z(3))]
    for key in ZORDER:
        zc[key].start()
    for c in onward:
        c.start()
    for d in (1, 3, 2):
        xc[0, d].start()
    for d in (1, 3, 2):
        ac[d].start()

    def weight_part(zh, out_at):
        def turn(u, carry):
            xi, half = u // 2, u % 2
            col = pl.multiple_of(u * 256, 256)
            xt[pl.ds(64, 128), pl.ds(col, 256)] = rv[zh, xi, half, pl.ds(0, 256), :].T
            cat_tokens(xt, 0, col, rv[zh, xi, half, pl.ds(256, 128), :])
            return carry
        lax.fori_loop(0, 8, turn, 0)
        def tile(n, carry):
            cols = pl.ds(pl.multiple_of(n * 256, 256), 256)
            total = jnp.zeros((192, 256), f32)
            for k in range(4):
                total += jnp.dot(xt[pl.ds(0, 192), pl.ds(k * 512, 512)], lv[k, :, cols], preferred_element_type=f32)
            out_at(cols, total)
            return carry
        lax.fori_loop(0, 4, tile, 0)

    def own_out(cols, total):
        gqw[:, cols] = total

    def sent_out(slot):
        def put(cols, total):
            pqs[slot, :, cols] = total.astype(bf16)
        return put

    def input_part(zh, first=False):
        def build(u, carry):
            half, e = u // 2, u % 2
            rows = pl.ds(pl.multiple_of(u * 128, 128), 128)
            krows = pl.ds(pl.multiple_of(e * 128, 128), 128)
            for p in range(2):
                a, b = 2 * p, 2 * p + 1
                qa = fv[zh, a, half, pl.ds(256, 128), :]
                qb = fv[zh, b, half, pl.ds(256, 128), :]
                low = e == 0
                qa = jnp.where(low, qa[:, :64], qa[:, 64:])
                qb = jnp.where(low, qb[:, :64], qb[:, 64:])
                mt[rows, pl.ds(p * 384, 384)] = jnp.concatenate(
                    [qa, fv[zh, a, half, krows, :], qb, fv[zh, b, half, krows, :]], axis=1)
            return carry
        lax.fori_loop(0, 4, build, 0)
        def tile(n, carry):
            cols = pl.ds(pl.multiple_of(n * 256, 256), 256)
            part = lax.dot_general(mt[...], wv[cols, pl.ds(pl.multiple_of(zh * 768, 128), 768)],
                                   (((1,), (1,)), ((), ())), preferred_element_type=f32)
            if first:
                acc[:, cols] = gv[z, :, cols].astype(f32) + part
            else:
                acc[:, cols] += part
            return carry
        lax.fori_loop(0, 4, tile, 0)

    loads[0].wait()
    loads[1].wait()
    here = pltpu.make_async_copy
    own = here(rv.at[z, x], fv.at[z, x], loc.at[5])
    own.start()
    weight_part(z, own_out)

    for c in loads[2:]:
        c.wait()

    def arrive(d, j):
        zc[d, j].wait_recv()
        if j:
            xc[d, j].start()

    locals_, qc, oc = {}, {}, {}

    def make_part(e):
        weight_part(zr4(-e), sent_out(e - 1))
        qc[e] = remote(pqs.at[e - 1], pqr.at[e - 1], qs.at[e - 1], qr.at[e - 1], to_z(-e))

    def take_own(e):
        locals_[e] = here(rv.at[zr4(-e), x], fv.at[zr4(-e), x], loc.at[5 + e])
        locals_[e].start()

    def turn_att(u, carry):
        zi, half = u // 2, u % 2
        col = pl.multiple_of(u * 256, 256)
        for xh in range(4):
            cat_tokens(xt, xh * 64, col, at[xh, zi, half])
        return carry

    def att_tile(n, carry):
        cols = pl.ds(pl.multiple_of(n * 256, 256), 256)
        total = jnp.zeros((256, 256), f32)
        for k in range(4):
            total += jnp.dot(xt[:, pl.ds(k * 512, 512)], gv[k, :, cols], preferred_element_type=f32)
        mine[:, cols] = total
        for xh in range(4):
            pos[xh, :, cols] = total[xh * 64:(xh + 1) * 64].astype(bf16)
        return carry

    for d, j in ZORDER[:8]:
        arrive(d, j)
    take_own(1)
    take_own(3)
    make_part(1)
    for d, j in ZORDER[8:10]:
        arrive(d, j)
    make_part(3)
    for d, j in ZORDER[10:]:
        arrive(d, j)
    take_own(2)
    qc[1].start()
    qc[3].start()
    make_part(2)
    qc[2].start()
    for d in (1, 3, 2):
        ac[d].wait_recv()
    for c in onward:
        c.wait_recv()
    lax.fori_loop(0, 8, turn_att, 0)
    lax.fori_loop(0, 4, att_tile, 0)
    gow[...] = mine[pl.ds(pl.multiple_of(x * 64, 64), 64), :]
    for d in (1, 3, 2):
        oc[d] = remote(pos.at[xr4(d)], por.at[d - 1], os_.at[d - 1], or_.at[d - 1], to_x(d))
        oc[d].start()
    for d in (1, 3, 2):
        xc[0, d].wait_recv()
    own.wait()
    input_part(z, first=True)
    for e in (1, 3, 2):
        for d in (1, 3, 2):
            xc[e, d].wait_recv()
        locals_[e].wait()
        input_part(zr4(-e))
    gin[...] = acc[...].astype(bf16)
    for d in (1, 3, 2):
        oc[d].wait_recv()
        gow[...] += por[d - 1].astype(f32)
    for d in (1, 3, 2):
        qc[d].wait_recv()
        gqw[...] += pqr[d - 1].astype(f32)
    for c in [*zc.values(), *xc.values(), *ac.values(), *oc.values(), *qc.values(), *onward]:
        c.wait_send()

def finish(gqkv, att, lg, g0, g1, g3, g2, w, cid=1):
    anys = pl.BlockSpec(memory_space=pl.ANY)
    vm = pl.BlockSpec(memory_space=pltpu.VMEM)
    D = pltpu.SemaphoreType.DMA
    return pl.pallas_call(finish_kernel,
        out_shape=[jax.ShapeDtypeStruct((512, 1024), bf16), jax.ShapeDtypeStruct((192, 1024), f32), jax.ShapeDtypeStruct((64, 1024), f32)],
        in_specs=[anys] * 8, out_specs=[vm] * 3,
        scratch_shapes=[
            pltpu.VMEM((4, 4, 2, 384, 128), bf16), pltpu.VMEM((4, 4, 2, 384, 128), bf16), pltpu.VMEM((4, 4, 2, 128, 128), bf16),
            pltpu.VMEM((4, 512, 1024), bf16), pltpu.VMEM((4, 512, 1024), bf16), pltpu.VMEM((1024, 3072), bf16),
            pltpu.VMEM((256, 2048), bf16), pltpu.VMEM((512, 768), bf16), pltpu.VMEM((512, 1024), f32),
            pltpu.VMEM((3, 192, 1024), bf16), pltpu.VMEM((3, 192, 1024), bf16),
            pltpu.VMEM((4, 64, 1024), bf16), pltpu.VMEM((3, 64, 1024), bf16), pltpu.VMEM((256, 1024), f32),
            D((12,)), D((3, 4)), D((3, 4)), D((4, 3)), D((4, 3)), D((3,)), D((3,)), D((3,)), D((3,)), D((3,)), D((3,)), D((2,)), D((2,))],
        compiler_params=pltpu.CompilerParams(collective_id=cid, has_side_effects=True, vmem_limit_bytes=62 * 2**20),
        cost_estimate=pl.CostEstimate(flops=8 * 10**9, bytes_accessed=2 * 10**7, transcendentals=0),
    )(gqkv.reshape(4, 4, 2, 384, 128), att.reshape(4, 4, 2, 128, 128), lg, g0, g1, g3, g2, w)


def begin_kernel(lin, hand, w, wo, hqkv, hd, lg, g, gt,
                 lv, gv, w4, wov, sq, sd, dv,
                 loc, hs, hr, gs, gr, zs, zr, ds_, dr, es, er):
    pipe = lax.axis_index("pipe")
    me = lax.axis_index("seq")
    z, x = me // 4, me % 4
    zr4 = lambda d: (z + d) % 4
    xr4 = lambda d: (x + d) % 4
    def to_z(d): return (pipe, zr4(d) * 4 + x)
    def to_x(d): return (pipe, z * 4 + xr4(d))
    barrier = pltpu.get_barrier_semaphore()
    for d in (1, 2, 3):
        pl.semaphore_signal(barrier, inc=1, device_id=to_z(d), device_id_type=MESH)
        pl.semaphore_signal(barrier, inc=1, device_id=to_x(d), device_id_type=MESH)
    pl.semaphore_signal(barrier, inc=1, device_id=((pipe + 1) % 8, me), device_id_type=MESH)

    def here(src, dst, sem):
        return pltpu.make_async_copy(src, dst, sem)

    def remote(src, dst, ss, rs, dev):
        return pltpu.make_async_remote_copy(src_ref=src, dst_ref=dst, send_sem=ss, recv_sem=rs, device_id=dev, device_id_type=MESH)

    load_l = here(lin, lv.at[x], loc.at[0])
    load_l.start()
    load_w = []
    for zh in range(4):
        first = pl.multiple_of(((12 * zh + 3 * x) // 2) * 128, 128)
        load_w.append(here(w.at[:, pl.ds(first, 256)], w4.at[zh], loc.at[1 + zh]))
        load_w[-1].start()
    load_wo = here(wo, wov, loc.at[5])
    load_wo.start()
    pl.semaphore_wait(barrier, 7)

    given = remote(hand, gv, hs, hr, ((pipe + 7) % 8, me))
    right = {h: remote(lin.at[h], lv.at[x, h], gs.at[0, h], gr.at[0, h], to_x(1)) for h in (0, 1)}
    left = {h: remote(lin.at[h], lv.at[x, h], gs.at[1, h], gr.at[1, h], to_x(3)) for h in (0, 1)}
    right[2] = remote(lv.at[xr4(3), 0], lv.at[xr4(3), 0], gs.at[0, 2], gr.at[0, 2], to_x(1))
    left[2] = remote(lv.at[xr4(1), 1], lv.at[xr4(1), 1], gs.at[1, 2], gr.at[1, 2], to_x(3))
    right[0].start()
    left[1].start()
    given.start()
    right[1].start()
    left[0].start()

    zc, own, kept = {}, [], []

    def project(r, h):
        xs = xr4(r)
        def head(zh, carry):
            part = jnp.dot(lv[xs, h], w4[zh], preferred_element_type=f32).astype(bf16)
            part = jnp.where(x % 2 == 1, jnp.concatenate([part[:, 64:], part[:, :64]], axis=1), part)
            sq[xs, zh, h, pl.ds(0, 256), :] = part[:, 64:192]
            sq[xs, zh, h, pl.ds(256, 128), :] = jnp.concatenate([part[:128, :64], part[128:, :64]], axis=1)
            return carry
        lax.fori_loop(0, 4, head, 0)
        for d in (1, 3, 2):
            zc[d, r, h] = remote(sq.at[xs, zr4(d), h], hqkv.at[z, xs, h], zs.at[d - 1, r, h], zr.at[d - 1, r, h], to_z(d))
            zc[d, r, h].start()
        own.append(here(sq.at[xs, z, h], hqkv.at[z, xs, h], loc.at[6 + 2 * r + h]))
        own[-1].start()

    load_l.wait()
    for c in load_w:
        c.wait()
    project(0, 0)
    project(0, 1)
    right[0].wait_recv()
    right[2].start()
    project(3, 0)
    left[1].wait_recv()
    left[2].start()
    project(1, 1)

    given.wait_recv()
    load_wo.wait()
    own.append(here(gv, g, loc.at[14]))
    own[-1].start()
    own.append(here(gv.at[pl.ds(0, NEAR)], gt, loc.at[20]))
    own[-1].start()
    def heads(n, carry):
        rows = pl.ds(pl.multiple_of(n * 256, 256), 256)
        part = lax.dot_general(gv[...], wov[rows, :], (((1,), (1,)), ((), ())), preferred_element_type=f32).astype(bf16)
        for i in range(4):
            cols = part[:, i * 64:(i + 1) * 64]
            for h in range(2):
                sd[n, i, h] = jnp.concatenate([cols[h * 256:h * 256 + 128], cols[h * 256 + 128:h * 256 + 256]], axis=1)
        return carry
    lax.fori_loop(0, 4, heads, 0)
    dz, dx = {}, {}
    for d in (1, 3, 2):
        dz[d] = remote(sd.at[zr4(d)], dv.at[z], ds_.at[d - 1], dr.at[d - 1], to_z(d))
        dz[d].start()
    own.append(here(sd.at[z, x], hd.at[z, x], loc.at[15]))
    own[-1].start()
    for d in (1, 3, 2):
        dx[0, d] = remote(sd.at[z, xr4(d)], hd.at[z, x], es.at[0, d - 1], er.at[0, d - 1], to_x(d))

    right[1].wait_recv()
    project(3, 1)
    left[0].wait_recv()
    project(1, 0)
    right[2].wait_recv()
    left[2].wait_recv()
    for d in (1, 3, 2):
        dx[0, d].start()
    project(2, 0)
    project(2, 1)
    for e in (1, 3, 2):
        dz[e].wait_recv()
        for d in (1, 3, 2):
            dx[e, d] = remote(dv.at[zr4(-e), xr4(d)], hd.at[zr4(-e), x], es.at[e, d - 1], er.at[e, d - 1], to_x(d))
            dx[e, d].start()
        own.append(here(dv.at[zr4(-e), x], hd.at[zr4(-e), x], loc.at[16 + e]))
        own[-1].start()
    store = here(lv, lg, loc.at[16])
    store.start()
    for c in [*zc.values(), *dx.values()]:
        c.wait_recv()
    for c in own:
        c.wait()
    store.wait()
    given.wait_send()
    for c in [*right.values(), *left.values(), *zc.values(), *dz.values(), *dx.values()]:
        c.wait_send()


def begin(lin, hand, w, wo, cid=2):
    anys = pl.BlockSpec(memory_space=pl.ANY)
    D = pltpu.SemaphoreType.DMA
    return pl.pallas_call(
        begin_kernel,
        out_shape=[
            jax.ShapeDtypeStruct((4, 4, 2, 384, 128), bf16),
            jax.ShapeDtypeStruct((4, 4, 2, 128, 128), bf16),
            jax.ShapeDtypeStruct((4, 2, 256, 1024), bf16),
            jax.ShapeDtypeStruct((512, 1024), bf16),
            jax.ShapeDtypeStruct((NEAR, 1024), bf16),
        ],
        in_specs=[anys] * 4,
        out_specs=[anys] * 5,
        scratch_shapes=[
            pltpu.VMEM((4, 2, 256, 1024), bf16), pltpu.VMEM((512, 1024), bf16),
            pltpu.VMEM((4, 1024, 256), bf16), pltpu.VMEM((1024, 1024), bf16),
            pltpu.VMEM((4, 4, 2, 384, 128), bf16), pltpu.VMEM((4, 4, 2, 128, 128), bf16), pltpu.VMEM((4, 4, 2, 128, 128), bf16),
            D((21,)), D, D, D((2, 3)), D((2, 3)), D((3, 4, 2)), D((3, 4, 2)), D((3,)), D((3,)), D((4, 3)), D((4, 3)),
        ],
        compiler_params=pltpu.CompilerParams(collective_id=cid, has_side_effects=True, vmem_limit_bytes=62 * 2**20),
        cost_estimate=pl.CostEstimate(flops=4 * 10**9, bytes_accessed=2 * 10**7, transcendentals=0),
    )(lin.reshape(2, 256, 1024), hand, w, wo)


def settle_kernel(a, b, c, oa, ob, oc, ha, hb, hc, ins, outs):
    loads, stores = [], []
    for src, held, dst, parts in ((a, ha, oa, 4), (b, hb, ob, 3), (c, hc, oc, 1)):
        rows = src.shape[0] // parts
        for p in range(parts):
            cut, n = pl.ds(p * rows, rows), len(loads)
            loads.append(pltpu.make_async_copy(src.at[cut], held.at[cut], ins.at[n]))
            stores.append(pltpu.make_async_copy(held.at[cut], dst.at[cut], outs.at[n]))
            loads[-1].start()
    for load, store in zip(loads, stores):
        load.wait()
        store.start()
    for store in stores:
        store.wait()


def settle(*arrays):
    anys = pl.BlockSpec(memory_space=pl.ANY)
    return pl.pallas_call(
        settle_kernel,
        out_shape=[jax.ShapeDtypeStruct(a.shape, a.dtype) for a in arrays],
        in_specs=[anys] * 3,
        out_specs=[anys] * 3,
        scratch_shapes=[pltpu.VMEM(a.shape, a.dtype) for a in arrays]
        + [pltpu.SemaphoreType.DMA((8,)), pltpu.SemaphoreType.DMA((8,))],
        compiler_params=pltpu.CompilerParams(has_side_effects=True, vmem_limit_bytes=62 * 2**20),
    )(*arrays)


def local(layer_input, handoff, qkv_weight, out_weight, neighbours, counts):
    weight_in = qkv_weight[0]
    hqkv, hd, lg, grad_out, near = begin(layer_input[0], handoff[0], weight_in, out_weight[0])
    def along(rows, d):
        return lax.ppermute(rows, "seq", [(i, (i + 4 * d) % 16) for i in range(16)])
    around = [along(grad_out, 1), along(grad_out, 3), along(near, 2)]
    gqkv, att = attention(hqkv.reshape(32, 384, 128), hd.reshape(32, 128, 128), neighbours[0, 0], counts[0, 0])
    grad_input, grad_qkv_weight, grad_out_weight = finish(gqkv, att, lg.reshape(4, 512, 1024), grad_out, *around, weight_in)
    grad_input, grad_qkv_weight, grad_out_weight = settle(grad_input, grad_qkv_weight, grad_out_weight)
    return (grad_input[None], grad_qkv_weight[None], grad_out_weight[None])


def solution(mesh):
    placed = (
        P("pipe", "seq", None),
        P("pipe", "seq", None),
        P("pipe", None, None),
        P("pipe", None, None),
        P("pipe", "seq", None, None),
        P("pipe", "seq", None),
    )
    return jax.shard_map(
        local,
        mesh=mesh,
        in_specs=placed,
        out_specs=(P("pipe", "seq", None), P("pipe", "seq", None), P("pipe", "seq", None)),
        check_vma=False,
    )
```
